32 devices in a mesh: dp: 16 (over z, y, x), mp: 2 (over core).
Axes of the slice: x: 2, y: 2, z: 4, core: 2. Of those that a mesh axis runs over, the one named last changes fastest.
Arguments:
- tokens_in: bfloat16 [16, 1024, 960], P('dp'), may hold values from -6 to 6
- segment_ids: int32 [16, 1024], P('dp'), may hold values from 0 to 7, never falling along the last dimension, each value on 1 to 512 neighbouring positions
- kv_owner: int32 [5], replicated, may hold values from 0 to 1, as said below
- w_query: bfloat16 [5, 960, 192], replicated, may hold values from -0.1875 to 0.1875
- w_key: bfloat16 [5, 960, 64], replicated, may hold values from -0.1875 to 0.1875
- w_value: bfloat16 [5, 960, 64], replicated, may hold values from -0.1875 to 0.1875
- w_out: bfloat16 [5, 192, 960], replicated, may hold values from -1.5 to 1.5
- attn_gain: bfloat16 [960], replicated, may hold values from 0.099609375 to 1.8984375
- w_gate: bfloat16 [960, 2560], P(None, 'mp'), may hold values from -0.1875 to 0.1875
- w_up: bfloat16 [960, 2560], P(None, 'mp'), may hold values from -0.1875 to 0.1875
- w_down: bfloat16 [2560, 960], P('mp'), may hold values from -0.125 to 0.125
- ffn_gain: bfloat16 [960], replicated, may hold values from 0.099609375 to 1.8984375
- cotangent: bfloat16 [16, 1024, 960], P('dp'), may hold values from -6 to 6
Outputs:
- tokens_out: bfloat16 [16, 1024, 960], P('dp')
- grad_in: float32 [16, 1024, 960], P('dp')
- grad_query: float32 [6, 960, 192], P('mp', 'dp')
- grad_key: float32 [6, 960, 64], P('mp', 'dp')
- grad_value: float32 [6, 960, 64], P('mp', 'dp')
- grad_out: float32 [6, 192, 960], P('mp', None, 'dp')
- grad_gate: float32 [960, 2560], P('dp', 'mp')
- grad_up: float32 [960, 2560], P('dp', 'mp')
- grad_down: float32 [2560, 960], P('mp', 'dp')
- grad_attn_gain: float32 [960], P('dp')
- grad_ffn_gain: float32 [960], P('dp')
The draws below stay inside these ranges and needn't reach their ends.
Inputs may be any that keep to these rules, and one draw needn't show every extreme that they name: Group g is worked on by the mp device kv_owner[g]; one device holds 3 groups, the other the remaining ones.
All inputs are finite; a program needn't handle non-finite values.
Results may differ from the reference program's by a relative error of at most 0.03.
Values may be sent and summed in bfloat16 or wider, within the bound.
No kernel may reach another device: no remote copies, remote signals or barrier semaphores. Data moves between devices by JAX's collectives and lax.ppermute only.
A program may use at most 320 MiB of HBM per device.

```python
import math
import jax
import jax.numpy as jnp
import numpy as np
from jax import lax

D = 960
HEADS = 15
KV = 5
HEAD = 64
FF = 2560
SEQ = 1024
REPEAT = 2
GQ = 3
SLOTS = 3
ROWS = 16
N_MP = 2


def draw_kv_owner(key, part):
    key = jax.random.fold_in(key, 11)
    raw_bits = jax.random.bits(jax.random.fold_in(key, 5), (KV,), jnp.uint32)
    scores = (raw_bits >> 8).astype(jnp.int32) * KV + jnp.arange(KV, dtype=jnp.int32)
    ranking = jnp.sum(jnp.where(scores[None, :] < scores[:, None], 1, 0), axis=1)
    heavy = jax.random.randint(jax.random.fold_in(key, 7), (), 0, 2, dtype=jnp.int32)
    return jnp.where(ranking < (KV + 1) // 2, heavy, 1 - heavy).astype(jnp.int32)


def raised(values, rng, source, target, parts, factor):
    def block_of(dim):
        return (jnp.arange(values.shape[dim]) // (values.shape[dim] // parts)).reshape((-1,) + (1,) * (values.ndim - 1 - dim))

    first = jax.random.permutation(rng, parts)[block_of(target)]
    other_side = (block_of(target) + parts // 2) % parts
    return jnp.where((block_of(source) == first) | (block_of(source) == other_side), factor * values, values)


def shard_levels(stream_key, shape, pieces, least, largest):
    def one(dim, parts):
        steps = jax.random.uniform(jax.random.fold_in(jax.random.fold_in(stream_key, 6), dim), (parts,), jnp.float32, least / len(pieces), largest / len(pieces))
        return jnp.repeat(jnp.exp(steps), shape[dim] // parts).reshape((-1,) + (1,) * (len(shape) - dim - 1))

    loudness = one(*pieces[0])
    for cut in pieces[1:]:
        loudness = loudness * one(*cut)
    return loudness


def split_up(number_of, total, bound, skew):
    portions = [(1 << 20) // math.isqrt(standing ** skew) + 1 for standing in range(2, number_of + 1)]
    surplus, given = total - bound - (number_of - 1), [1] * (number_of - 1)
    while surplus > 0:
        movable = [i for i in range(number_of - 1) if given[i] < bound]
        pool, left = sum([portions[i] for i in movable]), surplus
        for i in movable:
            addition = min(bound - given[i], max(1, left * portions[i] // pool), surplus)
            given[i] = given[i] + addition
            surplus = surplus - addition
    return np.array([bound] + given)


def ragged(rng, number_of, total, limit, slope):
    if number_of == 2:
        one = jax.random.randint(rng, (), max(1, total - limit), min(limit, total - 1) + 1)
        return jnp.stack([one, total - one])
    sizes = jnp.asarray(split_up(number_of, total, limit, slope), jnp.int32)
    pairs = (number_of - 1) // 2
    source_of, receiver = sizes[1:1 + 2 * pairs:2], sizes[2:2 + 2 * pairs:2]
    margin = jnp.minimum(source_of - 1, limit - receiver)
    passed = jax.random.randint(jax.random.fold_in(rng, 1), (pairs,), 0, 1 << 20) % (margin + 1)
    sizes = sizes.at[1:1 + 2 * pairs:2].set(source_of - passed).at[2:2 + 2 * pairs:2].set(receiver + passed)
    return sizes[jax.random.permutation(jax.random.fold_in(rng, 2), number_of)]


def gaussian(rng, dims, scale, most, shards=(), kind=jnp.bfloat16):
    factor_of = shard_levels(rng, dims, shards, -0.22, 0.18) if shards else 1.0
    values = jax.random.normal(rng, dims, jnp.float32) * scale * factor_of
    return jnp.minimum(jnp.maximum(values, -most), most).astype(kind)


def bell_draw_with(own_key, dims, spread, limit, split, heavy, kind=jnp.bfloat16):
    values = spread * jax.random.normal(own_key, dims, jnp.float32)
    if split:
        values = values * shard_levels(own_key, dims, split, -0.22, 0.18)
    return jnp.clip(raised(values, jax.random.fold_in(own_key, 3), *heavy), -limit, limit).astype(kind)


def setup_inputs(seed: int = 0) -> dict:
    streams_of = jax.random.split(jax.random.key(seed), 14)
    tokens_in = bell_draw_with(streams_of[0], (ROWS, SEQ, D), 1.0, 6.0, ((0, 16),), (0, 2, 16, 2.0))
    segment_ids = jax.vmap(lambda own: jnp.searchsorted(jnp.cumsum(ragged(own, 8, SEQ, SEQ // 2, 2)), jnp.arange(SEQ), side="right"))(jax.random.split(streams_of[1], ROWS)).reshape((ROWS, SEQ)).astype(jnp.int32)
    kv_owner = draw_kv_owner(jax.random.fold_in(streams_of[13], 71), 0)
    w_query = gaussian(streams_of[3], (KV, D, GQ * HEAD), D ** -0.5, 0.1875)
    w_key = gaussian(streams_of[4], (KV, D, HEAD), D ** -0.5, 0.1875)
    w_value = gaussian(streams_of[5], (KV, D, HEAD), D ** -0.5, 0.1875)
    w_out = gaussian(streams_of[6], (KV, GQ * HEAD, D), (HEADS * HEAD // 64) ** -0.5, 1.5)
    attn_gain = jnp.clip(1.0 + 0.18 * jax.random.normal(streams_of[7], (D,), jnp.float32), 0.099609375, 1.8984375).astype(jnp.bfloat16)
    w_gate = gaussian(streams_of[8], (D, FF), D ** -0.5, 0.1875, ((1, 2),))
    w_up = gaussian(streams_of[9], (D, FF), D ** -0.5, 0.1875, ((1, 2),))
    w_down = gaussian(streams_of[10], (FF, D), FF ** -0.5, 0.125, ((0, 2),))
    ffn_gain = jnp.clip(1.0 + 0.18 * jax.random.normal(streams_of[11], (D,), jnp.float32), 0.099609375, 1.8984375).astype(jnp.bfloat16)
    cotangent = gaussian(streams_of[12], (ROWS, SEQ, D), 1.0, 6.0, ((0, 16),))
    return {"tokens_in": tokens_in, "segment_ids": segment_ids, "kv_owner": kv_owner, "w_query": w_query, "w_key": w_key, "w_value": w_value, "w_out": w_out, "attn_gain": attn_gain, "w_gate": w_gate, "w_up": w_up, "w_down": w_down, "ffn_gain": ffn_gain, "cotangent": cotangent}


@jax.custom_vjp
def low(v):
    return lax.optimization_barrier(v.astype(jnp.bfloat16)).astype(jnp.float32)

@jax.custom_vjp
def low_back(v):
    return v

def low_keep(v):
    return (low(v), None)

def low_pass(kept, grad):
    return (grad,)

def back_keep(v):
    return (v, None)

def back_low(kept, grad):
    return (low(grad),)
low.defvjp(low_keep, low_pass)
low_back.defvjp(back_keep, back_low)
epsilon = 1e-05
highest = lax.Precision.HIGHEST
masked_value = -1e+30

def rotary_tables(length, width):
    half_width = width // 2
    position = jnp.arange(length, dtype=jnp.float32)[:, None]
    column = jnp.arange(half_width, dtype=jnp.float32)[None, :]
    angles = position * jnp.exp(column * (-2.0 * math.log(10000.0) / width))
    return (jnp.cos(angles), jnp.sin(angles))

def rotate(values, cosine, sine_table):
    half_width = values.shape[-1] // 2
    first_half = values[..., :half_width]
    second_half = values[..., half_width:]
    cosine = cosine[:, None, :]
    sine_table = sine_table[:, None, :]
    return jnp.concatenate([first_half * cosine - second_half * sine_table, second_half * cosine + first_half * sine_table], axis=-1)

def rms_norm(values, gain):
    return values * lax.rsqrt(lax.optimization_barrier(jnp.mean(values * values, axis=-1, keepdims=True)) + epsilon) * gain

def apply_block(hidden, allowed, cosine, sine_table, owner_onehot, params):
    w_query, w_key, w_value, w_out, attn_gain, w_gate, w_up, w_down, ffn_gain = params
    length = hidden.shape[0]
    score_scale = 1.0 / math.sqrt(HEAD)
    normed = low(rms_norm(hidden, attn_gain))
    query_pre = low_back(jnp.einsum('ld,gdc->lgc', normed, w_query, precision=highest))
    key_pre = low_back(jnp.einsum('ld,gdc->lgc', normed, w_key, precision=highest))
    values_all = low(low_back(jnp.einsum('ld,gdc->lgc', normed, w_value, precision=highest)))
    queries = low(rotate(query_pre.reshape(length, HEADS, HEAD), cosine, sine_table))
    queries = queries.reshape(length, KV, GQ, HEAD)
    keys_all = low(rotate(key_pre, cosine, sine_table))
    scores = low_back(jnp.einsum('qgjc,kgc->gjqk', queries, keys_all, precision=highest) * score_scale)
    scores = jnp.where(allowed[None, None], scores, masked_value)
    probabilities = low(jax.nn.softmax(scores, axis=-1))
    attended = jnp.einsum('gjqk,kgc->qgjc', probabilities, values_all, precision=highest)
    attended = low(low_back(attended.reshape(length, KV, GQ * HEAD)))
    branch = 0.0
    for device in range(N_MP):
        partial_sum = jnp.einsum('lgc,gcd,g->ld', attended, w_out, owner_onehot[device], precision=highest)
        branch = branch + low(partial_sum)
    middle = hidden + low_back(branch)
    normed_two = low(rms_norm(middle, ffn_gain))
    gate_value = low_back(jnp.dot(normed_two, w_gate, precision=highest))
    lift_value = low_back(jnp.dot(normed_two, w_up, precision=highest))
    inner = low(jax.nn.silu(gate_value) * lift_value)
    column_share = FF // N_MP
    branch_two = 0.0
    for device in range(N_MP):
        lower = device * column_share
        partial_sum = jnp.dot(inner[:, lower:lower + column_share], w_down[lower:lower + column_share], precision=highest)
        branch_two = branch_two + low(partial_sum)
    return middle + low_back(branch_two)

def forward(start_hidden, allowed, cosine, sine_table, owner_onehot, params):
    hidden = start_hidden
    for repeat_index in range(REPEAT):
        hidden = apply_block(hidden, allowed, cosine, sine_table, owner_onehot, params)
    return hidden

def reference(tokens_in, segment_ids, kv_owner, w_query, w_key, w_value, w_out, attn_gain, w_gate, w_up, w_down, ffn_gain, cotangent):
    params = tuple((array.astype(jnp.float32) for array in (w_query, w_key, w_value, w_out, attn_gain, w_gate, w_up, w_down, ffn_gain)))
    owner_onehot = (kv_owner[None, :] == jnp.arange(N_MP)[:, None]).astype(jnp.float32)
    cosine, sine_table = rotary_tables(SEQ, HEAD)
    positions = jnp.arange(SEQ)

    def one_row(totals, row_items):
        row_in, segment_row, row_cotangent = row_items
        allowed = (segment_row[:, None] == segment_row[None, :]) & (positions[None, :] <= positions[:, None])

        def run_block(start_hidden, weights):
            return forward(start_hidden, allowed, cosine, sine_table, owner_onehot, weights)
        result, pullback = jax.vjp(run_block, row_in.astype(jnp.float32), params)
        row_grad, weight_grads = pullback(row_cotangent.astype(jnp.float32))
        totals = jax.tree.map(jnp.add, totals, weight_grads)
        return (totals, (result.astype(jnp.bfloat16), row_grad))
    zero_grads = jax.tree.map(jnp.zeros_like, params)
    totals, (outputs, grad_inputs) = lax.scan(one_row, zero_grads, (tokens_in, segment_ids, cotangent))
    group_ids = jnp.arange(KV)
    same_owner = kv_owner[None, :] == kv_owner[:, None]
    group_rank = lax.optimization_barrier(jnp.sum(jnp.where(same_owner & (group_ids[None, :] < group_ids[:, None]), 1, 0), axis=1))
    slot_of = kv_owner * SLOTS + group_rank
    placement_table = (jnp.arange(N_MP * SLOTS)[:, None] == slot_of[None, :]).astype(jnp.float32)

    def to_slots(grads):
        return jnp.einsum('sg,g...->s...', placement_table, grads, precision=highest)
    return (outputs, grad_inputs, to_slots(totals[0]), to_slots(totals[1]), to_slots(totals[2]), to_slots(totals[3]), totals[5], totals[6], totals[7], totals[4], totals[8])
```

```python
import math

import jax
import jax.numpy as jnp
from jax import lax
from jax.sharding import PartitionSpec as P

REPEAT = 2


epsilon = 1e-05
masked_value = -1e30


def rotary_tables(length, width):
    half_width = width // 2
    position = lax.broadcasted_iota(jnp.float32, (length, half_width), 0)
    column = lax.broadcasted_iota(jnp.float32, (length, half_width), 1)
    angles = position * jnp.exp(column * (-2.0 * math.log(10000.0) / width))
    return (jnp.cos(angles), jnp.sin(angles))


def rotate(values, cosine, sine_table):
    half_width = values.shape[-1] // 2
    first_half = values[..., :half_width]
    second_half = values[..., half_width:]
    cosine = cosine[:, None, :]
    sine_table = sine_table[:, None, :]
    return jnp.concatenate(
        [
            first_half * cosine - second_half * sine_table,
            second_half * cosine + first_half * sine_table,
        ],
        axis=-1,
    )


def norm_back(values, inverse, gain, grad_normed):
    scaled = grad_normed * gain
    inner_mean = jnp.mean(scaled * values, axis=-1, keepdims=True)
    return inverse * scaled - values * (inverse * inverse * inverse) * inner_mean


def sum_over_mp(partial_sum):
    own = partial_sum.astype(jnp.bfloat16)
    other = lax.ppermute(own, "mp", [(0, 1), (1, 0)])
    return own.astype(jnp.float32) + other.astype(jnp.float32)


def stage_plans(bit_count):
    if bit_count < 4:
        return [[[bit] for bit in range(bit_count)]] * 3
    rest = list(range(4, bit_count))
    tail = [[bit] for bit in rest]
    return [
        [[0], [1], [2, 3]] + tail,
        [[1], [0], [2, 3]] + tail,
        [[2], [0], [1], [3]] + tail,
    ]


def shard_order(plan):
    bits = [bit for stage in plan for bit in stage]
    order = []
    for place in range(1 << len(bits)):
        shard = 0
        for rank, bit in enumerate(bits):
            if place >> (len(bits) - 1 - rank) & 1:
                shard |= 1 << bit
        order.append(shard)
    return order


def reduce_stage(current, stage, last):
    size = lax.axis_size("dp")
    index = lax.axis_index("dp")
    mine = 0
    for bit in stage:
        mine = mine * 2 + ((index >> bit) & 1)
    ways = 1 << len(stage)
    pieces = current.shape[0] // ways
    total = lax.dynamic_slice_in_dim(current, mine * pieces, pieces, 0).astype(jnp.float32)
    received = []
    for offset in range(1, ways):
        mask = 0
        for rank, bit in enumerate(stage):
            if offset >> (len(stage) - 1 - rank) & 1:
                mask |= 1 << bit
        outgoing = lax.dynamic_slice_in_dim(current, (mine ^ offset) * pieces, pieces, 0)
        received.append(lax.ppermute(outgoing, "dp", [(i, i ^ mask) for i in range(size)]))
    for piece in received:
        total = total + piece.astype(jnp.float32)
    return total if last else total.astype(jnp.bfloat16)


def reduce_scatter(payload, plan):
    for number, stage in enumerate(plan):
        payload = reduce_stage(payload, stage, number == len(plan) - 1)
    return payload[0]


def to_payload(grad, plan, extra=None):
    size = lax.axis_size("dp")
    rows = grad.shape[0] // size
    padded = -(-(rows + 1) // 16) * 16
    shards = grad.astype(jnp.bfloat16).reshape(size, rows, grad.shape[1])
    if extra is None:
        extra = jnp.zeros((size, padded - rows, grad.shape[1]), jnp.bfloat16)
    shards = jnp.concatenate([shards, extra], axis=1)
    return jnp.stack([shards[shard] for shard in shard_order(plan)])


def per_device(
    tokens_in,
    segment_ids,
    kv_owner,
    w_query,
    w_key,
    w_value,
    w_out,
    attn_gain,
    w_gate,
    w_up,
    w_down,
    ffn_gain,
    cotangent,
):
    length = tokens_in.shape[1]
    head_size = w_key.shape[2]
    group_cols = w_query.shape[2]
    group_heads = group_cols // head_size
    group_count = kv_owner.shape[0]
    slot_count = (group_count + lax.axis_size("mp") - 1) // lax.axis_size("mp")
    column_share = w_gate.shape[1]
    score_scale = 1.0 / math.sqrt(head_size)
    block_rows = min(512, length)
    block_count = length // block_rows
    owned = kv_owner == lax.axis_index("mp")
    group_ids = jnp.arange(group_count)
    group_rank = jnp.sum(
        jnp.where((group_ids[None, :] < group_ids[:, None]) & owned[None, :], 1, 0), axis=1
    )
    selector = ((group_rank[None, :] == jnp.arange(slot_count)[:, None]) & owned[None, :]).astype(
        jnp.bfloat16
    )
    stacked = jnp.concatenate([w_query, w_key, w_value], axis=2)
    qkv_slots = jnp.einsum(
        "sg,gdc->sdc", selector, stacked, preferred_element_type=jnp.float32
    ).astype(jnp.bfloat16)
    out_slots = jnp.einsum(
        "sg,gcd->scd", selector, w_out, preferred_element_type=jnp.float32
    ).astype(jnp.bfloat16)
    gate_up = jnp.concatenate([w_gate, w_up], axis=1)
    cosine, sine_table = rotary_tables(length, head_size)
    segment_row = segment_ids[0]
    positions = jnp.arange(length)
    starts = jnp.arange(block_count) * block_rows

    def attend_block(start, queries, keys_all):
        query_block = lax.dynamic_slice_in_dim(queries, start, block_rows, 1)
        query_block = query_block.reshape(slot_count, block_rows, group_heads, head_size)
        segment_block = lax.dynamic_slice_in_dim(segment_row, start, block_rows, 0)
        query_positions = start + jnp.arange(block_rows)
        allowed = (segment_block[:, None] == segment_row[None, :]) & (
            positions[None, :] <= query_positions[:, None]
        )
        scores = (
            jnp.einsum("sqjc,skc->sjqk", query_block, keys_all, preferred_element_type=jnp.float32)
            * score_scale
        )
        scores = jnp.where(allowed[None, None], scores, masked_value)
        row_max = jnp.max(scores, axis=-1, keepdims=True)
        exponent = jnp.exp(scores - row_max)
        probabilities = exponent / jnp.sum(exponent, axis=-1, keepdims=True)
        return (query_block, probabilities)

    hidden = tokens_in[0].astype(jnp.float32)
    inputs = []
    saved_all = []
    for repeat_index in range(REPEAT):
        inputs.append(hidden)
        forward_inverse_one = lax.rsqrt(jnp.mean(hidden * hidden, axis=-1, keepdims=True) + epsilon)
        forward_normed = (hidden * forward_inverse_one * attn_gain).astype(jnp.bfloat16)
        projected = jnp.einsum(
            "ld,sdc->slc", forward_normed, qkv_slots, preferred_element_type=jnp.float32
        )
        query_pre = projected[..., :group_cols].reshape(slot_count, length, group_heads, head_size)
        key_pre = projected[..., group_cols : group_cols + head_size][:, :, None, :]
        forward_queries = (
            rotate(query_pre, cosine, sine_table)
            .reshape(slot_count, length, group_cols)
            .astype(jnp.bfloat16)
        )
        forward_keys_all = rotate(key_pre, cosine, sine_table)[:, :, 0, :].astype(jnp.bfloat16)
        forward_values_all = projected[..., group_cols + head_size :].astype(jnp.bfloat16)

        def forward_one_block(start):
            query_block, probabilities = attend_block(start, forward_queries, forward_keys_all)
            piece = jnp.einsum(
                "sjqk,skc->sqjc",
                probabilities.astype(jnp.bfloat16),
                forward_values_all,
                preferred_element_type=jnp.float32,
            )
            return piece.astype(jnp.bfloat16).reshape(slot_count, block_rows, group_cols)

        pieces = lax.map(forward_one_block, starts)
        forward_attended = jnp.moveaxis(pieces, 0, 1).reshape(slot_count, length, group_cols)
        partial_sum = jnp.einsum(
            "slc,scd->ld", forward_attended, out_slots, preferred_element_type=jnp.float32
        )
        branch = sum_over_mp(partial_sum)
        forward_middle = hidden + branch
        forward_inverse_two = lax.rsqrt(
            jnp.mean(forward_middle * forward_middle, axis=-1, keepdims=True) + epsilon
        )
        forward_normed_two = (forward_middle * forward_inverse_two * ffn_gain).astype(jnp.bfloat16)
        forward_gate_pre = jnp.dot(forward_normed_two, gate_up, preferred_element_type=jnp.float32)
        forward_inner = (
            jax.nn.silu(forward_gate_pre[:, :column_share]) * forward_gate_pre[:, column_share:]
        ).astype(jnp.bfloat16)
        partial_two = jnp.dot(forward_inner, w_down, preferred_element_type=jnp.float32)
        branch_two = sum_over_mp(partial_two)
        forward_saved = (
            hidden,
            forward_inverse_one,
            forward_normed,
            forward_queries,
            forward_keys_all,
            forward_values_all,
            forward_attended,
            forward_middle,
            forward_inverse_two,
            forward_normed_two,
            forward_gate_pre,
            forward_inner,
        )
        hidden = forward_middle + branch_two
        saved = forward_saved
        saved_all.append(saved)
    grad_hidden = cotangent[0].astype(jnp.float32)
    totals = None
    reduced = None
    for repeat_index in reversed(range(REPEAT)):
        saved = saved_all[repeat_index]
        grad_out = grad_hidden
        (
            backward_hidden,
            inverse_one,
            normed,
            backward_queries,
            backward_keys_all,
            values_all,
            attended,
            middle,
            inverse_two,
            normed_two,
            gate_pre,
            inner,
        ) = saved
        ffn_grad = grad_out.astype(jnp.bfloat16)
        grad_inner = jnp.einsum("ld,fd->lf", ffn_grad, w_down, preferred_element_type=jnp.float32)
        gate_value = gate_pre[:, :column_share]
        lift_value = gate_pre[:, column_share:]
        sigmoid = jax.nn.sigmoid(gate_value)
        grad_gate = grad_inner * lift_value * sigmoid * (1.0 + gate_value * (1.0 - sigmoid))
        grad_lift = grad_inner * gate_value * sigmoid
        grad_gate_up = jnp.concatenate([grad_gate, grad_lift], axis=1).astype(jnp.bfloat16)
        grad_normed_two = sum_over_mp(
            jnp.einsum("lf,df->ld", grad_gate_up, gate_up, preferred_element_type=jnp.float32)
        )
        backward_d_gate_up = jnp.einsum(
            "ld,lf->df", normed_two, grad_gate_up, preferred_element_type=jnp.float32
        )
        backward_d_down = jnp.einsum(
            "ld,lf->df", ffn_grad, inner, preferred_element_type=jnp.float32
        )
        backward_d_ffn_gain = jnp.sum(grad_normed_two * middle * inverse_two, axis=0)
        grad_middle = grad_out + norm_back(middle, inverse_two, ffn_gain, grad_normed_two)
        attn_grad = grad_middle.astype(jnp.bfloat16)
        grad_attended = jnp.einsum(
            "ld,scd->slc", attn_grad, out_slots, preferred_element_type=jnp.float32
        ).astype(jnp.bfloat16)
        backward_d_out = jnp.einsum(
            "ld,slc->dsc", attn_grad, attended, preferred_element_type=jnp.float32
        ).reshape(attn_grad.shape[1], slot_count * group_cols)

        def backward_one_block(carry, start):
            grad_keys, grad_values = carry
            query_block, probabilities = attend_block(start, backward_queries, backward_keys_all)
            grad_block = lax.dynamic_slice_in_dim(grad_attended, start, block_rows, 1)
            grad_block = grad_block.reshape(slot_count, block_rows, group_heads, head_size)
            grad_probs = jnp.einsum(
                "sqjc,skc->sjqk", grad_block, values_all, preferred_element_type=jnp.float32
            )
            delta = jnp.sum(probabilities * grad_probs, axis=-1, keepdims=True)
            grad_scores = (probabilities * (grad_probs - delta)).astype(jnp.bfloat16)
            grad_query = (
                jnp.einsum(
                    "sjqk,skc->sqjc",
                    grad_scores,
                    backward_keys_all,
                    preferred_element_type=jnp.float32,
                )
                * score_scale
            )
            grad_keys = (
                grad_keys
                + jnp.einsum(
                    "sjqk,sqjc->skc", grad_scores, query_block, preferred_element_type=jnp.float32
                )
                * score_scale
            )
            grad_values = grad_values + jnp.einsum(
                "sjqk,sqjc->skc",
                probabilities.astype(jnp.bfloat16),
                grad_block,
                preferred_element_type=jnp.float32,
            )
            return ((grad_keys, grad_values), grad_query)

        zero_state = jnp.zeros((slot_count, length, head_size), jnp.float32)
        (grad_keys, grad_values), grad_pieces = lax.scan(
            backward_one_block, (zero_state, zero_state), starts
        )
        grad_queries = jnp.moveaxis(grad_pieces, 0, 1).reshape(
            slot_count, length, group_heads, head_size
        )
        grad_query_pre = rotate(grad_queries, cosine, -sine_table).reshape(
            slot_count, length, group_cols
        )
        grad_key_pre = rotate(grad_keys[:, :, None, :], cosine, -sine_table)[:, :, 0, :]
        grad_projected = jnp.concatenate(
            [grad_query_pre, grad_key_pre, grad_values], axis=2
        ).astype(jnp.bfloat16)
        grad_normed = sum_over_mp(
            jnp.einsum("slc,sdc->ld", grad_projected, qkv_slots, preferred_element_type=jnp.float32)
        )
        backward_d_qkv = jnp.einsum(
            "ld,slc->sdc", normed, grad_projected, preferred_element_type=jnp.float32
        )
        backward_d_attn_gain = jnp.sum(grad_normed * backward_hidden * inverse_one, axis=0)
        backward_grad_hidden = grad_middle + norm_back(
            backward_hidden, inverse_one, attn_gain, grad_normed
        )
        grad_hidden = backward_grad_hidden
        grads = (
            backward_d_qkv,
            backward_d_out,
            backward_d_gate_up,
            backward_d_down,
            backward_d_attn_gain,
            backward_d_ffn_gain,
        )
        totals = grads if totals is None else jax.tree.map(jnp.add, totals, grads)
    d_qkv, d_out, d_gate_up, d_down, d_attn_gain, d_ffn_gain = totals
    size = lax.axis_size("dp")
    features = d_attn_gain.shape[0]
    rows = features // size
    plans = stage_plans(size.bit_length() - 1)
    extra_rows = -(-(rows + 1) // 16) * 16 - rows
    gains = jnp.zeros((size, extra_rows, column_share), jnp.float32)
    gains = gains.at[:, 0, :rows].set(d_attn_gain.reshape(size, rows))
    gains = gains.at[:, 0, rows : 2 * rows].set(d_ffn_gain.reshape(size, rows))
    gains = gains.astype(jnp.bfloat16)
    gate_total = reduce_scatter(
        to_payload(d_gate_up[:, :column_share], plans[0], gains), plans[0]
    )
    up_total = reduce_scatter(to_payload(d_gate_up[:, column_share:], plans[1]), plans[1])
    down_total = reduce_scatter(to_payload(d_down, plans[2]), plans[2])
    qkv_total = reduce_scatter(
        to_payload(jnp.moveaxis(d_qkv, 0, 1).reshape(features, -1), plans[0]), plans[0]
    )
    out_total = reduce_scatter(to_payload(d_out, plans[1]), plans[1])
    qkv_total = jnp.moveaxis(qkv_total[:rows].reshape(rows, slot_count, -1), 1, 0)
    reduced = (
        qkv_total[..., :group_cols],
        qkv_total[..., group_cols : group_cols + head_size],
        qkv_total[..., group_cols + head_size :],
        out_total[:rows].T.reshape(slot_count, group_cols, rows),
        gate_total[:rows],
        up_total[:rows],
        down_total[:rows].T,
        gate_total[rows, :rows],
        gate_total[rows, rows : 2 * rows],
    )
    return (
        hidden.astype(jnp.bfloat16)[None],
        grad_hidden[None],
        reduced[0],
        reduced[1],
        reduced[2],
        reduced[3],
        reduced[4],
        reduced[5],
        reduced[6],
        reduced[7],
        reduced[8],
    )


def solution(mesh):
    in_specs = (
        P("dp", None, None),
        P("dp", None),
        P(),
        P(),
        P(),
        P(),
        P(),
        P(),
        P(None, "mp"),
        P(None, "mp"),
        P("mp", None),
        P(),
        P("dp", None, None),
    )
    out_specs = (
        P("dp", None, None),
        P("dp", None, None),
        P("mp", "dp", None),
        P("mp", "dp", None),
        P("mp", "dp", None),
        P("mp", None, "dp"),
        P("dp", "mp"),
        P("dp", "mp"),
        P("mp", "dp"),
        P("dp"),
        P("dp"),
    )
    return jax.shard_map(
        per_device, mesh=mesh, in_specs=in_specs, out_specs=out_specs, check_vma=False
    )
```

```python
import functools
import math

import jax
import jax.numpy as jnp
import numpy as np
from jax import lax
from jax.experimental import pallas as pl
from jax.experimental.pallas import tpu as pltpu
from jax.sharding import PartitionSpec as P

REPEAT = 2
BLOCK = 256
FFN_BLOCK = 256
LANES = 128
HEAD = 64
VROWS = 80
epsilon = 1e-05
masked_value = -1e30
LOG2E = math.log2(math.e)
LN2 = math.log(2.0)
f32 = jnp.float32
bf16 = jnp.bfloat16
NN = (((1,), (0,)), ((), ()))
NT = (((1,), (1,)), ((), ()))
TN = (((0,), (0,)), ((), ()))
MIB = 1024 * 1024


def matmul(a, b, dims=NN):
    return lax.dot_general(a, b, dims, preferred_element_type=f32)


def wide(column, width):
    return jnp.concatenate([column] * (width // LANES), axis=1)


def inverse_rms(values):
    return lax.rsqrt(jnp.mean(values * values, axis=0, keepdims=True) + epsilon)


def normalise(values, gain):
    return (values * inverse_rms(values) * wide(gain, values.shape[1])).astype(bf16)


def norm_back(values, gain, grad_normed):
    inverse = inverse_rms(values)
    scaled = grad_normed * wide(gain, values.shape[1])
    inner_mean = jnp.mean(scaled * values, axis=0, keepdims=True)
    return inverse * scaled - values * (inverse * inverse * inverse * inner_mean)


def joined_sum(own_ref, other_ref):
    return own_ref[...].astype(f32) + other_ref[...].astype(f32)


def three_parts(value):
    high = value.astype(bf16).astype(f32)
    rest = value - high
    middle = rest.astype(bf16).astype(f32)
    return high, middle, rest - middle


def part_rows(value, first):
    row = lax.broadcasted_iota(jnp.int32, (8, value.shape[1]), 0)
    out = jnp.zeros((8, value.shape[1]), f32)
    for number, part in enumerate(three_parts(value)):
        out = jnp.where(row == first + number, part, out)
    return out


def causal_bias():
    key = lax.broadcasted_iota(jnp.int32, (BLOCK, BLOCK), 0)
    query = lax.broadcasted_iota(jnp.int32, (BLOCK, BLOCK), 1)
    return jnp.where(key <= query, 0.0, masked_value)


def reaches(segments, step, back):
    last = jnp.maximum((step - back + 1) * BLOCK - 1, 0)
    return (step >= back) & (segments[last] == segments[step * BLOCK])


def block_at(index):
    return pl.ds(pl.multiple_of(index * BLOCK, BLOCK), BLOCK)


def turn(upper, lower, cosine, sine):
    return upper * cosine - lower * sine, lower * cosine + upper * sine


def attention_forward(joined, slots, heads, segments, *refs):
    refs = list(refs)
    hidden = refs.pop(0)[...].astype(f32)
    if joined:
        hidden = hidden + joined_sum(refs.pop(0), refs.pop(0))
    gain_ref, wqkv_ref, wout_ref, cos_ref, sin_ref, segment_ref = refs[:6]
    refs = refs[6:]
    if joined:
        refs.pop(0)[...] = hidden
    (normed_out, query_out, key_out, turned_key_out, value_out, attended_out, partial_out,
     turned_value, tri_ref) = refs
    step = pl.program_id(0)
    here = block_at(step)

    @pl.when(step == 0)
    def _():
        tri_ref[...] = causal_bias()

    normed = normalise(hidden, gain_ref[...])
    normed_out[...] = normed
    projected = matmul(wqkv_ref[...], normed)
    cosine, sine = cos_ref[...], sin_ref[...]
    total = slots * heads
    half = HEAD // 2

    same = lax.broadcasted_iota(jnp.int32, (8, BLOCK), 0) == segment_ref[...]
    query_rows = jnp.where(same, 1.0, 0.0)
    key_rows = jnp.where(same, 0.0, masked_value)
    row = lax.broadcasted_iota(jnp.int32, (8, BLOCK), 0)
    minus_rows = jnp.where(row < 3, -1.0, 0.0)
    scale = LOG2E / math.sqrt(HEAD)

    def rows_of(head):
        return projected[head * HEAD : (head + 1) * HEAD]

    for h in range(total + slots):
        piece = rows_of(h)
        upper, lower = turn(piece[:half], piece[half:], cosine, sine)
        if h < total:
            base = h * LANES
            query_out[base : base + HEAD, :] = jnp.concatenate(
                [upper * scale, lower * scale], axis=0
            ).astype(bf16)
            query_out[base + HEAD : base + LANES, :] = jnp.concatenate(
                [query_rows, jnp.zeros((LANES - HEAD - 8, BLOCK), f32)], axis=0
            ).astype(bf16)
        else:
            s = h - total
            turned_key_out[s * HEAD : (s + 1) * HEAD, :] = jnp.concatenate(
                [upper, lower], axis=0
            ).astype(bf16)
            whole = jnp.concatenate(
                [upper, lower, key_rows, minus_rows, jnp.zeros((LANES - HEAD - 16, BLOCK), f32)],
                axis=0,
            )
            key_out[here, s * LANES : (s + 1) * LANES] = whole.T.astype(bf16)
    for s in range(slots):
        value = rows_of(total + slots + s)
        value = jnp.concatenate([value, jnp.ones((LANES - HEAD, BLOCK), f32)], axis=0)
        value_out[here, s * LANES : (s + 1) * LANES] = value.T.astype(bf16)
        turned_value[s * VROWS : (s + 1) * VROWS, here] = value[:VROWS].astype(bf16)

    def attend(blocks):
        width = blocks * BLOCK
        keys = pl.ds(pl.multiple_of((step + 1 - blocks) * BLOCK, BLOCK), width)
        for s in range(slots):
            key = key_out[keys, s * LANES : (s + 1) * LANES]
            value = turned_value[s * VROWS : (s + 1) * VROWS, keys]
            for j in range(heads):
                h = s * heads + j
                scores = matmul(key, query_out[h * LANES : (h + 1) * LANES, :])
                last = scores[width - BLOCK :] + tri_ref[...]
                if blocks > 1:
                    scores = jnp.concatenate([scores[: width - BLOCK], last], axis=0)
                else:
                    scores = last
                top = jnp.max(scores, axis=0, keepdims=True)
                weights = jnp.exp2(scores - top).astype(bf16)
                summed = matmul(value, weights)
                weight_sum = summed[HEAD : HEAD + 1]
                attended_out[h * HEAD : (h + 1) * HEAD, :] = (
                    summed[:HEAD] * (1.0 / weight_sum)
                ).astype(bf16)
                query_out[h * LANES + HEAD : h * LANES + HEAD + 16, :] = jnp.concatenate(
                    [query_rows, part_rows(top + jnp.log2(weight_sum), 0)], axis=0
                ).astype(bf16)

    one = reaches(segments, step, 1)
    two = reaches(segments, step, 2)
    pl.when(jnp.logical_not(one))(functools.partial(attend, 1))
    pl.when(one & jnp.logical_not(two))(functools.partial(attend, 2))
    pl.when(two)(functools.partial(attend, 3))
    partial_out[...] = matmul(wout_ref[...], attended_out[...], TN).astype(bf16)


def token_spec(rows, width=BLOCK):
    return pl.BlockSpec((rows, width), lambda i, *_: (0, i))


def full_spec(shape):
    return pl.BlockSpec(
        shape, lambda *_: (0,) * len(shape), pipeline_mode=pl.Buffered(buffer_count=1)
    )


def out_full_spec(shape):
    return pl.BlockSpec(shape, lambda *_: (0,) * len(shape))


shape_of = jax.ShapeDtypeStruct


def call_attention_forward(segments, parts, gain, wqkv, wout, cosine, sine, slots, heads):
    features, length = parts[0].shape
    joined = len(parts) == 3
    total = slots * heads
    big = shape_of((features, length), bf16)
    outs = [
        (big, token_spec(features)),
        (shape_of((total * LANES, length), bf16), token_spec(total * LANES)),
        (shape_of((length, slots * LANES), bf16), out_full_spec((length, slots * LANES))),
        (shape_of((slots * HEAD, length), bf16), token_spec(slots * HEAD)),
        (shape_of((length, slots * LANES), bf16), out_full_spec((length, slots * LANES))),
        (shape_of((total * HEAD, length), bf16), token_spec(total * HEAD)),
        (big, token_spec(features)),
    ]
    if joined:
        outs.insert(0, (shape_of((features, length), f32), token_spec(features)))
    return pl.pallas_call(
        functools.partial(attention_forward, joined, slots, heads),
        grid_spec=pltpu.PrefetchScalarGridSpec(
            num_scalar_prefetch=1,
            grid=(length // BLOCK,),
            in_specs=[token_spec(features)] * len(parts)
            + [full_spec(a.shape) for a in (gain, wqkv, wout)]
            + [token_spec(HEAD // 2)] * 2
            + [token_spec(1)],
            out_specs=[spec for _, spec in outs],
            scratch_shapes=[
                pltpu.VMEM((slots * VROWS, length), bf16),
                pltpu.VMEM((BLOCK, BLOCK), f32),
            ],
        ),
        out_shape=[shape for shape, _ in outs],
        compiler_params=pltpu.CompilerParams(vmem_limit_bytes=32 * MIB),
        name="attention_forward",
    )(segments, *parts, gain, wqkv, wout, cosine, sine, segments[None, :])


def ffn_forward(hidden_ref, own_ref, other_ref, gain_ref, gate_ref, up_ref, down_ref,
                middle_out, normed_out, gate_out, lift_out, inner_out, partial_out):
    middle = hidden_ref[...].astype(f32) + joined_sum(own_ref, other_ref)
    middle_out[...] = middle
    normed = normalise(middle, gain_ref[...])
    normed_out[...] = normed
    gate = matmul(gate_ref[...], normed, TN)
    lift = matmul(up_ref[...], normed, TN)
    gate_out[...] = gate.astype(bf16)
    lift_out[...] = lift.astype(bf16)
    inner = (gate * jax.nn.sigmoid(gate) * lift).astype(bf16)
    inner_out[...] = inner
    partial_out[...] = matmul(down_ref[...], inner).astype(bf16)


def call_ffn_forward(hidden, own, other, gain, w_gate, w_up, w_down):
    features, length = hidden.shape
    units = w_gate.shape[1]
    spec = functools.partial(token_spec, width=FFN_BLOCK)
    return pl.pallas_call(
        ffn_forward,
        grid=(length // FFN_BLOCK,),
        in_specs=[spec(features)] * 3 + [full_spec(a.shape) for a in (gain, w_gate, w_up, w_down)],
        out_specs=[spec(features)] * 2 + [spec(units)] * 3 + [spec(features)],
        out_shape=[shape_of((features, length), f32), shape_of((features, length), bf16)]
        + [shape_of((units, length), bf16)] * 3
        + [shape_of((features, length), bf16)],
        compiler_params=pltpu.CompilerParams(vmem_limit_bytes=40 * MIB),
        name="ffn_forward",
    )(hidden, own, other, gain, w_gate, w_up, w_down)


def ffn_backward(joined, *refs):
    refs = list(refs)
    grad = refs.pop(0)[...].astype(f32)
    if joined:
        hidden_ref, own_ref, other_ref, gain_ref = refs[:4]
        refs = refs[4:]
        grad = grad + norm_back(
            hidden_ref[...].astype(f32), gain_ref[...], joined_sum(own_ref, other_ref)
        )
    gate_in, lift_in, gate_ref, up_ref, down_ref = refs[:5]
    refs = refs[5:]
    ffn_grad = grad.astype(bf16)
    if joined:
        refs.pop(0)[...] = grad
        refs.pop(0)[...] = ffn_grad
    grad_gate_out, grad_lift_out, partial_out = refs
    grad_inner = matmul(down_ref[...], ffn_grad, TN)
    gate = gate_in[...].astype(f32)
    lift = lift_in[...].astype(f32)
    sigmoid = jax.nn.sigmoid(gate)
    grad_gate = (grad_inner * lift * sigmoid * (1.0 + gate * (1.0 - sigmoid))).astype(bf16)
    grad_lift = (grad_inner * gate * sigmoid).astype(bf16)
    grad_gate_out[...] = grad_gate
    grad_lift_out[...] = grad_lift
    partial = matmul(gate_ref[...], grad_gate) + matmul(up_ref[...], grad_lift)
    partial_out[...] = partial.astype(bf16)


def call_ffn_backward(grad, joint, gate, lift, w_gate, w_up, w_down):
    features, length = grad.shape
    units = w_gate.shape[1]
    joined = joint is not None
    spec = functools.partial(token_spec, width=FFN_BLOCK)
    extra_in, extra_specs, extra_outs = [], [], []
    if joined:
        extra_in = list(joint)
        extra_specs = [spec(features)] * 3 + [full_spec(joint[3].shape)]
        extra_outs = [shape_of((features, length), f32), shape_of((features, length), bf16)]
    return pl.pallas_call(
        functools.partial(ffn_backward, joined),
        grid=(length // FFN_BLOCK,),
        in_specs=[spec(features)] + extra_specs + [spec(units)] * 2
        + [full_spec(a.shape) for a in (w_gate, w_up, w_down)],
        out_specs=[spec(features)] * len(extra_outs) + [spec(units)] * 2 + [spec(features)],
        out_shape=extra_outs + [shape_of((units, length), bf16)] * 2
        + [shape_of((features, length), bf16)],
        compiler_params=pltpu.CompilerParams(vmem_limit_bytes=40 * MIB),
        name="ffn_backward",
    )(grad, *extra_in, gate, lift, w_gate, w_up, w_down)


def attention_backward(slots, heads, segments, grad_ref, own_ref, other_ref, middle_ref, gain_ref,
                       wout_ref, wqkv_ref, attended_ref, query_ref, key_ref, turned_key_ref, value_ref,
                       cos_ref, sin_ref,
                       grad_out, attn_grad_out, projected_out, partial_out,
                       key_total, value_total, query_total, grad_heads, tri_ref):
    step = pl.num_programs(0) - 1 - pl.program_id(0)
    total = slots * heads
    half = HEAD // 2

    @pl.when(pl.program_id(0) == 0)
    def _():
        key_total[...] = jnp.zeros_like(key_total)
        value_total[...] = jnp.zeros_like(value_total)
        tri_ref[...] = causal_bias()

    grad = grad_ref[...].astype(f32)
    grad = grad + norm_back(middle_ref[...], gain_ref[...], joined_sum(own_ref, other_ref))
    grad_out[...] = grad
    attn_grad = grad.astype(bf16)
    attn_grad_out[...] = attn_grad
    grad_attended = matmul(wout_ref[...], attn_grad).astype(bf16)
    for h in range(total):
        s, j = divmod(h, heads)
        mine = grad_attended[h * HEAD : (h + 1) * HEAD]
        out = attended_ref[h * HEAD : (h + 1) * HEAD, :]
        delta = jnp.sum(mine.astype(f32) * out.astype(f32), axis=0, keepdims=True)
        lanes = slice(j * BLOCK, (j + 1) * BLOCK)
        grad_heads[s, :HEAD, lanes] = mine
        grad_heads[s, HEAD:, lanes] = jnp.concatenate(
            [part_rows(-delta, 0), jnp.zeros((LANES - HEAD - 8, BLOCK), f32)], axis=0
        ).astype(bf16)

    for s in range(slots):
        columns = slice(s * LANES, (s + 1) * LANES)
        features = slice(s * HEAD, (s + 1) * HEAD)

        def visit(back, s=s, columns=columns, features=features):
            keys = block_at(step - back)
            queries = jnp.concatenate(
                [query_ref[(s * heads + j) * LANES : (s * heads + j + 1) * LANES, :] for j in range(heads)],
                axis=1,
            )
            grads = grad_heads[s]
            scores = matmul(key_ref[keys, columns], queries)
            if back == 0:
                scores = scores + jnp.concatenate([tri_ref[...]] * heads, axis=1)
            weights = jnp.exp2(scores)
            value_total[features, keys] += matmul(grads[:HEAD], weights.astype(bf16), NT)
            grad_weights = matmul(value_ref[keys, columns], grads)
            grad_scores = (weights * grad_weights).astype(bf16)
            key_total[features, keys] += matmul(queries[:HEAD], grad_scores, NT)
            update = matmul(turned_key_ref[features, keys], grad_scores)
            if back == 0:
                query_total[s] = update
            else:
                query_total[s] += update

        visit(0)
        for back in (1, 2):
            pl.when(reaches(segments, step, back))(functools.partial(visit, back))

    cosine, sine = cos_ref[...], sin_ref[...]
    here = block_at(step)
    for h in range(total + 2 * slots):
        if h < total:
            s, j = divmod(h, heads)
            piece = query_total[s, :, j * BLOCK : (j + 1) * BLOCK] * (1.0 / math.sqrt(HEAD))
        elif h < total + slots:
            s = h - total
            piece = key_total[s * HEAD : (s + 1) * HEAD, here] * LN2
        else:
            s = h - total - slots
            piece = value_total[s * HEAD : (s + 1) * HEAD, here]
        if h < total + slots:
            upper, lower = turn(piece[:half], piece[half:], cosine, -sine)
            piece = jnp.concatenate([upper, lower], axis=0)
        projected_out[h * HEAD : (h + 1) * HEAD, :] = piece.astype(bf16)
    partial_out[...] = matmul(wqkv_ref[...], projected_out[...], TN).astype(bf16)


def call_attention_backward(segments, grad, own, other, middle, gain, wout, wqkv, attended, query, key,
                            turned_key, value, cosine, sine, slots, heads):
    features, length = middle.shape
    count = length // BLOCK

    def spec(rows):
        return pl.BlockSpec((rows, BLOCK), lambda i, *_: (0, count - 1 - i))

    return pl.pallas_call(
        functools.partial(attention_backward, slots, heads),
        grid_spec=pltpu.PrefetchScalarGridSpec(
            num_scalar_prefetch=1,
            grid=(count,),
            in_specs=[spec(features)] * 4
            + [full_spec(a.shape) for a in (gain, wout, wqkv)]
            + [spec(attended.shape[0]), spec(query.shape[0])]
            + [full_spec(a.shape) for a in (key, turned_key, value)]
            + [spec(HEAD // 2)] * 2,
            out_specs=[spec(features)] * 2 + [spec(wqkv.shape[0]), spec(features)],
            scratch_shapes=[
                pltpu.VMEM((slots * HEAD, length), f32),
                pltpu.VMEM((slots * HEAD, length), f32),
                pltpu.VMEM((slots, HEAD, heads * BLOCK), f32),
                pltpu.VMEM((slots, LANES, heads * BLOCK), bf16),
                pltpu.VMEM((BLOCK, BLOCK), f32),
            ],
        ),
        out_shape=[
            shape_of((features, length), f32), shape_of((features, length), bf16),
            shape_of((wqkv.shape[0], length), bf16), shape_of((features, length), bf16),
        ],
        compiler_params=pltpu.CompilerParams(vmem_limit_bytes=40 * MIB),
        name="attention_backward",
    )(segments, grad, own, other, middle, gain, wout, wqkv, attended, query, key, turned_key, value,
      cosine, sine)


def weight_grad(order, rows, count, *refs):
    lefts, rights = refs[:count], refs[count : 2 * count]
    out_ref = refs[2 * count]
    total = matmul(lefts[0][...], rights[0][...], NT)
    for number in range(1, count):
        total = total + matmul(lefts[number][...], rights[number][...], NT)
    width = total.shape[1]
    total = total.astype(out_ref.dtype)
    for place, shard in enumerate(order):
        out_ref[place, :rows, :width] = total[shard * rows : (shard + 1) * rows]
        if out_ref.shape[1] > rows:
            out_ref[place, rows:, :] = jnp.zeros(
                (out_ref.shape[1] - rows, out_ref.shape[2]), out_ref.dtype
            )
        if out_ref.shape[2] > width:
            out_ref[place, :rows, width:] = jnp.zeros(
                (rows, out_ref.shape[2] - width), out_ref.dtype
            )


def call_weight_grad(lefts, rights, order, width):
    features, length = lefts[0].shape
    columns = rights[0].shape[0]
    steps = -(-columns // width)
    size = len(order)
    rows = features // size
    padded = -(-rows // 16) * 16
    count = len(lefts)
    out_width = -(-width // LANES) * LANES
    return pl.pallas_call(
        functools.partial(weight_grad, order, rows, count),
        grid=(steps,),
        in_specs=[full_spec((features, length))] * count
        + [pl.BlockSpec((width, length), lambda i: (i, 0))] * count,
        out_specs=pl.BlockSpec((size, padded, out_width), lambda i: (0, 0, i)),
        out_shape=shape_of((size, padded, steps * out_width), bf16),
        compiler_params=pltpu.CompilerParams(vmem_limit_bytes=32 * MIB),
        name="weight_grad",
    )(*lefts, *rights)


def finish(grad_ref, hidden_ref, own_ref, other_ref, gain_ref, out_ref):
    out_ref[...] = grad_ref[...] + norm_back(
        hidden_ref[...].astype(f32), gain_ref[...], joined_sum(own_ref, other_ref)
    )


def call_finish(grad, hidden, own, other, gain):
    features, length = grad.shape
    return pl.pallas_call(
        finish,
        grid=(length // BLOCK,),
        in_specs=[token_spec(features)] * 4 + [full_spec(gain.shape)],
        out_specs=token_spec(features),
        out_shape=shape_of((features, length), f32),
        compiler_params=pltpu.CompilerParams(vmem_limit_bytes=32 * MIB),
        name="finish",
    )(grad, hidden, own, other, gain)


def gather_groups(owner, device, query_ref, key_ref, value_ref, out_ref, wqkv_out, wout_out):
    slot = pl.program_id(0)
    slots = pl.num_programs(0)
    _, held = group_of(slot, owner, device)
    group_cols, head = query_ref.shape[1], key_ref.shape[1]

    def place(first, height, piece):
        rows = pl.ds(pl.multiple_of(first, 16), height)
        return rows, jnp.where(held, piece, jnp.zeros_like(piece))

    rows, piece = place(slot * group_cols, group_cols, query_ref[0])
    wqkv_out[rows, :] = piece
    wout_out[rows, :] = place(slot * group_cols, group_cols, out_ref[0])[1]
    rows, piece = place(slots * group_cols + slot * head, head, key_ref[0])
    wqkv_out[rows, :] = piece
    rows, piece = place(slots * (group_cols + head) + slot * head, head, value_ref[0])
    wqkv_out[rows, :] = piece


def group_of(slot, owner, device):
    found, count = 0, 0
    for group in range(owner.shape[0]):
        mine = owner[group] == device[0]
        found = jnp.where(mine & (count == slot), group, found)
        count = count + jnp.where(mine, 1, 0)
    return found, count > slot


def call_gather_groups(owner, device, w_query, w_key, w_value, w_out, slots):
    features = w_query.shape[2]
    arrays = (w_query, w_key, w_value, w_out)
    joint = slots * (w_query.shape[1] + w_key.shape[1] + w_value.shape[1])
    outs = [(joint, features), (slots * w_out.shape[1], features)]
    return pl.pallas_call(
        gather_groups,
        grid_spec=pltpu.PrefetchScalarGridSpec(
            num_scalar_prefetch=2,
            grid=(slots,),
            in_specs=[
                pl.BlockSpec(
                    (1,) + a.shape[1:], lambda s, owner, device: (group_of(s, owner, device)[0], 0, 0)
                )
                for a in arrays
            ],
            out_specs=[out_full_spec(o) for o in outs],
        ),
        out_shape=[shape_of(o, bf16) for o in outs],
        name="gather_groups",
    )(owner, device, *arrays)


def rotary_tables(length):
    position = np.arange(length, dtype=np.float64)[None, :]
    column = np.arange(HEAD // 2, dtype=np.float64)[:, None]
    angles = position * np.exp(column * (-2.0 * math.log(10000.0) / HEAD))
    return jnp.asarray(np.cos(angles), f32), jnp.asarray(np.sin(angles), f32)


def exchange(own):
    return lax.ppermute(own, "mp", [(0, 1), (1, 0)])


def stage_plans(bit_count):
    if bit_count < 4:
        return [[[bit] for bit in range(bit_count)]] * 3
    tail = [[bit] for bit in range(4, bit_count)]
    return [
        [[0], [1], [2, 3]] + tail,
        [[1], [0], [2, 3]] + tail,
        [[2], [0], [1], [3]] + tail,
    ]


def shard_order(plan):
    bits = [bit for stage in plan for bit in stage]
    order = []
    for place in range(1 << len(bits)):
        shard = 0
        for rank, bit in enumerate(bits):
            if place >> (len(bits) - 1 - rank) & 1:
                shard |= 1 << bit
        order.append(shard)
    return order


def reduce_stage(current, stage, last):
    size = lax.axis_size("dp")
    index = lax.axis_index("dp")
    mine = 0
    for bit in stage:
        mine = mine * 2 + ((index >> bit) & 1)
    ways = 1 << len(stage)
    pieces = current.shape[0] // ways
    total = lax.dynamic_slice_in_dim(current, mine * pieces, pieces, 0).astype(f32)
    received = []
    for offset in range(1, ways):
        mask = 0
        for rank, bit in enumerate(stage):
            if offset >> (len(stage) - 1 - rank) & 1:
                mask |= 1 << bit
        outgoing = lax.dynamic_slice_in_dim(current, (mine ^ offset) * pieces, pieces, 0)
        received.append(lax.ppermute(outgoing, "dp", [(i, i ^ mask) for i in range(size)]))
    for piece in received:
        total = total + piece.astype(f32)
    return total if last else total.astype(bf16)


def reduce_scatter(payload, plan):
    for number, stage in enumerate(plan):
        payload = reduce_stage(payload, stage, number == len(plan) - 1)
    return payload[0]


def per_device(
    tokens_in,
    segment_ids,
    kv_owner,
    w_query,
    w_key,
    w_value,
    w_out,
    attn_gain,
    w_gate,
    w_up,
    w_down,
    ffn_gain,
    cotangent,
):
    features = tokens_in.shape[2]
    length = tokens_in.shape[1]
    group_cols = w_query.shape[2]
    heads = group_cols // HEAD
    slots = (kv_owner.shape[0] + lax.axis_size("mp") - 1) // lax.axis_size("mp")
    size = lax.axis_size("dp")
    rows = features // size

    device = lax.axis_index("mp").astype(jnp.int32)[None]
    wqkv, wout = call_gather_groups(
        kv_owner, device, *(jnp.swapaxes(w, 1, 2) for w in (w_query, w_key, w_value)), w_out, slots
    )
    w_down = w_down.T
    segments = segment_ids[0]
    cosine, sine = rotary_tables(length)
    gain_one, gain_two = (
        jnp.broadcast_to(gain.astype(f32)[:, None], (features, LANES)) for gain in (attn_gain, ffn_gain)
    )

    parts = (tokens_in[0].T,)
    saved = []
    for _ in range(REPEAT):
        outs = list(call_attention_forward(segments, parts, gain_one, wqkv, wout, cosine, sine, slots, heads))
        hidden = outs.pop(0) if len(parts) == 3 else parts[0]
        normed, query, key, turned_key, value, attended, partial = outs
        middle, normed_two, gate, lift, inner, partial_two = call_ffn_forward(
            hidden, partial, exchange(partial), gain_two, w_gate, w_up, w_down
        )
        parts = (middle, partial_two, exchange(partial_two))
        saved.append((hidden, normed, query, key, turned_key, value, attended, middle, normed_two, gate, lift, inner))
    tokens_out = (parts[0] + (parts[1].astype(f32) + parts[2].astype(f32))).astype(bf16)

    plans = stage_plans(size.bit_length() - 1)
    orders = [shard_order(plan) for plan in plans]
    joint = None
    grad = cotangent[0].T
    lefts, rights = [], []
    for r in reversed(range(REPEAT)):
        hidden, normed, query, key, turned_key, value, attended, middle, normed_two, gate, lift, inner = saved[r]
        outs = list(call_ffn_backward(grad, joint, gate, lift, w_gate, w_up, w_down))
        if joint is None:
            ffn_grad = grad
        else:
            grad = outs.pop(0)
            ffn_grad = outs.pop(0)
        grad_gate, grad_lift, partial = outs
        grad, attn_grad, projected, partial_two = call_attention_backward(
            segments, grad, partial, exchange(partial), middle, gain_two, wout, wqkv, attended, query,
            key, turned_key, value, cosine, sine, slots, heads,
        )
        joint = (hidden, partial_two, exchange(partial_two), gain_one)
        lefts.append((normed_two, ffn_grad, attn_grad, normed))
        rights.append((grad_gate, grad_lift, inner, attended, projected))
    grad_in = call_finish(grad, *joint)
    lefts = list(zip(*lefts))
    rights = list(zip(*rights))
    out_cols = slots * group_cols
    gate_total = reduce_scatter(call_weight_grad(lefts[0], rights[0], orders[0], 256), plans[0])
    up_total = reduce_scatter(call_weight_grad(lefts[0], rights[1], orders[1], 256), plans[1])
    down_total = reduce_scatter(call_weight_grad(lefts[1], rights[2], orders[2], 256), plans[2])
    out_total = reduce_scatter(call_weight_grad(lefts[2], rights[3], orders[1], out_cols), plans[1])
    qkv_total = reduce_scatter(
        call_weight_grad(lefts[3], rights[4], orders[0], wqkv.shape[0]), plans[0]
    )

    start = lax.axis_index("dp") * rows

    def my_rows(weights):
        return lax.dynamic_slice_in_dim(weights, start, rows, 0).astype(f32)

    gate_total, up_total, down_total, out_total, qkv_total = (
        total[:rows] for total in (gate_total, up_total, down_total, out_total, qkv_total)
    )
    qkv_total = qkv_total[:, : wqkv.shape[0]]
    wqkv_rows = lax.dynamic_slice_in_dim(wqkv, start, rows, 1).T.astype(f32)
    gains = jnp.stack([
        jnp.sum(qkv_total * wqkv_rows, axis=1),
        jnp.sum(gate_total * my_rows(w_gate) + up_total * my_rows(w_up), axis=1),
    ])
    gains = gains + exchange(gains)
    gains = gains / lax.dynamic_slice_in_dim(jnp.stack([attn_gain, ffn_gain]), start, rows, 1).astype(f32)

    def by_slot(array):
        return jnp.moveaxis(array.reshape(rows, slots, -1), 1, 0)

    key_start = slots * group_cols
    value_start = key_start + slots * HEAD
    return (
        tokens_out.T[None],
        grad_in.T[None],
        by_slot(qkv_total[:, :key_start]),
        by_slot(qkv_total[:, key_start:value_start]),
        by_slot(qkv_total[:, value_start:]),
        jnp.swapaxes(by_slot(out_total[:, :out_cols]), 1, 2),
        gate_total,
        up_total,
        down_total.T,
        gains[0],
        gains[1],
    )


def solution(mesh):
    in_specs = (
        P("dp", None, None),
        P("dp", None),
        P(),
        P(),
        P(),
        P(),
        P(),
        P(),
        P(None, "mp"),
        P(None, "mp"),
        P("mp", None),
        P(),
        P("dp", None, None),
    )
    out_specs = (
        P("dp", None, None),
        P("dp", None, None),
        P("mp", "dp", None),
        P("mp", "dp", None),
        P("mp", "dp", None),
        P("mp", None, "dp"),
        P("dp", "mp"),
        P("dp", "mp"),
        P("mp", "dp"),
        P("dp"),
        P("dp"),
    )
    return jax.shard_map(
        per_device, mesh=mesh, in_specs=in_specs, out_specs=out_specs, check_vma=False
    )
```

```python
import functools
import math

import jax
import jax.numpy as jnp
import numpy as np
from jax import lax
from jax.experimental import pallas as pl
from jax.experimental.pallas import tpu as pltpu
from jax.sharding import PartitionSpec as P

REPEAT = 2
BLOCK = 256
FFN_BLOCK = 512
LANES = 128
HEAD = 64
GROUP = 3
VROWS = 80
epsilon = 1e-05
masked_value = -1e30
LOG2E = math.log2(math.e)
LN2 = math.log(2.0)
f32 = jnp.float32
bf16 = jnp.bfloat16
NN = (((1,), (0,)), ((), ()))
NT = (((1,), (1,)), ((), ()))
TN = (((0,), (0,)), ((), ()))
MIB = 1024 * 1024


def matmul(a, b, dims=NN):
    return lax.dot_general(a, b, dims, preferred_element_type=f32)


def wide(column, width):
    return jnp.concatenate([column] * (width // LANES), axis=1)


def inverse_rms(values):
    return lax.rsqrt(jnp.mean(values * values, axis=0, keepdims=True) + epsilon)


def normalise(values, gain):
    return (values * inverse_rms(values) * wide(gain, values.shape[1])).astype(bf16)


def norm_back(values, gain, grad_normed):
    inverse = inverse_rms(values)
    scaled = grad_normed * wide(gain, values.shape[1])
    inner_mean = jnp.mean(scaled * values, axis=0, keepdims=True)
    return inverse * scaled - values * (inverse * inverse * inverse * inner_mean)


def joined_sum(own_ref, other_ref):
    return own_ref[...].astype(f32) + other_ref[...].astype(f32)


def three_parts(value):
    high = value.astype(bf16).astype(f32)
    rest = value - high
    middle = rest.astype(bf16).astype(f32)
    return high, middle, rest - middle


def part_rows(value, first):
    row = lax.broadcasted_iota(jnp.int32, (8, value.shape[1]), 0)
    out = jnp.zeros((8, value.shape[1]), f32)
    for number, part in enumerate(three_parts(value)):
        out = jnp.where(row == first + number, part, out)
    return out


def causal_bias(heads):
    key = lax.broadcasted_iota(jnp.int32, (BLOCK, heads * BLOCK), 0)
    query = lax.broadcasted_iota(jnp.int32, (BLOCK, heads * BLOCK), 1) % BLOCK
    return jnp.where(key <= query, 0.0, masked_value)


def reaches(segments, step, back):
    last = jnp.maximum((step - back + 1) * BLOCK - 1, 0)
    return (step >= back) & (segments[last] == segments[step * BLOCK])


def block_at(index):
    return pl.ds(pl.multiple_of(index * BLOCK, BLOCK), BLOCK)


def turn(upper, lower, cosine, sine):
    return upper * cosine - lower * sine, lower * cosine + upper * sine


def attention_forward(joined, slots, heads, segments, *refs):
    refs = list(refs)
    hidden = refs.pop(0)[...].astype(f32)
    if joined:
        hidden = hidden + joined_sum(refs.pop(0), refs.pop(0))
    gain_ref, wqkv_ref, wout_ref, cos_ref, sin_ref, segment_ref = refs[:6]
    refs = refs[6:]
    if joined:
        refs.pop(0)[...] = hidden
    (normed_out, query_out, key_out, turned_key_out, value_out, attended_out, partial_out,
     turned_value, tri_ref) = refs
    step = pl.program_id(0)
    here = block_at(step)

    @pl.when(step == 0)
    def _():
        tri_ref[...] = causal_bias(heads)

    normed = normalise(hidden, gain_ref[...])
    normed_out[...] = normed
    projected = matmul(wqkv_ref[...], normed)
    cosine, sine = cos_ref[...], sin_ref[...]
    half = HEAD // 2

    same = lax.broadcasted_iota(jnp.int32, (8, BLOCK), 0) == segment_ref[...]
    query_rows = jnp.where(same, 1.0, 0.0)
    key_rows = jnp.where(same, 0.0, masked_value)
    row = lax.broadcasted_iota(jnp.int32, (8, BLOCK), 0)
    minus_rows = jnp.where(row < 3, -1.0, 0.0)
    scale = LOG2E / math.sqrt(HEAD)
    query_fill = jnp.concatenate(
        [query_rows, jnp.zeros((LANES - HEAD - 8, BLOCK), f32)], axis=0
    ).astype(bf16)

    for s in range(slots):
        for j in range(heads + 2):
            first = (s * (heads + 2) + j) * HEAD
            piece = projected[first : first + HEAD]
            if j > heads:
                value = jnp.concatenate([piece, jnp.ones((LANES - HEAD, BLOCK), f32)], axis=0)
                value_out[here, s * LANES : (s + 1) * LANES] = value.T.astype(bf16)
                turned_value[s * VROWS : (s + 1) * VROWS, here] = value[:VROWS].astype(bf16)
                continue
            upper, lower = turn(piece[:half], piece[half:], cosine, sine)
            if j < heads:
                lanes = slice(j * BLOCK, (j + 1) * BLOCK)
                query_out[0, s, :HEAD, lanes] = jnp.concatenate(
                    [upper * scale, lower * scale], axis=0
                ).astype(bf16)
                query_out[0, s, HEAD:, lanes] = query_fill
            else:
                turned_key_out[s * HEAD : (s + 1) * HEAD, :] = jnp.concatenate(
                    [upper, lower], axis=0
                ).astype(bf16)
                whole = jnp.concatenate(
                    [upper, lower, key_rows, minus_rows, jnp.zeros((LANES - HEAD - 16, BLOCK), f32)],
                    axis=0,
                )
                key_out[here, s * LANES : (s + 1) * LANES] = whole.T.astype(bf16)

    query_rows = jnp.concatenate([query_rows] * heads, axis=1)

    def attend(blocks):
        width = blocks * BLOCK
        keys = pl.ds(pl.multiple_of((step + 1 - blocks) * BLOCK, BLOCK), width)
        scores = [
            matmul(key_out[keys, s * LANES : (s + 1) * LANES], query_out[0, s]) for s in range(slots)
        ]
        tops, weights = [], []
        for score in scores:
            last = score[width - BLOCK :] + tri_ref[...]
            if blocks > 1:
                score = jnp.concatenate([score[: width - BLOCK], last], axis=0)
            else:
                score = last
            tops.append(jnp.max(score, axis=0, keepdims=True))
            weights.append(jnp.exp2(score - tops[-1]).astype(bf16))
        summed = [
            matmul(turned_value[s * VROWS : (s + 1) * VROWS, keys], weights[s]) for s in range(slots)
        ]
        for s in range(slots):
            weight_sum = summed[s][HEAD : HEAD + 1]
            out = (summed[s][:HEAD] * (1.0 / weight_sum)).astype(bf16)
            for j in range(heads):
                first = (s * heads + j) * HEAD
                attended_out[first : first + HEAD, :] = out[:, j * BLOCK : (j + 1) * BLOCK]
            query_out[0, s, HEAD : HEAD + 16, :] = jnp.concatenate(
                [query_rows, part_rows(tops[s] + jnp.log2(weight_sum), 0)], axis=0
            ).astype(bf16)

    one = reaches(segments, step, 1)
    two = reaches(segments, step, 2)
    pl.when(jnp.logical_not(one))(functools.partial(attend, 1))
    pl.when(one & jnp.logical_not(two))(functools.partial(attend, 2))
    pl.when(two)(functools.partial(attend, 3))
    partial_out[...] = matmul(wout_ref[...], attended_out[...], TN).astype(bf16)


def chunks(width):
    return [slice(start, start + 256) for start in range(0, width, 256)]


def cost(flops, *arrays):
    size = sum(math.prod(a.shape) * a.dtype.itemsize for a in arrays)
    return pl.CostEstimate(flops=int(flops), bytes_accessed=size, transcendentals=0)


def token_spec(rows, width=BLOCK):
    return pl.BlockSpec((rows, width), lambda i, *_: (0, i))


def full_spec(shape):
    return pl.BlockSpec(
        shape, lambda *_: (0,) * len(shape), pipeline_mode=pl.Buffered(buffer_count=1)
    )


def out_full_spec(shape):
    return pl.BlockSpec(shape, lambda *_: (0,) * len(shape))


shape_of = jax.ShapeDtypeStruct


def call_attention_forward(segments, parts, gain, wqkv, wout, cosine, sine, slots, heads):
    features, length = parts[0].shape
    joined = len(parts) == 3
    total = slots * heads
    big = shape_of((features, length), bf16)
    outs = [
        (big, token_spec(features)),
        (
            shape_of((length // BLOCK, slots, LANES, heads * BLOCK), bf16),
            pl.BlockSpec((1, slots, LANES, heads * BLOCK), lambda i, *_: (i, 0, 0, 0)),
        ),
        (shape_of((length, slots * LANES), bf16), out_full_spec((length, slots * LANES))),
        (shape_of((slots * HEAD, length), bf16), token_spec(slots * HEAD)),
        (shape_of((length, slots * LANES), bf16), out_full_spec((length, slots * LANES))),
        (shape_of((total * HEAD, length), bf16), token_spec(total * HEAD)),
        (big, token_spec(features)),
    ]
    if joined:
        outs.insert(0, (shape_of((features, length), f32), token_spec(features)))
    return pl.pallas_call(
        functools.partial(attention_forward, joined, slots, heads),
        grid_spec=pltpu.PrefetchScalarGridSpec(
            num_scalar_prefetch=1,
            grid=(length // BLOCK,),
            in_specs=[token_spec(features)] * len(parts)
            + [full_spec(a.shape) for a in (gain, wqkv, wout)]
            + [token_spec(HEAD // 2)] * 2
            + [token_spec(1)],
            out_specs=[spec for _, spec in outs],
            scratch_shapes=[
                pltpu.VMEM((slots * VROWS, length), bf16),
                pltpu.VMEM((BLOCK, heads * BLOCK), f32),
            ],
        ),
        out_shape=[shape for shape, _ in outs],
        compiler_params=pltpu.CompilerParams(vmem_limit_bytes=32 * MIB),
        cost_estimate=cost(2 * length * features * (wqkv.shape[0] + wout.shape[0]) + 12e9, *parts),
        name="attention_forward",
    )(segments, *parts, gain, wqkv, wout, cosine, sine, segments[None, :])


def ffn_forward(hidden_ref, own_ref, other_ref, gain_ref, gate_ref, up_ref, down_ref,
                middle_out, normed_out, gate_out, lift_out, inner_out, partial_out):
    middle = hidden_ref[...].astype(f32) + joined_sum(own_ref, other_ref)
    middle_out[...] = middle
    normed = normalise(middle, gain_ref[...])
    normed_out[...] = normed
    for chunk in chunks(gate_ref.shape[1]):
        gate = matmul(gate_ref[:, chunk], normed, TN)
        lift = matmul(up_ref[:, chunk], normed, TN)
        gate_out[chunk, :] = gate.astype(bf16)
        lift_out[chunk, :] = lift.astype(bf16)
        inner_out[chunk, :] = (gate * jax.nn.sigmoid(gate) * lift).astype(bf16)
    partial_out[...] = matmul(down_ref[...], inner_out[...]).astype(bf16)


def call_ffn_forward(hidden, own, other, gain, w_gate, w_up, w_down):
    features, length = hidden.shape
    units = w_gate.shape[1]
    spec = functools.partial(token_spec, width=FFN_BLOCK)
    return pl.pallas_call(
        ffn_forward,
        grid=(length // FFN_BLOCK,),
        in_specs=[spec(features)] * 3 + [full_spec(a.shape) for a in (gain, w_gate, w_up, w_down)],
        out_specs=[spec(features)] * 2 + [spec(units)] * 3 + [spec(features)],
        out_shape=[shape_of((features, length), f32), shape_of((features, length), bf16)]
        + [shape_of((units, length), bf16)] * 3
        + [shape_of((features, length), bf16)],
        compiler_params=pltpu.CompilerParams(vmem_limit_bytes=40 * MIB),
        cost_estimate=cost(6 * length * features * units, hidden),
        name="ffn_forward",
    )(hidden, own, other, gain, w_gate, w_up, w_down)


def ffn_backward(grad_ref, gate_in, lift_in, gate_ref, up_ref, down_ref,
                 grad_gate_out, grad_lift_out, partial_out):
    ffn_grad = grad_ref[...]
    for chunk in chunks(gate_ref.shape[1]):
        grad_inner = matmul(down_ref[:, chunk], ffn_grad, TN)
        gate = gate_in[chunk, :].astype(f32)
        lift = lift_in[chunk, :].astype(f32)
        sigmoid = jax.nn.sigmoid(gate)
        grad_gate = grad_inner * lift * sigmoid * (1.0 + gate * (1.0 - sigmoid))
        grad_gate_out[chunk, :] = grad_gate.astype(bf16)
        grad_lift_out[chunk, :] = (grad_inner * gate * sigmoid).astype(bf16)
    partial = matmul(gate_ref[...], grad_gate_out[...]) + matmul(up_ref[...], grad_lift_out[...])
    partial_out[...] = partial.astype(bf16)


def call_ffn_backward(grad, gate, lift, w_gate, w_up, w_down):
    features, length = grad.shape
    units = w_gate.shape[1]
    spec = functools.partial(token_spec, width=FFN_BLOCK)
    return pl.pallas_call(
        ffn_backward,
        grid=(length // FFN_BLOCK,),
        in_specs=[spec(features)] + [spec(units)] * 2
        + [full_spec(a.shape) for a in (w_gate, w_up, w_down)],
        out_specs=[spec(units)] * 2 + [spec(features)],
        out_shape=[shape_of((units, length), bf16)] * 2 + [shape_of((features, length), bf16)],
        compiler_params=pltpu.CompilerParams(vmem_limit_bytes=40 * MIB),
        cost_estimate=cost(6 * length * features * units, grad),
        name="ffn_backward",
    )(grad, gate, lift, w_gate, w_up, w_down)


def attention_entry(slots, heads, grad_ref, own_ref, other_ref, middle_ref, gain_ref, wout_ref,
                    attended_ref, grad_out, attn_grad_out, heads_out):
    grad = grad_ref[...].astype(f32)
    grad = grad + norm_back(middle_ref[...], gain_ref[...], joined_sum(own_ref, other_ref))
    grad_out[...] = grad
    attn_grad = grad.astype(bf16)
    attn_grad_out[...] = attn_grad
    grad_attended = matmul(wout_ref[...], attn_grad).astype(bf16)
    zeros = jnp.zeros((LANES - HEAD - 8, BLOCK), f32)
    for s in range(slots):
        for j in range(heads):
            first = (s * heads + j) * HEAD
            mine = grad_attended[first : first + HEAD]
            out = attended_ref[first : first + HEAD, :]
            delta = jnp.sum(mine.astype(f32) * out.astype(f32), axis=0, keepdims=True)
            lanes = slice(j * BLOCK, (j + 1) * BLOCK)
            heads_out[0, s, :HEAD, lanes] = mine
            heads_out[0, s, HEAD:, lanes] = jnp.concatenate(
                [part_rows(-delta, 0), zeros], axis=0
            ).astype(bf16)


def call_attention_entry(grad, own, other, middle, gain, wout, attended, slots, heads):
    features, length = middle.shape
    wide_heads = heads * BLOCK
    return pl.pallas_call(
        functools.partial(attention_entry, slots, heads),
        grid=(length // BLOCK,),
        in_specs=[token_spec(features)] * 4
        + [full_spec(a.shape) for a in (gain, wout)]
        + [token_spec(attended.shape[0])],
        out_specs=[token_spec(features)] * 2
        + [pl.BlockSpec((1, slots, LANES, wide_heads), lambda i: (i, 0, 0, 0))],
        out_shape=[
            shape_of((features, length), f32), shape_of((features, length), bf16),
            shape_of((length // BLOCK, slots, LANES, wide_heads), bf16),
        ],
        compiler_params=pltpu.CompilerParams(vmem_limit_bytes=32 * MIB),
        cost_estimate=cost(2 * length * features * wout.shape[0], grad, own, other, middle),
        name="attention_entry",
    )(grad, own, other, middle, gain, wout, attended)


def attention_backward(slots, heads, segments, query_ref, grad_ref, key_ref, turned_key_ref, value_ref,
                       cos_ref, sin_ref, projected_out,
                       key_total, value_total, query_total, tri_ref):
    step = pl.num_programs(0) - 1 - pl.program_id(0)
    half = HEAD // 2

    @pl.when(pl.program_id(0) == 0)
    def _():
        key_total[...] = jnp.zeros_like(key_total)
        value_total[...] = jnp.zeros_like(value_total)
        tri_ref[...] = causal_bias(heads)

    def visit(back):
        keys = block_at(step - back)
        columns = [slice(s * LANES, (s + 1) * LANES) for s in range(slots)]
        features = [slice(s * HEAD, (s + 1) * HEAD) for s in range(slots)]
        scores = [matmul(key_ref[keys, columns[s]], query_ref[0, s]) for s in range(slots)]
        grad_weights = [matmul(value_ref[keys, columns[s]], grad_ref[0, s]) for s in range(slots)]
        weights, grad_scores = [], []
        for s in range(slots):
            score = scores[s] + tri_ref[...] if back == 0 else scores[s]
            weight = jnp.exp2(score)
            weights.append(weight.astype(bf16))
            grad_scores.append((weight * grad_weights[s]).astype(bf16))
        for s in range(slots):
            value_total[features[s], keys] += matmul(grad_ref[0, s, :HEAD, :], weights[s], NT)
            key_total[features[s], keys] += matmul(query_ref[0, s, :HEAD, :], grad_scores[s], NT)
            update = matmul(turned_key_ref[features[s], keys], grad_scores[s])
            if back == 0:
                query_total[s] = update
            else:
                query_total[s] += update

    visit(0)
    for back in (1, 2):
        pl.when(reaches(segments, step, back))(functools.partial(visit, back))

    cosine, sine = cos_ref[...], sin_ref[...]
    here = block_at(step)
    for s in range(slots):
        for j in range(heads + 2):
            if j < heads:
                piece = query_total[s, :, j * BLOCK : (j + 1) * BLOCK] * (1.0 / math.sqrt(HEAD))
            elif j == heads:
                piece = key_total[s * HEAD : (s + 1) * HEAD, here] * LN2
            else:
                piece = value_total[s * HEAD : (s + 1) * HEAD, here]
            if j <= heads:
                upper, lower = turn(piece[:half], piece[half:], cosine, -sine)
                piece = jnp.concatenate([upper, lower], axis=0)
            first = (s * (heads + 2) + j) * HEAD
            projected_out[first : first + HEAD, :] = piece.astype(bf16)


def call_attention_backward(
    segments, first, slots, query, grad_heads, key, turned_key, value, cosine, sine
):
    length = key.shape[0]
    count = length // BLOCK
    wide_heads = query.shape[3]
    heads = wide_heads // BLOCK
    block = first // slots

    def heads_spec():
        return pl.BlockSpec((1, slots, LANES, wide_heads), lambda i, *_: (count - 1 - i, block, 0, 0))

    def spec(rows):
        return pl.BlockSpec((rows, BLOCK), lambda i, *_: (0, count - 1 - i))

    once = pl.Buffered(buffer_count=1)
    return pl.pallas_call(
        functools.partial(attention_backward, slots, heads),
        grid_spec=pltpu.PrefetchScalarGridSpec(
            num_scalar_prefetch=1,
            grid=(count,),
            in_specs=[
                heads_spec(), heads_spec(),
                pl.BlockSpec((length, slots * LANES), lambda i, *_: (0, block), pipeline_mode=once),
                pl.BlockSpec((slots * HEAD, length), lambda i, *_: (block, 0), pipeline_mode=once),
                pl.BlockSpec((length, slots * LANES), lambda i, *_: (0, block), pipeline_mode=once),
                spec(HEAD // 2), spec(HEAD // 2),
            ],
            out_specs=spec(slots * (heads + 2) * HEAD),
            scratch_shapes=[
                pltpu.VMEM((slots * HEAD, length), f32),
                pltpu.VMEM((slots * HEAD, length), f32),
                pltpu.VMEM((slots, HEAD, wide_heads), f32),
                pltpu.VMEM((BLOCK, wide_heads), f32),
            ],
        ),
        out_shape=shape_of((slots * (heads + 2) * HEAD, length), bf16),
        compiler_params=pltpu.CompilerParams(vmem_limit_bytes=32 * MIB),
        cost_estimate=cost(slots * 8e9, query, grad_heads),
        name="attention_backward",
    )(segments, query, grad_heads, key, turned_key, value, cosine, sine)


def projection_backward(count, wqkv_ref, *refs):
    projected = jnp.concatenate([ref[...] for ref in refs[:count]], axis=0)
    refs[count][...] = matmul(wqkv_ref[...], projected, TN).astype(bf16)


def call_projection_backward(wqkv, pieces):
    features = wqkv.shape[1]
    length = pieces[0].shape[1]
    width = 512
    return pl.pallas_call(
        functools.partial(projection_backward, len(pieces)),
        grid=(length // width,),
        in_specs=[full_spec(wqkv.shape)] + [token_spec(p.shape[0], width) for p in pieces],
        out_specs=token_spec(features, width),
        out_shape=shape_of((features, length), bf16),
        compiler_params=pltpu.CompilerParams(vmem_limit_bytes=32 * MIB),
        cost_estimate=cost(2 * wqkv.shape[0] * features * length, wqkv, *pieces),
        name="projection_backward",
    )(wqkv, *pieces)


def shard_rows(total, out_ref, order, rows):
    total = total.astype(bf16)
    for place, shard in enumerate(order):
        out_ref[place, :rows, :] = total[shard * rows : (shard + 1) * rows]
        if out_ref.shape[1] > rows:
            out_ref[place, rows:, :] = jnp.zeros((out_ref.shape[1] - rows, total.shape[1]), bf16)


def summed_products(lefts, rights):
    total = matmul(lefts[0][...], rights[0][...], NT)
    for left, right in zip(lefts[1:], rights[1:]):
        total = total + matmul(left[...], right[...], NT)
    return total


def weight_grad(orders, rows, count, sources, *refs):
    lefts, refs = refs[:count], refs[count:]
    outs = refs[count * len(sources) :]
    width = outs[0].shape[2]
    step = pl.program_id(0)
    for number, (start, steps, _) in enumerate(sources):

        def work(rights=refs[number * count : (number + 1) * count]):
            total = summed_products(lefts, rights)
            for place, (order, out_ref) in enumerate(zip(orders, outs)):
                shard_rows(total[:, place * width : (place + 1) * width], out_ref, order, rows)

        if len(sources) == 1:
            work()
        else:
            pl.when((step >= start) & (step < start + steps))(work)


def call_weight_grad(lefts, rights, orders, width):
    features, length = lefts[0].shape
    size = len(orders[0])
    rows = features // size
    padded = -(-rows // 16) * 16
    count = len(lefts)
    sources, in_specs, arrays, total = [], [full_spec((features, length))] * count, [], 0
    for pair, first, blocks in rights:
        sources.append((total, blocks, first))
        arrays += pair

        def index(i, start=total, blocks=blocks, first=first):
            return (jnp.clip(i - start, 0, blocks - 1) + first, 0)

        in_specs += [pl.BlockSpec((width, length), index)] * count
        total += blocks
    share = width // len(orders)
    return pl.pallas_call(
        functools.partial(weight_grad, orders, rows, count, sources),
        grid=(total,),
        in_specs=in_specs,
        out_specs=[pl.BlockSpec((size, padded, share), lambda i: (0, 0, i))] * len(orders),
        out_shape=[shape_of((size, padded, total * share), bf16)] * len(orders),
        compiler_params=pltpu.CompilerParams(vmem_limit_bytes=32 * MIB),
        cost_estimate=cost(2 * count * length * features * total * width, *lefts),
        name="weight_grad",
    )(*lefts, *arrays)


def slot_grad(cuts, rows, count, *refs):
    normed, projected, grads, attended = (refs[i * count : (i + 1) * count] for i in range(4))
    total = jnp.concatenate(
        [summed_products(normed, projected), summed_products(grads, attended)], axis=1
    )
    for (order, first, last), out_ref in zip(cuts, refs[4 * count :]):
        shard_rows(total[:, first:last], out_ref, order, rows)


def call_slot_grad(slot, normed, projected, grads, attended, orders):
    features, length = normed[0].shape
    size = len(orders[0])
    rows = features // size
    padded = -(-rows // 16) * 16
    heads_rows = (GROUP + 2) * HEAD
    out_rows = GROUP * HEAD
    width = (heads_rows + out_rows) // len(orders)
    cuts = [(order, number * width, (number + 1) * width) for number, order in enumerate(orders)]
    in_specs = [full_spec((features, length))] * len(normed)
    for _, block in projected:
        in_specs.append(pl.BlockSpec((heads_rows, length), lambda i, block=block: (block, 0)))
    in_specs += [full_spec((features, length))] * len(grads)
    in_specs += [pl.BlockSpec((out_rows, length), lambda i: (slot, 0))] * len(attended)
    return pl.pallas_call(
        functools.partial(slot_grad, cuts, rows, len(normed)),
        grid=(1,),
        in_specs=in_specs,
        out_specs=[pl.BlockSpec((size, padded, width), lambda i: (0, 0, 0))] * len(orders),
        out_shape=[shape_of((size, padded, width), bf16)] * len(orders),
        compiler_params=pltpu.CompilerParams(vmem_limit_bytes=32 * MIB),
        cost_estimate=cost(2 * len(normed) * length * features * (heads_rows + out_rows), *normed, *grads),
        name="slot_grad",
    )(*normed, *(p for p, _ in projected), *grads, *attended)


def block_grad(grad_ref, hidden_ref, own_ref, other_ref, gain_ref, out_ref, *low_ref):
    grad = grad_ref[...] + norm_back(
        hidden_ref[...].astype(f32), gain_ref[...], joined_sum(own_ref, other_ref)
    )
    out_ref[...] = grad
    if low_ref:
        low_ref[0][...] = grad.astype(bf16)


def call_block_grad(grad, hidden, own, other, gain, types):
    features, length = grad.shape
    return pl.pallas_call(
        block_grad,
        grid=(length // BLOCK,),
        in_specs=[token_spec(features)] * 4 + [full_spec(gain.shape)],
        out_specs=[token_spec(features)] * len(types),
        out_shape=[shape_of((features, length), t) for t in types],
        compiler_params=pltpu.CompilerParams(vmem_limit_bytes=32 * MIB),
        cost_estimate=cost(0, grad, grad, hidden, own, other),
        name="block_grad",
    )(grad, hidden, own, other, gain)


def gather_groups(owner, device, query_ref, key_ref, value_ref, out_ref, wqkv_out, wout_out):
    slot = pl.program_id(0)
    _, held = group_of(slot, owner, device)
    group_cols, head = query_ref.shape[1], key_ref.shape[1]

    def place(first, height, piece):
        rows = pl.ds(pl.multiple_of(first, 16), height)
        return rows, jnp.where(held, piece, jnp.zeros_like(piece))

    base = slot * (group_cols + 2 * head)
    rows, piece = place(base, group_cols, query_ref[0])
    wqkv_out[rows, :] = piece
    rows, piece = place(base + group_cols, head, key_ref[0])
    wqkv_out[rows, :] = piece
    rows, piece = place(base + group_cols + head, head, value_ref[0])
    wqkv_out[rows, :] = piece
    rows, piece = place(slot * group_cols, group_cols, out_ref[0])
    wout_out[rows, :] = piece


def group_of(slot, owner, device):
    found, count = 0, 0
    for group in range(owner.shape[0]):
        mine = owner[group] == device[0]
        found = jnp.where(mine & (count == slot), group, found)
        count = count + jnp.where(mine, 1, 0)
    return found, count > slot


def call_gather_groups(owner, device, w_query, w_key, w_value, w_out, slots):
    features = w_query.shape[2]
    arrays = (w_query, w_key, w_value, w_out)
    joint = slots * (w_query.shape[1] + w_key.shape[1] + w_value.shape[1])
    outs = [(joint, features), (slots * w_out.shape[1], features)]
    return pl.pallas_call(
        gather_groups,
        grid_spec=pltpu.PrefetchScalarGridSpec(
            num_scalar_prefetch=2,
            grid=(slots,),
            in_specs=[
                pl.BlockSpec(
                    (1,) + a.shape[1:], lambda s, owner, device: (group_of(s, owner, device)[0], 0, 0)
                )
                for a in arrays
            ],
            out_specs=[out_full_spec(o) for o in outs],
        ),
        out_shape=[shape_of(o, bf16) for o in outs],
        name="gather_groups",
    )(owner, device, *arrays)


def rotary_tables(length):
    position = np.arange(length, dtype=np.float64)[None, :]
    column = np.arange(HEAD // 2, dtype=np.float64)[:, None]
    angles = position * np.exp(column * (-2.0 * math.log(10000.0) / HEAD))
    return jnp.asarray(np.cos(angles), f32), jnp.asarray(np.sin(angles), f32)


def exchange(own):
    return lax.ppermute(own, "mp", [(0, 1), (1, 0)])


def stage_plans(bit_count):
    bits = list(range(bit_count))
    return [
        [[bit] for bit in bits],
        [[bit] for bit in bits[1:2] + bits[:1] + bits[2:]],
        [[bit] for bit in bits[2:3] + bits[:2] + bits[3:]],
        [[bit] for bit in bits[2:0:-1] + bits[:1] + bits[3:]],
    ]


def shard_order(plan):
    bits = [bit for stage in plan for bit in stage]
    order = []
    for place in range(1 << len(bits)):
        shard = 0
        for rank, bit in enumerate(bits):
            if place >> (len(bits) - 1 - rank) & 1:
                shard |= 1 << bit
        order.append(shard)
    return order


def after(value, *others):
    return lax.optimization_barrier((value, others))[0]


class Stream:
    def __init__(self, payload, plan):
        self.current, self.stages, self.received = payload, list(plan), []

    def send(self):
        stage = self.stages.pop(0)
        size = lax.axis_size("dp")
        index = lax.axis_index("dp")
        mine = 0
        for bit in stage:
            mine = mine * 2 + ((index >> bit) & 1)
        ways = 1 << len(stage)
        pieces = self.current.shape[0] // ways
        self.kept = lax.dynamic_slice_in_dim(self.current, mine * pieces, pieces, 0)
        self.received, sent = [], []
        for offset in range(1, ways):
            mask = 0
            for rank, bit in enumerate(stage):
                if offset >> (len(stage) - 1 - rank) & 1:
                    mask |= 1 << bit
            piece = lax.dynamic_slice_in_dim(self.current, (mine ^ offset) * pieces, pieces, 0)
            sent.append(piece)
            self.received.append(lax.ppermute(piece, "dp", [(i, i ^ mask) for i in range(size)]))
        return tuple(sent)

    def add(self, *others):
        received = after(tuple(self.received), *others) if others else self.received
        total = self.kept.astype(f32)
        for piece in received:
            total = total + piece.astype(f32)
        self.current = total.astype(bf16) if self.stages else total
        self.received = []

    def next_stage(self, *others):
        if self.received:
            self.add(*others)
        return self.send() if self.stages else (self.current,)


def merged(streams, *others):
    for stream in streams:
        stream.add(*others)
    return Stream(jnp.concatenate([stream.current for stream in streams], axis=2), streams[0].stages)


def per_device(
    tokens_in,
    segment_ids,
    kv_owner,
    w_query,
    w_key,
    w_value,
    w_out,
    attn_gain,
    w_gate,
    w_up,
    w_down,
    ffn_gain,
    cotangent,
):
    features = tokens_in.shape[2]
    length = tokens_in.shape[1]
    group_cols = w_query.shape[2]
    heads = group_cols // HEAD
    slots = (kv_owner.shape[0] + lax.axis_size("mp") - 1) // lax.axis_size("mp")
    size = lax.axis_size("dp")
    rows = features // size

    device = lax.axis_index("mp").astype(jnp.int32)[None]
    wqkv, wout = call_gather_groups(
        kv_owner, device, *(jnp.swapaxes(w, 1, 2) for w in (w_query, w_key, w_value)), w_out, slots
    )
    w_down = w_down.T
    segments = segment_ids[0]
    cosine, sine = rotary_tables(length)
    gain_one, gain_two = (
        jnp.broadcast_to(gain.astype(f32)[:, None], (features, LANES)) for gain in (attn_gain, ffn_gain)
    )

    parts = (tokens_in[0].T,)
    saved = []
    for _ in range(REPEAT):
        outs = list(call_attention_forward(segments, parts, gain_one, wqkv, wout, cosine, sine, slots, heads))
        hidden = outs.pop(0) if len(parts) == 3 else parts[0]
        normed, query, key, turned_key, value, attended, partial = outs
        middle, normed_two, gate, lift, inner, partial_two = call_ffn_forward(
            hidden, partial, exchange(partial), gain_two, w_gate, w_up, w_down
        )
        parts = (middle, partial_two, exchange(partial_two))
        saved.append((hidden, normed, query, key, turned_key, value, attended, middle, normed_two, gate, lift, inner))

    plans = stage_plans(size.bit_length() - 1)
    orders = [shard_order(plan) for plan in plans]
    joint = None
    grad = ffn_grad = cotangent[0].T
    for r in reversed(range(REPEAT)):
        hidden, normed, query, key, turned_key, value, attended, middle, normed_two, gate, lift, inner = saved[r]
        last = r == 0
        if joint is not None:
            grad, ffn_grad = call_block_grad(grad, *joint, (f32, bf16))
        if last:
            units = inner.shape[0]
            pairs = ((above["inner"], inner), 0, 1)
            payloads = call_weight_grad((above["ffn_grad"], ffn_grad), [pairs], orders[:2], units)
            downs = [Stream(payload, plan) for payload, plan in zip(payloads, plans)]
            ffn_grad = after(ffn_grad, [stream.send() for stream in downs])
        grad_gate, grad_lift, partial = call_ffn_backward(ffn_grad, gate, lift, w_gate, w_up, w_down)
        other = exchange(partial)
        if not last:
            parts, other = lax.optimization_barrier((parts, other))
        if last:
            lefts = (above["normed_two"], normed_two)
            sent = [stream.next_stage() for stream in downs]
            blocks = units // 256
            some = blocks // 2 + 1
            gates = (above["grad_gate"], after(grad_gate, sent))
            (payload,) = call_weight_grad(lefts, [(gates, 0, some)], orders[:1], 256)
            track_a = Stream(payload, plans[0])
            lifts = (above["grad_lift"], after(grad_lift, track_a.send()))
            (payload,) = call_weight_grad(
                lefts, [(gates, some, blocks - some), (lifts, 0, blocks - some)], orders[1:2], 256
            )
            track_b = Stream(payload, plans[1])
            sent = track_b.send()
            down = merged(downs)
            lifts = (lifts[0], after(lifts[1], sent, down.send()))
            (payload,) = call_weight_grad(lefts, [(lifts, blocks - some, some)], orders[2:3], 256)
            track_c = Stream(payload, plans[2])
            partial = after(partial, track_c.send())
        grad, attn_grad, grad_heads = call_attention_entry(
            grad, partial, other, middle, gain_two, wout, attended, slots, heads
        )
        core = functools.partial(
            call_attention_backward, segments, query=query, key=key, turned_key=turned_key, value=value,
            cosine=cosine, sine=sine,
        )
        if not last:
            pieces = [core(0, slots, grad_heads=grad_heads)]
            above = dict(
                ffn_grad=ffn_grad, inner=inner, normed_two=normed_two, grad_lift=grad_lift,
                grad_gate=grad_gate, attn_grad=attn_grad, projected=pieces[0], normed=normed,
                attended=attended,
            )
        else:
            grad_heads = after(grad_heads, down.next_stage(attn_grad))

            def slot_streams(slot, piece, block, numbers):
                payloads = call_slot_grad(
                    slot, (above["normed"], normed), ((above["projected"], slot), (piece, block)),
                    (above["attn_grad"], attn_grad), (above["attended"], attended),
                    [orders[n] for n in numbers],
                )
                return [Stream(payload, plans[n]) for payload, n in zip(payloads, numbers)]

            early = slots - 1
            pieces = [core(0, early, grad_heads=grad_heads)]
            for stream in (down, track_a, track_b, track_c):
                stream.add(pieces[0])
            sent = track_a.send(), track_b.send(), track_c.send(), down.current
            held = after(pieces[0], sent)
            tracks = [slot_streams(slot, held, slot, (3 - 2 * (slot % 2),))[0] for slot in range(early)]
            sent = [stream.send() for stream in tracks]
            pieces.append(core(early, 1, grad_heads=after(grad_heads, sent)))
            both = merged((track_a, track_b), pieces[1])
            track_c.add(pieces[1])
            held = after(pieces[1], both.send(), track_c.current)
            (final,) = slot_streams(early, held, 0, (0,))
            sent = [final.send()] + [stream.next_stage(final.current) for stream in tracks]
            pieces[1] = after(held, sent)
        partial_two = call_projection_backward(wqkv, pieces)
        other_two = exchange(partial_two)
        if last:
            sent = [stream.next_stage(other_two) for stream in (final, both)]
            grad = after(grad, sent, track_c.send())
        joint = (hidden, partial_two, other_two, gain_one)
    (grad_in,) = call_block_grad(grad, *joint, (f32,))
    sent = [stream.next_stage(grad_in) for stream in (*tracks, track_c)]
    parts = after(parts, grad_in, sent)
    tokens_out = (parts[0] + (parts[1].astype(f32) + parts[2].astype(f32))).astype(bf16)
    pending = [final, both, track_c, *tracks, down]
    first_round = True
    while any(stream.stages for stream in pending):
        for stream in pending:
            if stream.stages:
                if first_round:
                    stream.next_stage(tokens_out)
                else:
                    stream.next_stage()
        first_round = False
    for stream in pending:
        if stream.received:
            stream.add()
    down_total = down.current[0]
    both_total = both.current[0]
    first = some * 256
    second = (blocks - some) * 256
    gate_total = both_total[:, : first + second]
    up_total = jnp.concatenate([both_total[:, first + second :], track_c.current[0]], axis=1)
    slot_totals = [stream.current[0, :rows] for stream in (*tracks, final)]

    start = lax.axis_index("dp") * rows

    def my_rows(weights):
        return lax.dynamic_slice_in_dim(weights, start, rows, 0).astype(f32)

    gate_total, up_total, down_total = (total[:rows] for total in (gate_total, up_total, down_total))
    wqkv = after(wqkv, tokens_out)
    chosen = (jnp.arange(rows)[:, None] + start == jnp.arange(features)[None, :]).astype(bf16)
    wqkv_rows = matmul(chosen, wqkv, NT)
    ends = [group_cols, group_cols + HEAD, group_cols + 2 * HEAD]
    gains = jnp.stack([
        sum(
            jnp.sum(total[:, : ends[2]] * wqkv_rows[:, s * ends[2] : (s + 1) * ends[2]], axis=1)
            for s, total in enumerate(slot_totals)
        ),
        jnp.sum(gate_total * my_rows(w_gate) + up_total * my_rows(w_up), axis=1),
    ])
    gains = gains + exchange(gains)
    gains = gains / lax.dynamic_slice_in_dim(jnp.stack([attn_gain, ffn_gain]), start, rows, 1).astype(f32)

    return (
        tokens_out.T[None],
        grad_in.T[None],
        jnp.stack([total[:, : ends[0]] for total in slot_totals]),
        jnp.stack([total[:, ends[0] : ends[1]] for total in slot_totals]),
        jnp.stack([total[:, ends[1] : ends[2]] for total in slot_totals]),
        jnp.swapaxes(jnp.stack([total[:, ends[2] :] for total in slot_totals]), 1, 2),
        gate_total,
        up_total,
        down_total.T,
        gains[0],
        gains[1],
    )


def solution(mesh):
    in_specs = (
        P("dp", None, None),
        P("dp", None),
        P(),
        P(),
        P(),
        P(),
        P(),
        P(),
        P(None, "mp"),
        P(None, "mp"),
        P("mp", None),
        P(),
        P("dp", None, None),
    )
    out_specs = (
        P("dp", None, None),
        P("dp", None, None),
        P("mp", "dp", None),
        P("mp", "dp", None),
        P("mp", "dp", None),
        P("mp", None, "dp"),
        P("dp", "mp"),
        P("dp", "mp"),
        P("mp", "dp"),
        P("dp"),
        P("dp"),
    )
    return jax.shard_map(
        per_device, mesh=mesh, in_specs=in_specs, out_specs=out_specs, check_vma=False
    )
```

```python
import functools
import math

import jax
import jax.numpy as jnp
import numpy as np
from jax import lax
from jax.experimental import pallas as pl
from jax.experimental.pallas import tpu as pltpu
from jax.sharding import PartitionSpec as P

REPEAT = 2
BLOCK = 256
FFN_BLOCK = 512
LANES = 128
HEAD = 64
GROUP = 3
VROWS = 80
epsilon = 1e-05
masked_value = -1e30
LOG2E = math.log2(math.e)
LN2 = math.log(2.0)
f32 = jnp.float32
bf16 = jnp.bfloat16
NN = (((1,), (0,)), ((), ()))
NT = (((1,), (1,)), ((), ()))
TN = (((0,), (0,)), ((), ()))
MIB = 1024 * 1024


def matmul(a, b, dims=NN):
    return lax.dot_general(a, b, dims, preferred_element_type=f32)


def wide(column, width):
    return jnp.concatenate([column] * (width // LANES), axis=1)


def inverse_rms(values):
    return lax.rsqrt(jnp.mean(values * values, axis=0, keepdims=True) + epsilon)


def normalise(values, gain, inverse_out):
    inverse = inverse_rms(values)
    inverse_out[...] = inverse
    return (values * inverse * wide(gain, values.shape[1])).astype(bf16)


def norm_back(normed, inverse, gain, grad_normed):
    normed = normed.astype(f32)
    inner_mean = jnp.mean(grad_normed * normed, axis=0, keepdims=True)
    width = normed.shape[1]
    return inverse * (grad_normed * wide(gain, width) - normed * wide(1.0 / gain, width) * inner_mean)


def joined_sum(own_ref, other_ref):
    return own_ref[...].astype(f32) + other_ref[...].astype(f32)


def three_parts(value):
    high = value.astype(bf16).astype(f32)
    rest = value - high
    middle = rest.astype(bf16).astype(f32)
    return high, middle, rest - middle


def part_rows(value, first):
    row = lax.broadcasted_iota(jnp.int32, (8, value.shape[1]), 0)
    out = jnp.zeros((8, value.shape[1]), f32)
    for number, part in enumerate(three_parts(value)):
        out = jnp.where(row == first + number, part, out)
    return out


def causal_bias(heads):
    key = lax.broadcasted_iota(jnp.int32, (BLOCK, heads * BLOCK), 0)
    query = lax.broadcasted_iota(jnp.int32, (BLOCK, heads * BLOCK), 1) % BLOCK
    return jnp.where(key <= query, 0.0, masked_value)


def reaches(segments, step, back):
    last = jnp.maximum((step - back + 1) * BLOCK - 1, 0)
    return (step >= back) & (segments[last] == segments[step * BLOCK])


def block_at(index):
    return pl.ds(pl.multiple_of(index * BLOCK, BLOCK), BLOCK)


def turn(upper, lower, cosine, sine):
    return upper * cosine - lower * sine, lower * cosine + upper * sine


def attention_forward(joined, slots, heads, segments, *refs):
    refs = list(refs)
    hidden = refs.pop(0)[...].astype(f32)
    if joined:
        hidden = hidden + joined_sum(refs.pop(0), refs.pop(0))
    gain_ref, wqkv_ref, wout_ref, cos_ref, sin_ref, segment_ref = refs[:6]
    refs = refs[6:]
    if joined:
        refs.pop(0)[...] = hidden
    (normed_out, inverse_out, query_out, key_out, turned_key_out, value_out, attended_out, partial_out,
     turned_value, tri_ref) = refs
    step = pl.program_id(0)
    here = block_at(step)

    @pl.when(step == 0)
    def _():
        tri_ref[...] = causal_bias(heads)

    normed = normalise(hidden, gain_ref[...], inverse_out)
    normed_out[...] = normed
    projected = matmul(wqkv_ref[...], normed)
    cosine, sine = cos_ref[...], sin_ref[...]
    half = HEAD // 2

    same = lax.broadcasted_iota(jnp.int32, (8, BLOCK), 0) == segment_ref[...]
    query_rows = jnp.where(same, 1.0, 0.0)
    key_rows = jnp.where(same, 0.0, masked_value)
    row = lax.broadcasted_iota(jnp.int32, (8, BLOCK), 0)
    minus_rows = jnp.where(row < 3, -1.0, 0.0)
    scale = LOG2E / math.sqrt(HEAD)
    query_fill = jnp.concatenate(
        [query_rows, jnp.zeros((LANES - HEAD - 8, BLOCK), f32)], axis=0
    ).astype(bf16)

    for s in range(slots):
        for j in range(heads + 2):
            first = (s * (heads + 2) + j) * HEAD
            piece = projected[first : first + HEAD]
            if j > heads:
                value = jnp.concatenate([piece, jnp.ones((LANES - HEAD, BLOCK), f32)], axis=0)
                value_out[here, s * LANES : (s + 1) * LANES] = value.T.astype(bf16)
                turned_value[s * VROWS : (s + 1) * VROWS, here] = value[:VROWS].astype(bf16)
                continue
            upper, lower = turn(piece[:half], piece[half:], cosine, sine)
            if j < heads:
                lanes = slice(j * BLOCK, (j + 1) * BLOCK)
                query_out[0, s, :HEAD, lanes] = jnp.concatenate(
                    [upper * scale, lower * scale], axis=0
                ).astype(bf16)
                query_out[0, s, HEAD:, lanes] = query_fill
            else:
                turned_key_out[s * HEAD : (s + 1) * HEAD, :] = jnp.concatenate(
                    [upper, lower], axis=0
                ).astype(bf16)
                whole = jnp.concatenate(
                    [upper, lower, key_rows, minus_rows, jnp.zeros((LANES - HEAD - 16, BLOCK), f32)],
                    axis=0,
                )
                key_out[here, s * LANES : (s + 1) * LANES] = whole.T.astype(bf16)

    query_rows = jnp.concatenate([query_rows] * heads, axis=1)

    def attend(blocks):
        width = blocks * BLOCK
        keys = pl.ds(pl.multiple_of((step + 1 - blocks) * BLOCK, BLOCK), width)
        scores = [
            matmul(key_out[keys, s * LANES : (s + 1) * LANES], query_out[0, s]) for s in range(slots)
        ]
        tops, weights = [], []
        for score in scores:
            last = score[width - BLOCK :] + tri_ref[...]
            if blocks > 1:
                score = jnp.concatenate([score[: width - BLOCK], last], axis=0)
            else:
                score = last
            tops.append(jnp.max(score, axis=0, keepdims=True))
            weights.append(jnp.exp2(score - tops[-1]).astype(bf16))
        summed = [
            matmul(turned_value[s * VROWS : (s + 1) * VROWS, keys], weights[s]) for s in range(slots)
        ]
        for s in range(slots):
            weight_sum = summed[s][HEAD : HEAD + 1]
            out = (summed[s][:HEAD] * (1.0 / weight_sum)).astype(bf16)
            for j in range(heads):
                first = (s * heads + j) * HEAD
                attended_out[first : first + HEAD, :] = out[:, j * BLOCK : (j + 1) * BLOCK]
            query_out[0, s, HEAD : HEAD + 16, :] = jnp.concatenate(
                [query_rows, part_rows(tops[s] + jnp.log2(weight_sum), 0)], axis=0
            ).astype(bf16)

    one = reaches(segments, step, 1)
    two = reaches(segments, step, 2)
    pl.when(jnp.logical_not(one))(functools.partial(attend, 1))
    pl.when(one & jnp.logical_not(two))(functools.partial(attend, 2))
    pl.when(two)(functools.partial(attend, 3))
    partial_out[...] = matmul(wout_ref[...], attended_out[...], TN).astype(bf16)


def chunks(width):
    return [slice(start, start + 256) for start in range(0, width, 256)]


def cost(flops, *arrays):
    size = sum(math.prod(a.shape) * a.dtype.itemsize for a in arrays)
    return pl.CostEstimate(flops=int(flops), bytes_accessed=size, transcendentals=0)


def token_spec(rows, width=BLOCK):
    return pl.BlockSpec((rows, width), lambda i, *_: (0, i))


def full_spec(shape):
    return pl.BlockSpec(
        shape, lambda *_: (0,) * len(shape), pipeline_mode=pl.Buffered(buffer_count=1)
    )


def out_full_spec(shape):
    return pl.BlockSpec(shape, lambda *_: (0,) * len(shape))


shape_of = pltpu.HBM
anywhere = jax.ShapeDtypeStruct


def in_hbm(*arrays):
    return tuple(pltpu.with_memory_space_constraint(array, pltpu.HBM) for array in arrays)


def call_attention_forward(segments, parts, gain, wqkv, wout, cosine, sine, slots, heads):
    features, length = parts[0].shape
    joined = len(parts) == 3
    total = slots * heads
    big = shape_of((features, length), bf16)
    outs = [
        (big, token_spec(features)),
        (shape_of((1, length), f32), token_spec(1)),
        (
            shape_of((length // BLOCK, slots, LANES, heads * BLOCK), bf16),
            pl.BlockSpec((1, slots, LANES, heads * BLOCK), lambda i, *_: (i, 0, 0, 0)),
        ),
        (shape_of((length, slots * LANES), bf16), out_full_spec((length, slots * LANES))),
        (shape_of((slots * HEAD, length), bf16), token_spec(slots * HEAD)),
        (shape_of((length, slots * LANES), bf16), out_full_spec((length, slots * LANES))),
        (shape_of((total * HEAD, length), bf16), token_spec(total * HEAD)),
        (anywhere((features, length), bf16), token_spec(features)),
    ]
    if joined:
        outs.insert(0, (shape_of((features, length), f32), token_spec(features)))
    return pl.pallas_call(
        functools.partial(attention_forward, joined, slots, heads),
        grid_spec=pltpu.PrefetchScalarGridSpec(
            num_scalar_prefetch=1,
            grid=(length // BLOCK,),
            in_specs=[token_spec(features)] * len(parts)
            + [full_spec(a.shape) for a in (gain, wqkv, wout)]
            + [token_spec(HEAD // 2)] * 2
            + [token_spec(1)],
            out_specs=[spec for _, spec in outs],
            scratch_shapes=[
                pltpu.VMEM((slots * VROWS, length), bf16),
                pltpu.VMEM((BLOCK, heads * BLOCK), f32),
            ],
        ),
        out_shape=[shape for shape, _ in outs],
        compiler_params=pltpu.CompilerParams(vmem_limit_bytes=32 * MIB),
        cost_estimate=cost(2 * length * features * (wqkv.shape[0] + wout.shape[0]) + 12e9, *parts),
        name="attention_forward",
    )(segments, *in_hbm(parts[0]), *parts[1:], gain, wqkv, wout, cosine, sine, segments[None, :])


def ffn_forward(hidden_ref, own_ref, other_ref, gain_ref, gate_ref, up_ref, down_ref,
                middle_out, normed_out, inverse_out, gate_out, lift_out, inner_out, partial_out):
    middle = hidden_ref[...].astype(f32) + joined_sum(own_ref, other_ref)
    middle_out[...] = middle
    normed = normalise(middle, gain_ref[...], inverse_out)
    normed_out[...] = normed
    for chunk in chunks(gate_ref.shape[1]):
        gate = matmul(gate_ref[:, chunk], normed, TN)
        lift = matmul(up_ref[:, chunk], normed, TN)
        gate_out[chunk, :] = gate.astype(bf16)
        lift_out[chunk, :] = lift.astype(bf16)
        inner_out[chunk, :] = (gate * jax.nn.sigmoid(gate) * lift).astype(bf16)
    partial_out[...] = matmul(down_ref[...], inner_out[...]).astype(bf16)


def call_ffn_forward(hidden, own, other, gain, w_gate, w_up, w_down):
    features, length = hidden.shape
    units = w_gate.shape[1]
    spec = functools.partial(token_spec, width=FFN_BLOCK)
    return pl.pallas_call(
        ffn_forward,
        grid=(length // FFN_BLOCK,),
        in_specs=[spec(features)] * 3 + [full_spec(a.shape) for a in (gain, w_gate, w_up, w_down)],
        out_specs=[spec(features)] * 2 + [spec(1)] + [spec(units)] * 3 + [spec(features)],
        out_shape=[
            shape_of((features, length), f32), shape_of((features, length), bf16),
            shape_of((1, length), f32), *[shape_of((units, length), bf16)] * 3,
            anywhere((features, length), bf16),
        ],
        compiler_params=pltpu.CompilerParams(vmem_limit_bytes=40 * MIB),
        cost_estimate=cost(6 * length * features * units, hidden),
        name="ffn_forward",
    )(*in_hbm(hidden), own, other, gain, w_gate, w_up, w_down)


def ffn_backward(joined, grad_ref, *refs):
    grad = grad_ref[...]
    if joined:
        normed_ref, inverse_ref, own_ref, other_ref, gain_ref = refs[:5]
        refs = refs[5:]
        back = norm_back(normed_ref[...], inverse_ref[...], gain_ref[...], joined_sum(own_ref, other_ref))
        grad = (grad.astype(f32) + back).astype(bf16)
    gate_in, lift_in, gate_ref, up_ref, down_ref = refs[:5]
    refs = refs[5:]
    if joined:
        refs[0][...] = grad
        refs = refs[1:]
    grad_gate_out, grad_lift_out, partial_out = refs
    for chunk in chunks(gate_ref.shape[1]):
        grad_inner = matmul(down_ref[:, chunk], grad, TN)
        gate = gate_in[chunk, :].astype(f32)
        lift = lift_in[chunk, :].astype(f32)
        sigmoid = jax.nn.sigmoid(gate)
        grad_gate = grad_inner * lift * sigmoid * (1.0 + gate * (1.0 - sigmoid))
        grad_gate_out[chunk, :] = grad_gate.astype(bf16)
        grad_lift_out[chunk, :] = (grad_inner * gate * sigmoid).astype(bf16)
    partial = matmul(gate_ref[...], grad_gate_out[...]) + matmul(up_ref[...], grad_lift_out[...])
    partial_out[...] = partial.astype(bf16)


def call_ffn_backward(grad, joint, gate, lift, w_gate, w_up, w_down):
    features, length = grad.shape
    units = w_gate.shape[1]
    spec = functools.partial(token_spec, width=FFN_BLOCK)
    joint_specs, extra = [], []
    if joint:
        normed, inverse, own, other, gain = joint
        joint = (*in_hbm(normed), inverse, own, other, gain)
        joint_specs = [spec(features), spec(1), spec(features), spec(features), full_spec(gain.shape)]
        extra = [(shape_of((features, length), bf16), spec(features))]
    outs = extra + [(shape_of((units, length), bf16), spec(units))] * 2
    outs.append((anywhere((features, length), bf16), spec(features)))
    return pl.pallas_call(
        functools.partial(ffn_backward, bool(joint)),
        grid=(length // FFN_BLOCK,),
        in_specs=[spec(features)] + joint_specs + [spec(units)] * 2
        + [full_spec(a.shape) for a in (w_gate, w_up, w_down)],
        out_specs=[spec for _, spec in outs],
        out_shape=[shape for shape, _ in outs],
        compiler_params=pltpu.CompilerParams(vmem_limit_bytes=40 * MIB),
        cost_estimate=cost(6 * length * features * units, grad),
        name="ffn_backward",
    )(*in_hbm(grad), *joint, *in_hbm(gate, lift), w_gate, w_up, w_down)


def attention_backward(slots, heads, segments, grad_ref, own_ref, other_ref, normed_ref, inverse_ref,
                       gain_ref, wout_ref, wqkv_ref, attended_ref, query_ref, key_ref, turned_key_ref,
                       value_ref, cos_ref, sin_ref,
                       attn_grad_out, projected_out, partial_out,
                       key_total, value_total, query_total, grad_heads, tri_ref):
    step = pl.num_programs(0) - 1 - pl.program_id(0)
    half = HEAD // 2

    @pl.when(pl.program_id(0) == 0)
    def _():
        key_total[...] = jnp.zeros_like(key_total)
        value_total[...] = jnp.zeros_like(value_total)
        tri_ref[...] = causal_bias(heads)

    back = norm_back(normed_ref[...], inverse_ref[...], gain_ref[...], joined_sum(own_ref, other_ref))
    attn_grad = (grad_ref[...].astype(f32) + back).astype(bf16)
    attn_grad_out[...] = attn_grad
    grad_attended = matmul(wout_ref[...], attn_grad).astype(bf16)
    zeros = jnp.zeros((LANES - HEAD - 8, BLOCK), f32)
    for s in range(slots):
        for j in range(heads):
            first = (s * heads + j) * HEAD
            mine = grad_attended[first : first + HEAD]
            out = attended_ref[first : first + HEAD, :]
            delta = jnp.sum(mine.astype(f32) * out.astype(f32), axis=0, keepdims=True)
            lanes = slice(j * BLOCK, (j + 1) * BLOCK)
            grad_heads[s, :HEAD, lanes] = mine
            grad_heads[s, HEAD:, lanes] = jnp.concatenate(
                [part_rows(-delta, 0), zeros], axis=0
            ).astype(bf16)

    def visit(back):
        keys = block_at(step - back)
        columns = [slice(s * LANES, (s + 1) * LANES) for s in range(slots)]
        features = [slice(s * HEAD, (s + 1) * HEAD) for s in range(slots)]
        scores = [matmul(key_ref[keys, columns[s]], query_ref[0, s]) for s in range(slots)]
        grad_weights = [matmul(value_ref[keys, columns[s]], grad_heads[s]) for s in range(slots)]
        weights, grad_scores = [], []
        for s in range(slots):
            score = scores[s] + tri_ref[...] if back == 0 else scores[s]
            weight = jnp.exp2(score)
            weights.append(weight.astype(bf16))
            grad_scores.append((weight * grad_weights[s]).astype(bf16))
        for s in range(slots):
            value_total[features[s], keys] += matmul(grad_heads[s, :HEAD, :], weights[s], NT)
            key_total[features[s], keys] += matmul(query_ref[0, s, :HEAD, :], grad_scores[s], NT)
            update = matmul(turned_key_ref[features[s], keys], grad_scores[s])
            if back == 0:
                query_total[s] = update
            else:
                query_total[s] += update

    visit(0)
    for back in (1, 2):
        pl.when(reaches(segments, step, back))(functools.partial(visit, back))

    cosine, sine = cos_ref[...], sin_ref[...]
    here = block_at(step)
    for s in range(slots):
        for j in range(heads + 2):
            if j < heads:
                piece = query_total[s, :, j * BLOCK : (j + 1) * BLOCK] * (1.0 / math.sqrt(HEAD))
            elif j == heads:
                piece = key_total[s * HEAD : (s + 1) * HEAD, here] * LN2
            else:
                piece = value_total[s * HEAD : (s + 1) * HEAD, here]
            if j <= heads:
                upper, lower = turn(piece[:half], piece[half:], cosine, -sine)
                piece = jnp.concatenate([upper, lower], axis=0)
            first = (s * (heads + 2) + j) * HEAD
            projected_out[first : first + HEAD, :] = piece.astype(bf16)
    partial_out[...] = matmul(wqkv_ref[...], projected_out[...], TN).astype(bf16)


def call_attention_backward(segments, grad, own, other, normed, inverse, gain, wout, wqkv, attended, query,
                            key, turned_key, value, cosine, sine):
    features, length = grad.shape
    count = length // BLOCK
    slots, wide_heads = query.shape[1], query.shape[3]
    heads = wide_heads // BLOCK

    def spec(rows):
        return pl.BlockSpec((rows, BLOCK), lambda i, *_: (0, count - 1 - i))

    return pl.pallas_call(
        functools.partial(attention_backward, slots, heads),
        grid_spec=pltpu.PrefetchScalarGridSpec(
            num_scalar_prefetch=1,
            grid=(count,),
            in_specs=[spec(features)] * 4 + [spec(1)]
            + [full_spec(a.shape) for a in (gain, wout, wqkv)]
            + [spec(attended.shape[0])]
            + [pl.BlockSpec((1, slots, LANES, wide_heads), lambda i, *_: (count - 1 - i, 0, 0, 0))]
            + [full_spec(a.shape) for a in (key, turned_key, value)]
            + [spec(HEAD // 2)] * 2,
            out_specs=[spec(features), spec(wqkv.shape[0]), spec(features)],
            scratch_shapes=[
                pltpu.VMEM((slots * HEAD, length), f32),
                pltpu.VMEM((slots * HEAD, length), f32),
                pltpu.VMEM((slots, HEAD, wide_heads), f32),
                pltpu.VMEM((slots, LANES, wide_heads), bf16),
                pltpu.VMEM((BLOCK, wide_heads), f32),
            ],
        ),
        out_shape=[
            shape_of((features, length), bf16), shape_of((wqkv.shape[0], length), bf16),
            anywhere((features, length), bf16),
        ],
        compiler_params=pltpu.CompilerParams(vmem_limit_bytes=30 * MIB),
        cost_estimate=cost(2 * length * features * (wqkv.shape[0] + wout.shape[0]) + slots * 8e9, grad),
        name="attention_backward",
    )(segments, *in_hbm(grad), own, other, *in_hbm(normed), inverse, gain, wout, wqkv,
      *in_hbm(attended, query), key, turned_key, value, cosine, sine)


def shard_rows(total, out_ref, order, rows):
    total = total.astype(bf16)
    for place, shard in enumerate(order):
        out_ref[place, :rows, :] = total[shard * rows : (shard + 1) * rows]
        if out_ref.shape[1] > rows:
            out_ref[place, rows:, :] = jnp.zeros((out_ref.shape[1] - rows, total.shape[1]), bf16)


def half_of(ref, number):
    width = ref.shape[1] // 2
    return ref.at[:, pl.ds(number * width, width)]


def ffn_weight_grad(orders, rows, blocks, normed_one, normed_two, grad_one, grad_two, *refs):
    rights, outs = refs[:6], refs[6:9]
    normed, grads, arrived = refs[9:]
    step = pl.program_id(0)
    copies = [
        pltpu.make_async_copy(source, half_of(target, number), arrived.at[place])
        for place, (source, target, number) in enumerate((
            (normed_one, normed, 0), (normed_two, normed, 1), (grad_one, grads, 0), (grad_two, grads, 1),
        ))
    ]

    @pl.when(step == 0)
    def _():
        for copy in copies:
            copy.start()
        copies[0].wait()
        copies[1].wait()

    @pl.when(step == 2 * blocks)
    def _():
        copies[2].wait()
        copies[3].wait()

    for number, (left, order, out_ref) in enumerate(zip((normed, normed, grads), orders, outs)):

        def work(left=left, order=order, out_ref=out_ref, pair=rights[2 * number : 2 * number + 2]):
            right = jnp.concatenate([pair[0][...], pair[1][...]], axis=1)
            total = matmul(left[...], right, NT)
            shard_rows(total, out_ref, order, rows)

        pl.when((step >= number * blocks) & (step < (number + 1) * blocks))(work)


def call_ffn_weight_grad(normed, grads, rights, orders):
    features, length = normed[0].shape
    units = rights[0][0].shape[0]
    size = len(orders[0])
    rows = features // size
    padded = -(-rows // 16) * 16
    width = 256
    blocks = units // width
    in_specs, out_specs = [pl.BlockSpec(memory_space=pl.ANY)] * 4, []
    for number in range(3):

        def block_of(i, first=number * blocks):
            return jnp.clip(i - first, 0, blocks - 1)

        in_specs += [pl.BlockSpec((width, length), lambda i, f=block_of: (f(i), 0))] * 2
        out_specs.append(pl.BlockSpec((size, padded, width), lambda i, f=block_of: (0, 0, f(i))))
    return pl.pallas_call(
        functools.partial(ffn_weight_grad, orders, rows, blocks),
        grid=(3 * blocks,),
        in_specs=in_specs,
        out_specs=out_specs,
        out_shape=[shape_of((size, padded, units), bf16)] * 3,
        scratch_shapes=[
            pltpu.VMEM((features, 2 * length), bf16),
            pltpu.VMEM((features, 2 * length), bf16),
            pltpu.SemaphoreType.DMA((4,)),
        ],
        compiler_params=pltpu.CompilerParams(vmem_limit_bytes=32 * MIB),
        cost_estimate=cost(12 * length * features * units, *normed, *grads),
        name="ffn_weight_grad",
    )(*in_hbm(*normed, *grads), *in_hbm(*(array for pair in rights for array in pair)))


def attention_weight_grad(orders, rows, *refs):
    sources, outs, targets, arrived = refs[:8], refs[8:11], refs[11:15], refs[15]
    copies = []
    for number, source in enumerate(sources):
        target = half_of(targets[number % 4], number // 4)
        copies.append(pltpu.make_async_copy(source, target, arrived.at[number]))
    for number in (0, 1, 4, 5, 2, 3, 6, 7):
        copies[number].start()
    for number in (0, 1, 4, 5):
        copies[number].wait()
    projections = matmul(targets[0][...], targets[1][...], NT).astype(bf16)
    for number in (2, 3, 6, 7):
        copies[number].wait()
    outward = matmul(targets[2][...], targets[3][...], NT).astype(bf16)
    total = jnp.concatenate([projections, outward], axis=1)
    width = total.shape[1] // len(orders)
    for number, (order, out_ref) in enumerate(zip(orders, outs)):
        shard_rows(total[:, number * width : (number + 1) * width], out_ref, order, rows)


def call_attention_weight_grad(above, below, orders):
    features, length = above[0].shape
    size = len(orders[0])
    rows = features // size
    padded = -(-rows // 16) * 16
    columns = above[1].shape[0] + above[3].shape[0]
    out = (size, padded, columns // len(orders))
    return pl.pallas_call(
        functools.partial(attention_weight_grad, orders, rows),
        in_specs=[pl.BlockSpec(memory_space=pl.ANY)] * 8,
        out_specs=[pl.BlockSpec(memory_space=pltpu.VMEM)] * len(orders),
        out_shape=[shape_of(out, bf16)] * len(orders),
        scratch_shapes=[pltpu.VMEM((a.shape[0], 2 * length), bf16) for a in above]
        + [pltpu.SemaphoreType.DMA((8,))],
        compiler_params=pltpu.CompilerParams(vmem_limit_bytes=44 * MIB),
        cost_estimate=cost(4 * length * features * columns, *above, *below),
        name="attention_weight_grad",
    )(*in_hbm(*above, *below))


def block_grad(grad_ref, normed_ref, inverse_ref, own_ref, other_ref, gain_ref, out_ref):
    back = norm_back(normed_ref[...], inverse_ref[...], gain_ref[...], joined_sum(own_ref, other_ref))
    out_ref[...] = (grad_ref[...].astype(f32) + back).astype(out_ref.dtype)


def call_block_grad(grad, normed, inverse, own, other, gain, kind):
    features, length = grad.shape
    spec = functools.partial(token_spec, width=FFN_BLOCK)
    return pl.pallas_call(
        block_grad,
        grid=(length // FFN_BLOCK,),
        in_specs=[spec(features)] * 2 + [spec(1)] + [spec(features)] * 2 + [full_spec(gain.shape)],
        out_specs=spec(features),
        out_shape=shape_of((features, length), kind),
        compiler_params=pltpu.CompilerParams(vmem_limit_bytes=32 * MIB),
        cost_estimate=cost(0, grad, normed, own, other),
        name="block_grad",
    )(*in_hbm(grad, normed), inverse, own, other, gain)


def gather_groups(owner, device, query_ref, key_ref, value_ref, out_ref, wqkv_out, wout_out):
    slot = pl.program_id(0)
    _, held = group_of(slot, owner, device)
    group_cols, head = query_ref.shape[1], key_ref.shape[1]

    def place(first, height, piece):
        rows = pl.ds(pl.multiple_of(first, 16), height)
        return rows, jnp.where(held, piece, jnp.zeros_like(piece))

    base = slot * (group_cols + 2 * head)
    rows, piece = place(base, group_cols, query_ref[0])
    wqkv_out[rows, :] = piece
    rows, piece = place(base + group_cols, head, key_ref[0])
    wqkv_out[rows, :] = piece
    rows, piece = place(base + group_cols + head, head, value_ref[0])
    wqkv_out[rows, :] = piece
    rows, piece = place(slot * group_cols, group_cols, out_ref[0])
    wout_out[rows, :] = piece


def group_of(slot, owner, device):
    found, count = 0, 0
    for group in range(owner.shape[0]):
        mine = owner[group] == device[0]
        found = jnp.where(mine & (count == slot), group, found)
        count = count + jnp.where(mine, 1, 0)
    return found, count > slot


def call_gather_groups(owner, device, w_query, w_key, w_value, w_out, slots):
    features = w_query.shape[2]
    arrays = (w_query, w_key, w_value, w_out)
    joint = slots * (w_query.shape[1] + w_key.shape[1] + w_value.shape[1])
    outs = [(joint, features), (slots * w_out.shape[1], features)]
    return pl.pallas_call(
        gather_groups,
        grid_spec=pltpu.PrefetchScalarGridSpec(
            num_scalar_prefetch=2,
            grid=(slots,),
            in_specs=[
                pl.BlockSpec(
                    (1,) + a.shape[1:], lambda s, owner, device: (group_of(s, owner, device)[0], 0, 0)
                )
                for a in arrays
            ],
            out_specs=[out_full_spec(o) for o in outs],
        ),
        out_shape=[shape_of(o, bf16) for o in outs],
        name="gather_groups",
    )(owner, device, *arrays)


def rotary_tables(length):
    position = np.arange(length, dtype=np.float64)[None, :]
    column = np.arange(HEAD // 2, dtype=np.float64)[:, None]
    angles = position * np.exp(column * (-2.0 * math.log(10000.0) / HEAD))
    return jnp.asarray(np.cos(angles), f32), jnp.asarray(np.sin(angles), f32)


def exchange(own):
    return lax.ppermute(own, "mp", [(0, 1), (1, 0)])


def stage_plans(bit_count):
    bits = list(range(bit_count))
    turned = [bits[:3], bits[1:3] + bits[:1], bits[2:3] + bits[:2]]
    return [[[bit] for bit in first + bits[3:]] for first in turned]


def shard_order(plan):
    bits = [bit for stage in plan for bit in stage]
    order = []
    for place in range(1 << len(bits)):
        shard = 0
        for rank, bit in enumerate(bits):
            if place >> (len(bits) - 1 - rank) & 1:
                shard |= 1 << bit
        order.append(shard)
    return order


def after(value, *others):
    return lax.optimization_barrier((value, others))[0]


class Stream:
    def __init__(self, payload, plan):
        self.current, self.stages, self.received = payload, list(plan), []

    def send(self):
        stage = self.stages.pop(0)
        size = lax.axis_size("dp")
        index = lax.axis_index("dp")
        mine = 0
        for bit in stage:
            mine = mine * 2 + ((index >> bit) & 1)
        ways = 1 << len(stage)
        pieces = self.current.shape[0] // ways
        self.kept = lax.dynamic_slice_in_dim(self.current, mine * pieces, pieces, 0)
        self.received, sent = [], []
        for offset in range(1, ways):
            mask = 0
            for rank, bit in enumerate(stage):
                if offset >> (len(stage) - 1 - rank) & 1:
                    mask |= 1 << bit
            piece = lax.dynamic_slice_in_dim(self.current, (mine ^ offset) * pieces, pieces, 0)
            sent.append(piece)
            self.received.append(lax.ppermute(piece, "dp", [(i, i ^ mask) for i in range(size)]))
        return tuple(sent)

    def add(self, *others):
        received = after(tuple(self.received), *others) if others else self.received
        total = self.kept.astype(f32)
        for piece in received:
            total = total + piece.astype(f32)
        self.current = total.astype(bf16) if self.stages else total
        self.received = []

    def next_stage(self, *others):
        if self.received:
            self.add(*others)
        return self.send() if self.stages else (self.current,)


def merged(streams, *others):
    for stream in streams:
        stream.add(*others)
    return Stream(jnp.concatenate([stream.current for stream in streams], axis=2), streams[0].stages)


def per_device(
    tokens_in,
    segment_ids,
    kv_owner,
    w_query,
    w_key,
    w_value,
    w_out,
    attn_gain,
    w_gate,
    w_up,
    w_down,
    ffn_gain,
    cotangent,
):
    features = tokens_in.shape[2]
    length = tokens_in.shape[1]
    group_cols = w_query.shape[2]
    heads = group_cols // HEAD
    slots = (kv_owner.shape[0] + lax.axis_size("mp") - 1) // lax.axis_size("mp")
    size = lax.axis_size("dp")
    rows = features // size

    device = lax.axis_index("mp").astype(jnp.int32)[None]
    wqkv, wout = call_gather_groups(
        kv_owner, device, *(jnp.swapaxes(w, 1, 2) for w in (w_query, w_key, w_value)), w_out, slots
    )
    w_down = w_down.T
    segments = segment_ids[0]
    cosine, sine = rotary_tables(length)
    gain_one, gain_two = (
        jnp.broadcast_to(gain.astype(f32)[:, None], (features, LANES)) for gain in (attn_gain, ffn_gain)
    )

    parts = (tokens_in[0].T,)
    saved = []
    for _ in range(REPEAT):
        outs = list(call_attention_forward(segments, parts, gain_one, wqkv, wout, cosine, sine, slots, heads))
        hidden = outs.pop(0) if len(parts) == 3 else parts[0]
        normed, inverse, query, key, turned_key, value, attended, partial = outs
        middle, normed_two, inverse_two, gate, lift, inner, partial_two = call_ffn_forward(
            hidden, partial, exchange(partial), gain_two, w_gate, w_up, w_down
        )
        parts = (middle, partial_two, exchange(partial_two))
        saved.append((
            normed, inverse, query, key, turned_key, value, attended, normed_two, inverse_two, gate, lift, inner,
        ))

    plans = stage_plans(size.bit_length() - 1)
    orders = [shard_order(plan) for plan in plans]
    joint = ()
    grad = cotangent[0].T
    for r in reversed(range(REPEAT)):
        (normed, inverse, query, key, turned_key, value, attended,
         normed_two, inverse_two, gate, lift, inner) = saved[r]
        last = r == 0
        outs = list(call_ffn_backward(grad, joint, gate, lift, w_gate, w_up, w_down))
        if joint:
            grad = outs.pop(0)
        ffn_grad = grad
        grad_gate, grad_lift, partial = outs
        other = exchange(partial)
        if not last:
            parts = after(parts, partial)
            tokens_out = (parts[0] + (parts[1].astype(f32) + parts[2].astype(f32))).astype(bf16)
            grad = after(grad, tokens_out)
        else:
            payloads = call_ffn_weight_grad(
                (above["normed_two"], normed_two), (above["ffn_grad"], ffn_grad),
                ((above["grad_gate"], grad_gate), (above["grad_lift"], grad_lift), (above["inner"], inner)),
                orders,
            )
            track_a, track_b, down = (Stream(payload, plan) for payload, plan in zip(payloads, plans))
            partial = after(partial, [stream.send() for stream in (track_a, track_b, down)])
        grad, projected, partial_two = call_attention_backward(
            segments, grad, partial, other, normed_two, inverse_two, gain_two, wout, wqkv, attended, query,
            key, turned_key, value, cosine, sine,
        )
        other_two = exchange(partial_two)
        if not last:
            above = dict(
                ffn_grad=ffn_grad, inner=inner, normed_two=normed_two, grad_lift=grad_lift,
                grad_gate=grad_gate, attention=(normed, projected, grad, attended),
            )
        joint = (normed, inverse, partial_two, other_two, gain_one)
    sent = [stream.next_stage(projected) for stream in (track_a, track_b, down)]
    payloads = call_attention_weight_grad(
        above["attention"], (normed, after(projected, sent), grad, attended), orders
    )
    tracks = [Stream(payload, plan) for payload, plan in zip(payloads, plans)]
    for stream in (track_a, track_b, down):
        stream.add(payloads, other_two)
    sent = [stream.send() for stream in (track_a, track_b, *tracks)]
    grad_in = call_block_grad(after(grad, sent), *joint, f32)
    both = merged((track_a, track_b), grad_in)
    down.current = after(down.current, grad_in)
    sent = [both.send(), down.send()]
    sent = [stream.next_stage(sent) for stream in tracks]
    sent = [down.next_stage(sent)]
    while len(tracks[0].stages) > 1:
        sent = [stream.next_stage(sent) for stream in tracks]
    attn = merged(tracks, sent)
    pending = [both, down, attn]
    while any(stream.stages for stream in pending):
        for stream in pending:
            stream.next_stage()
    for stream in pending:
        if stream.received:
            stream.add()
    gate_total, up_total = jnp.split(both.current[0], 2, axis=1)
    down_total = down.current[0]
    attn_total = attn.current[0, :rows]

    start = lax.axis_index("dp") * rows

    def my_rows(weights):
        return lax.dynamic_slice_in_dim(weights, start, rows, 0).astype(f32)

    gate_total, up_total, down_total = (total[:rows] for total in (gate_total, up_total, down_total))
    wqkv = after(wqkv, grad_in)
    chosen = (jnp.arange(rows)[:, None] + start == jnp.arange(features)[None, :]).astype(bf16)
    wqkv_rows = matmul(chosen, wqkv, NT)
    joint_cols = wqkv.shape[0]
    gains = jnp.stack([
        jnp.sum(attn_total[:, :joint_cols] * wqkv_rows, axis=1),
        jnp.sum(gate_total * my_rows(w_gate) + up_total * my_rows(w_up), axis=1),
    ])
    gains = gains + exchange(gains)
    gains = gains / lax.dynamic_slice_in_dim(jnp.stack([attn_gain, ffn_gain]), start, rows, 1).astype(f32)

    ends = [group_cols, group_cols + HEAD]
    by_slot = jnp.moveaxis(attn_total[:, :joint_cols].reshape(rows, slots, -1), 1, 0)
    return (
        tokens_out.T[None],
        grad_in.T[None],
        by_slot[:, :, : ends[0]],
        by_slot[:, :, ends[0] : ends[1]],
        by_slot[:, :, ends[1] :],
        attn_total[:, joint_cols:].T.reshape(slots, group_cols, rows),
        gate_total,
        up_total,
        down_total.T,
        gains[0],
        gains[1],
    )


def solution(mesh):
    in_specs = (
        P("dp", None, None),
        P("dp", None),
        P(),
        P(),
        P(),
        P(),
        P(),
        P(),
        P(None, "mp"),
        P(None, "mp"),
        P("mp", None),
        P(),
        P("dp", None, None),
    )
    out_specs = (
        P("dp", None, None),
        P("dp", None, None),
        P("mp", "dp", None),
        P("mp", "dp", None),
        P("mp", "dp", None),
        P("mp", None, "dp"),
        P("dp", "mp"),
        P("dp", "mp"),
        P("mp", "dp"),
        P("dp"),
        P("dp"),
    )
    return jax.shard_map(
        per_device, mesh=mesh, in_specs=in_specs, out_specs=out_specs, check_vma=False
    )
```

```python
import functools
import math

import jax
import jax.numpy as jnp
import numpy as np
from jax import lax
from jax.experimental import pallas as pl
from jax.experimental.pallas import tpu as pltpu
from jax.sharding import PartitionSpec as P

REPEAT = 2
BLOCK = 256
FFN_BLOCK = 512
LANES = 128
HEAD = 64
GROUP = 3
VROWS = 80
epsilon = 1e-05
masked_value = -1e30
LOG2E = math.log2(math.e)
LN2 = math.log(2.0)
f32 = jnp.float32
bf16 = jnp.bfloat16
NN = (((1,), (0,)), ((), ()))
NT = (((1,), (1,)), ((), ()))
TN = (((0,), (0,)), ((), ()))
MIB = 1024 * 1024


def matmul(a, b, dims=NN):
    return lax.dot_general(a, b, dims, preferred_element_type=f32)


def wide(column, width):
    return jnp.concatenate([column] * (width // LANES), axis=1)


def inverse_rms(values):
    return lax.rsqrt(jnp.mean(values * values, axis=0, keepdims=True) + epsilon)


def normalise(values, gain, inverse_out):
    inverse = inverse_rms(values)
    inverse_out[...] = inverse
    return (values * inverse * wide(gain, values.shape[1])).astype(bf16)


def norm_back(normed, inverse, gain, grad_normed):
    normed = normed.astype(f32)
    inner_mean = jnp.mean(grad_normed * normed, axis=0, keepdims=True)
    width = normed.shape[1]
    return inverse * (grad_normed * wide(gain, width) - normed * wide(1.0 / gain, width) * inner_mean)


def joined_sum(own_ref, other_ref):
    return own_ref[...].astype(f32) + other_ref[...].astype(f32)


def three_parts(value):
    high = value.astype(bf16).astype(f32)
    rest = value - high
    middle = rest.astype(bf16).astype(f32)
    return high, middle, rest - middle


def part_rows(value, first):
    row = lax.broadcasted_iota(jnp.int32, (8, value.shape[1]), 0)
    out = jnp.zeros((8, value.shape[1]), f32)
    for number, part in enumerate(three_parts(value)):
        out = jnp.where(row == first + number, part, out)
    return out


def causal_bias(heads):
    key = lax.broadcasted_iota(jnp.int32, (BLOCK, heads * BLOCK), 0)
    query = lax.broadcasted_iota(jnp.int32, (BLOCK, heads * BLOCK), 1) % BLOCK
    return jnp.where(key <= query, 0.0, masked_value)


def reaches(segments, step, back):
    last = jnp.maximum((step - back + 1) * BLOCK - 1, 0)
    return (step >= back) & (segments[last] == segments[step * BLOCK])


def block_at(index):
    return pl.ds(pl.multiple_of(index * BLOCK, BLOCK), BLOCK)


def turn(upper, lower, cosine, sine):
    return upper * cosine - lower * sine, lower * cosine + upper * sine


def attention_forward(joined, slots, heads, segments, *refs):
    refs = list(refs)
    hidden = refs.pop(0)[...].astype(f32)
    if joined:
        hidden = hidden + joined_sum(refs.pop(0), refs.pop(0))
    gain_ref, wqkv_ref, wout_ref, cos_ref, sin_ref, segment_ref = refs[:6]
    refs = refs[6:]
    if joined:
        refs.pop(0)[...] = hidden
    (normed_out, inverse_out, query_out, key_out, turned_key_out, value_out, attended_out, partial_out,
     turned_value, tri_ref) = refs
    step = pl.program_id(0)
    here = block_at(step)

    @pl.when(step == 0)
    def _():
        tri_ref[...] = causal_bias(heads)

    normed = normalise(hidden, gain_ref[...], inverse_out)
    normed_out[...] = normed
    projected = matmul(wqkv_ref[...], normed)
    cosine, sine = cos_ref[...], sin_ref[...]
    half = HEAD // 2

    same = lax.broadcasted_iota(jnp.int32, (8, BLOCK), 0) == segment_ref[...]
    query_rows = jnp.where(same, 1.0, 0.0)
    key_rows = jnp.where(same, 0.0, masked_value)
    row = lax.broadcasted_iota(jnp.int32, (8, BLOCK), 0)
    minus_rows = jnp.where(row < 3, -1.0, 0.0)
    scale = LOG2E / math.sqrt(HEAD)
    query_fill = jnp.concatenate(
        [query_rows, jnp.zeros((LANES - HEAD - 8, BLOCK), f32)], axis=0
    ).astype(bf16)

    for s in range(slots):
        for j in range(heads + 2):
            first = (s * (heads + 2) + j) * HEAD
            piece = projected[first : first + HEAD]
            if j > heads:
                value = jnp.concatenate([piece, jnp.ones((LANES - HEAD, BLOCK), f32)], axis=0)
                value_out[here, s * LANES : (s + 1) * LANES] = value.T.astype(bf16)
                turned_value[s * VROWS : (s + 1) * VROWS, here] = value[:VROWS].astype(bf16)
                continue
            upper, lower = turn(piece[:half], piece[half:], cosine, sine)
            if j < heads:
                lanes = slice(j * BLOCK, (j + 1) * BLOCK)
                query_out[0, s, :HEAD, lanes] = jnp.concatenate(
                    [upper * scale, lower * scale], axis=0
                ).astype(bf16)
                query_out[0, s, HEAD:, lanes] = query_fill
            else:
                turned_key_out[s * HEAD : (s + 1) * HEAD, :] = jnp.concatenate(
                    [upper, lower], axis=0
                ).astype(bf16)
                whole = jnp.concatenate(
                    [upper, lower, key_rows, minus_rows, jnp.zeros((LANES - HEAD - 16, BLOCK), f32)],
                    axis=0,
                )
                key_out[here, s * LANES : (s + 1) * LANES] = whole.T.astype(bf16)

    query_rows = jnp.concatenate([query_rows] * heads, axis=1)

    def attend(blocks):
        width = blocks * BLOCK
        keys = pl.ds(pl.multiple_of((step + 1 - blocks) * BLOCK, BLOCK), width)
        scores = [
            matmul(key_out[keys, s * LANES : (s + 1) * LANES], query_out[0, s]) for s in range(slots)
        ]
        tops, weights = [], []
        for score in scores:
            last = score[width - BLOCK :] + tri_ref[...]
            if blocks > 1:
                score = jnp.concatenate([score[: width - BLOCK], last], axis=0)
            else:
                score = last
            tops.append(jnp.max(score, axis=0, keepdims=True))
            weights.append(jnp.exp2(score - tops[-1]).astype(bf16))
        summed = [
            matmul(turned_value[s * VROWS : (s + 1) * VROWS, keys], weights[s]) for s in range(slots)
        ]
        for s in range(slots):
            weight_sum = summed[s][HEAD : HEAD + 1]
            out = (summed[s][:HEAD] * (1.0 / weight_sum)).astype(bf16)
            for j in range(heads):
                first = (s * heads + j) * HEAD
                attended_out[first : first + HEAD, :] = out[:, j * BLOCK : (j + 1) * BLOCK]
            query_out[0, s, HEAD : HEAD + 16, :] = jnp.concatenate(
                [query_rows, part_rows(tops[s] + jnp.log2(weight_sum), 0)], axis=0
            ).astype(bf16)

    one = reaches(segments, step, 1)
    two = reaches(segments, step, 2)
    pl.when(jnp.logical_not(one))(functools.partial(attend, 1))
    pl.when(one & jnp.logical_not(two))(functools.partial(attend, 2))
    pl.when(two)(functools.partial(attend, 3))
    partial_out[...] = matmul(wout_ref[...], attended_out[...], TN).astype(bf16)


def chunks(width):
    return [slice(start, start + 256) for start in range(0, width, 256)]


def cost(flops, *arrays):
    size = sum(math.prod(a.shape) * a.dtype.itemsize for a in arrays)
    return pl.CostEstimate(flops=int(flops), bytes_accessed=size, transcendentals=0)


def token_spec(rows, width=BLOCK):
    return pl.BlockSpec((rows, width), lambda i, *_: (0, i))


def unit_shape(units, length):
    return shape_of((length // FFN_BLOCK, units, FFN_BLOCK), bf16)


def unit_spec(units):
    return pl.BlockSpec((1, units, FFN_BLOCK), lambda i: (i, 0, 0))


def full_spec(shape):
    return pl.BlockSpec(
        shape, lambda *_: (0,) * len(shape), pipeline_mode=pl.Buffered(buffer_count=1)
    )


def out_full_spec(shape):
    return pl.BlockSpec(shape, lambda *_: (0,) * len(shape))


shape_of = pltpu.HBM
anywhere = jax.ShapeDtypeStruct


def in_hbm(*arrays):
    return tuple(pltpu.with_memory_space_constraint(array, pltpu.HBM) for array in arrays)


def call_attention_forward(segments, parts, gain, wqkv, wout, cosine, sine, slots, heads):
    features, length = parts[0].shape
    joined = len(parts) == 3
    total = slots * heads
    big = shape_of((features, length), bf16)
    outs = [
        (big, token_spec(features)),
        (shape_of((1, length), f32), token_spec(1)),
        (
            shape_of((length // BLOCK, slots, LANES, heads * BLOCK), bf16),
            pl.BlockSpec((1, slots, LANES, heads * BLOCK), lambda i, *_: (i, 0, 0, 0)),
        ),
        (shape_of((length, slots * LANES), bf16), out_full_spec((length, slots * LANES))),
        (shape_of((slots * HEAD, length), bf16), token_spec(slots * HEAD)),
        (shape_of((length, slots * LANES), bf16), out_full_spec((length, slots * LANES))),
        (shape_of((total * HEAD, length), bf16), token_spec(total * HEAD)),
        (anywhere((features, length), bf16), token_spec(features)),
    ]
    if joined:
        outs.insert(0, (shape_of((features, length), f32), token_spec(features)))
    return pl.pallas_call(
        functools.partial(attention_forward, joined, slots, heads),
        grid_spec=pltpu.PrefetchScalarGridSpec(
            num_scalar_prefetch=1,
            grid=(length // BLOCK,),
            in_specs=[token_spec(features)] * len(parts)
            + [full_spec(a.shape) for a in (gain, wqkv, wout)]
            + [token_spec(HEAD // 2)] * 2
            + [token_spec(1)],
            out_specs=[spec for _, spec in outs],
            scratch_shapes=[
                pltpu.VMEM((slots * VROWS, length), bf16),
                pltpu.VMEM((BLOCK, heads * BLOCK), f32),
            ],
        ),
        out_shape=[shape for shape, _ in outs],
        compiler_params=pltpu.CompilerParams(vmem_limit_bytes=32 * MIB),
        cost_estimate=cost(2 * length * features * (wqkv.shape[0] + wout.shape[0]) + 12e9, *parts),
        name="attention_forward",
    )(segments, *in_hbm(parts[0]), *parts[1:], gain, wqkv, wout, cosine, sine, segments[None, :])


def ffn_forward(hidden_ref, own_ref, other_ref, gain_ref, gate_ref, up_ref, down_ref,
                middle_out, normed_out, inverse_out, gate_out, lift_out, inner_out, partial_out):
    middle = hidden_ref[...].astype(f32) + joined_sum(own_ref, other_ref)
    middle_out[...] = middle
    normed = normalise(middle, gain_ref[...], inverse_out)
    normed_out[...] = normed
    for chunk in chunks(gate_ref.shape[1]):
        gate = matmul(gate_ref[:, chunk], normed, TN)
        lift = matmul(up_ref[:, chunk], normed, TN)
        gate_out[0, chunk, :] = gate.astype(bf16)
        lift_out[0, chunk, :] = lift.astype(bf16)
        inner_out[0, chunk, :] = (gate * jax.nn.sigmoid(gate) * lift).astype(bf16)
    partial_out[...] = matmul(down_ref[...], inner_out[0]).astype(bf16)


def call_ffn_forward(hidden, own, other, gain, w_gate, w_up, w_down):
    features, length = hidden.shape
    units = w_gate.shape[1]
    spec = functools.partial(token_spec, width=FFN_BLOCK)
    return pl.pallas_call(
        ffn_forward,
        grid=(length // FFN_BLOCK,),
        in_specs=[spec(features)] * 3 + [full_spec(a.shape) for a in (gain, w_gate, w_up, w_down)],
        out_specs=[spec(features)] * 2 + [spec(1)] + [unit_spec(units)] * 3 + [spec(features)],
        out_shape=[
            shape_of((features, length), f32), shape_of((features, length), bf16),
            shape_of((1, length), f32), *[unit_shape(units, length)] * 3,
            anywhere((features, length), bf16),
        ],
        compiler_params=pltpu.CompilerParams(vmem_limit_bytes=40 * MIB),
        cost_estimate=cost(6 * length * features * units, hidden),
        name="ffn_forward",
    )(*in_hbm(hidden), own, other, gain, w_gate, w_up, w_down)


def ffn_backward(joined, grad_ref, *refs):
    grad = grad_ref[...]
    if joined:
        normed_ref, inverse_ref, own_ref, other_ref, gain_ref = refs[:5]
        refs = refs[5:]
        back = norm_back(normed_ref[...], inverse_ref[...], gain_ref[...], joined_sum(own_ref, other_ref))
        grad = (grad.astype(f32) + back).astype(bf16)
    gate_in, lift_in, gate_ref, up_ref, down_ref = refs[:5]
    refs = refs[5:]
    if joined:
        refs[0][...] = grad
        refs = refs[1:]
    grad_gate_out, grad_lift_out, partial_out = refs
    for chunk in chunks(gate_ref.shape[1]):
        grad_inner = matmul(down_ref[:, chunk], grad, TN)
        gate = gate_in[0, chunk, :].astype(f32)
        lift = lift_in[0, chunk, :].astype(f32)
        sigmoid = jax.nn.sigmoid(gate)
        grad_gate = grad_inner * lift * sigmoid * (1.0 + gate * (1.0 - sigmoid))
        grad_gate_out[0, chunk, :] = grad_gate.astype(bf16)
        grad_lift_out[0, chunk, :] = (grad_inner * gate * sigmoid).astype(bf16)
    partial = matmul(gate_ref[...], grad_gate_out[0]) + matmul(up_ref[...], grad_lift_out[0])
    partial_out[...] = partial.astype(bf16)


def call_ffn_backward(grad, joint, gate, lift, w_gate, w_up, w_down):
    features, length = grad.shape
    units = w_gate.shape[1]
    spec = functools.partial(token_spec, width=FFN_BLOCK)
    joint_specs, extra = [], []
    if joint:
        normed, inverse, own, other, gain = joint
        joint = (*in_hbm(normed), inverse, own, other, gain)
        joint_specs = [spec(features), spec(1), spec(features), spec(features), full_spec(gain.shape)]
        extra = [(shape_of((features, length), bf16), spec(features))]
    outs = extra + [(unit_shape(units, length), unit_spec(units))] * 2
    outs.append((anywhere((features, length), bf16), spec(features)))
    return pl.pallas_call(
        functools.partial(ffn_backward, bool(joint)),
        grid=(length // FFN_BLOCK,),
        in_specs=[spec(features)] + joint_specs + [unit_spec(units)] * 2
        + [full_spec(a.shape) for a in (w_gate, w_up, w_down)],
        out_specs=[spec for _, spec in outs],
        out_shape=[shape for shape, _ in outs],
        compiler_params=pltpu.CompilerParams(vmem_limit_bytes=40 * MIB),
        cost_estimate=cost(6 * length * features * units, grad),
        name="ffn_backward",
    )(*in_hbm(grad), *joint, *in_hbm(gate, lift), w_gate, w_up, w_down)


def attention_backward(slots, heads, segments, grad_ref, own_ref, other_ref, normed_ref, inverse_ref,
                       gain_ref, wout_ref, wqkv_ref, attended_ref, query_ref, key_ref, turned_key_ref,
                       value_ref, cos_ref, sin_ref,
                       attn_grad_out, projected_out, partial_out,
                       key_total, value_total, query_total, grad_heads, tri_ref):
    step = pl.num_programs(0) - 1 - pl.program_id(0)
    half = HEAD // 2

    @pl.when(pl.program_id(0) == 0)
    def _():
        key_total[...] = jnp.zeros_like(key_total)
        value_total[...] = jnp.zeros_like(value_total)
        tri_ref[...] = causal_bias(heads)

    back = norm_back(normed_ref[...], inverse_ref[...], gain_ref[...], joined_sum(own_ref, other_ref))
    attn_grad = (grad_ref[...].astype(f32) + back).astype(bf16)
    attn_grad_out[...] = attn_grad
    grad_attended = matmul(wout_ref[...], attn_grad).astype(bf16)
    zeros = jnp.zeros((LANES - HEAD - 8, BLOCK), f32)
    for s in range(slots):
        for j in range(heads):
            first = (s * heads + j) * HEAD
            mine = grad_attended[first : first + HEAD]
            out = attended_ref[first : first + HEAD, :]
            delta = jnp.sum(mine.astype(f32) * out.astype(f32), axis=0, keepdims=True)
            lanes = slice(j * BLOCK, (j + 1) * BLOCK)
            grad_heads[s, :HEAD, lanes] = mine
            grad_heads[s, HEAD:, lanes] = jnp.concatenate(
                [part_rows(-delta, 0), zeros], axis=0
            ).astype(bf16)

    def visit(back):
        keys = block_at(step - back)
        columns = [slice(s * LANES, (s + 1) * LANES) for s in range(slots)]
        features = [slice(s * HEAD, (s + 1) * HEAD) for s in range(slots)]
        scores = [matmul(key_ref[keys, columns[s]], query_ref[0, s]) for s in range(slots)]
        grad_weights = [matmul(value_ref[keys, columns[s]], grad_heads[s]) for s in range(slots)]
        weights, grad_scores = [], []
        for s in range(slots):
            score = scores[s] + tri_ref[...] if back == 0 else scores[s]
            weight = jnp.exp2(score)
            weights.append(weight.astype(bf16))
            grad_scores.append((weight * grad_weights[s]).astype(bf16))
        for s in range(slots):
            value_total[features[s], keys] += matmul(grad_heads[s, :HEAD, :], weights[s], NT)
            key_total[features[s], keys] += matmul(query_ref[0, s, :HEAD, :], grad_scores[s], NT)
            update = matmul(turned_key_ref[features[s], keys], grad_scores[s])
            if back == 0:
                query_total[s] = update
            else:
                query_total[s] += update

    visit(0)
    for back in (1, 2):
        pl.when(reaches(segments, step, back))(functools.partial(visit, back))

    cosine, sine = cos_ref[...], sin_ref[...]
    here = block_at(step)
    for s in range(slots):
        for j in range(heads + 2):
            if j < heads:
                piece = query_total[s, :, j * BLOCK : (j + 1) * BLOCK] * (1.0 / math.sqrt(HEAD))
            elif j == heads:
                piece = key_total[s * HEAD : (s + 1) * HEAD, here] * LN2
            else:
                piece = value_total[s * HEAD : (s + 1) * HEAD, here]
            if j <= heads:
                upper, lower = turn(piece[:half], piece[half:], cosine, -sine)
                piece = jnp.concatenate([upper, lower], axis=0)
            first = (s * (heads + 2) + j) * HEAD
            projected_out[first : first + HEAD, :] = piece.astype(bf16)
    partial_out[...] = matmul(wqkv_ref[...], projected_out[...], TN).astype(bf16)


def call_attention_backward(segments, grad, own, other, normed, inverse, gain, wout, wqkv, attended, query,
                            key, turned_key, value, cosine, sine):
    features, length = grad.shape
    count = length // BLOCK
    slots, wide_heads = query.shape[1], query.shape[3]
    heads = wide_heads // BLOCK

    def spec(rows):
        return pl.BlockSpec((rows, BLOCK), lambda i, *_: (0, count - 1 - i))

    return pl.pallas_call(
        functools.partial(attention_backward, slots, heads),
        grid_spec=pltpu.PrefetchScalarGridSpec(
            num_scalar_prefetch=1,
            grid=(count,),
            in_specs=[spec(features)] * 4 + [spec(1)]
            + [full_spec(a.shape) for a in (gain, wout, wqkv)]
            + [spec(attended.shape[0])]
            + [pl.BlockSpec((1, slots, LANES, wide_heads), lambda i, *_: (count - 1 - i, 0, 0, 0))]
            + [full_spec(a.shape) for a in (key, turned_key, value)]
            + [spec(HEAD // 2)] * 2,
            out_specs=[spec(features), spec(wqkv.shape[0]), spec(features)],
            scratch_shapes=[
                pltpu.VMEM((slots * HEAD, length), f32),
                pltpu.VMEM((slots * HEAD, length), f32),
                pltpu.VMEM((slots, HEAD, wide_heads), f32),
                pltpu.VMEM((slots, LANES, wide_heads), bf16),
                pltpu.VMEM((BLOCK, wide_heads), f32),
            ],
        ),
        out_shape=[
            shape_of((features, length), bf16), shape_of((wqkv.shape[0], length), bf16),
            anywhere((features, length), bf16),
        ],
        compiler_params=pltpu.CompilerParams(vmem_limit_bytes=30 * MIB),
        cost_estimate=cost(2 * length * features * (wqkv.shape[0] + wout.shape[0]) + slots * 8e9, grad),
        name="attention_backward",
    )(segments, *in_hbm(grad), own, other, *in_hbm(normed), inverse, gain, wout, wqkv,
      *in_hbm(attended, query), key, turned_key, value, cosine, sine)


def shard_rows(total, out_ref, order, rows, mine, first=0):
    total = total.astype(bf16)
    columns = slice(first, first + total.shape[1])
    half = len(order) // 2
    for place, shard in enumerate(order):
        side = mine if place < half else 1 - mine
        out_ref[side, place % half, :rows, columns] = total[shard * rows : (shard + 1) * rows]
        if out_ref.shape[2] > rows:
            out_ref[side, place % half, rows:, columns] = jnp.zeros(
                (out_ref.shape[2] - rows, total.shape[1]), bf16
            )


def begin_sending(staged, kept, sent, kept_signal, sent_signal):
    copies = [
        pltpu.make_async_copy(staged.at[1], sent, sent_signal),
        pltpu.make_async_copy(staged.at[0], kept, kept_signal),
    ]
    begin(copies)
    return copies


def fetches(pairs, arrived):
    groups, count = [], 0
    for sources, target in pairs:
        parts = []
        for source in sources:
            parts += [source] if len(source.shape) == 2 else [source.at[i] for i in range(source.shape[0])]
        first, group = 0, []
        for part in parts:
            lanes = target.at[:, pl.ds(first, part.shape[1])]
            group.append(pltpu.make_async_copy(part, lanes, arrived.at[count]))
            first += part.shape[1]
            count += 1
        groups.append(group)
    return groups


def begin(copies):
    for copy in copies:
        copy.start()


def finish(copies):
    for copy in copies:
        copy.wait()


def halves_product(left, right, copies):
    length = left.shape[1] // 2
    finish(copies[:2])
    total = matmul(left[:, :length], right[:, :length], NT)
    finish(copies[2:])
    return total + matmul(left[:, length:], right[:, length:], NT)


def ffn_weight_grad(orders, rows, bits, *refs):
    sources, outs = refs[:10], refs[10:16]
    buffers, staged, arrived, left = refs[16:21], refs[21], refs[22], refs[23]
    copies = fetches([(sources[2 * i : 2 * i + 2], buffers[i]) for i in range(5)], arrived)
    normed, gates, lifts, grads, inners = buffers
    begin(copies[0] + copies[1])
    outgoing = []

    def write(number, product):
        slot = number % 2
        if number >= 2:
            finish(outgoing[number - 2])
        for chunk in chunks(staged.shape[4]):
            shard_rows(product(chunk), staged.at[slot], orders[number], rows, bits[number], chunk.start)
        outgoing.append(
            begin_sending(
                staged.at[slot], outs[2 * number], outs[2 * number + 1],
                left.at[2 * number], left.at[2 * number + 1],
            )
        )

    finish(copies[0] + copies[1])
    begin(copies[2] + copies[3] + copies[4])
    write(0, lambda chunk: matmul(normed[...], gates[chunk, :], NT))
    finish(copies[2])
    write(1, lambda chunk: matmul(normed[...], lifts[chunk, :], NT))
    finish(copies[3] + copies[4])
    write(2, lambda chunk: matmul(grads[...], inners[chunk, :], NT))
    for pair in outgoing[1:]:
        finish(pair)


def call_weight_grad(kernel, name, bits, pairs, orders, columns, stages, flops):
    features, length = pairs[0][0].shape
    arrivals = sum(len(pair) * (1 if pair[0].ndim == 2 else pair[0].shape[0]) for pair in pairs)
    size = len(orders[0])
    rows = features // size
    padded = -(-rows // 16) * 16
    out = (size // 2, padded, columns)
    outs = pl.pallas_call(
        functools.partial(kernel, orders, rows),
        grid_spec=pltpu.PrefetchScalarGridSpec(
            num_scalar_prefetch=1,
            grid=(1,),
            in_specs=[pl.BlockSpec(memory_space=pl.ANY)] * (2 * len(pairs)),
            out_specs=[pl.BlockSpec(memory_space=pl.ANY)] * (2 * len(orders)),
            scratch_shapes=[pltpu.VMEM((pair[0].shape[-2], 2 * length), bf16) for pair in pairs]
            + [pltpu.VMEM((stages, 2) + out, bf16)]
            + [pltpu.SemaphoreType.DMA((arrivals,)), pltpu.SemaphoreType.DMA((2 * len(orders),))],
        ),
        out_shape=[shape_of(out, bf16)] * (2 * len(orders)),
        compiler_params=pltpu.CompilerParams(vmem_limit_bytes=52 * MIB),
        cost_estimate=cost(flops, *(array for pair in pairs for array in pair)),
        name=name,
    )(bits, *in_hbm(*(array for pair in pairs for array in pair)))
    return list(zip(outs[::2], outs[1::2]))


def call_ffn_weight_grad(bits, normed, grads, rights, orders):
    units = rights[0][0].shape[1]
    pairs = (normed, rights[0], rights[1], grads, rights[2])
    flops = 12 * normed[0].shape[0] * normed[0].shape[1] * units
    return call_weight_grad(ffn_weight_grad, "ffn_weight_grad", bits, pairs, orders, units, 2, flops)


def attention_weight_grad(orders, rows, bits, *refs):
    sources, outs = refs[:8], refs[8:14]
    buffers, staged, arrived, left = refs[14:18], refs[18], refs[19], refs[20]
    copies = fetches([(sources[2 * i : 2 * i + 2], buffers[i]) for i in range(4)], arrived)
    begin(copies[0] + copies[1])
    outgoing = []
    width = staged.shape[4]

    def write(number, pieces):
        column = 0
        for piece in pieces:
            shard_rows(piece, staged.at[number], orders[number], rows, bits[number], column)
            column += piece.shape[1]
        outgoing.extend(
            begin_sending(
                staged.at[number], outs[2 * number], outs[2 * number + 1],
                left.at[2 * number], left.at[2 * number + 1],
            )
        )

    def project(start, stop):
        return matmul(buffers[0][...], buffers[1][start:stop, :], NT)

    def outward(start, stop):
        return matmul(buffers[2][...], buffers[3][start:stop, :], NT)

    columns, most = buffers[1].shape[0], buffers[3].shape[0]
    rest = 2 * width - columns
    finish(copies[0] + copies[1])
    begin(copies[2] + copies[3])
    write(0, [project(start, start + 256) for start in range(0, width, 256)])
    body, tail = project(width, width + 256), project(width + 256, columns)
    finish(copies[2] + copies[3])
    write(1, [body, jnp.concatenate([tail, outward(0, rest)], axis=1)])
    write(2, [outward(start, min(start + 256, most)) for start in range(rest, most, 256)])
    finish(outgoing)


def call_attention_weight_grad(bits, above, below, orders):
    columns = above[1].shape[0] + above[3].shape[0]
    flops = 4 * above[0].shape[0] * above[0].shape[1] * columns
    return call_weight_grad(
        attention_weight_grad, "attention_weight_grad", bits, list(zip(above, below)), orders,
        columns // len(orders), len(orders), flops,
    )


def block_grad(grad_ref, normed_ref, inverse_ref, own_ref, other_ref, gain_ref, out_ref):
    back = norm_back(normed_ref[...], inverse_ref[...], gain_ref[...], joined_sum(own_ref, other_ref))
    out_ref[...] = (grad_ref[...].astype(f32) + back).astype(out_ref.dtype)


def call_block_grad(grad, normed, inverse, own, other, gain, kind):
    features, length = grad.shape
    spec = functools.partial(token_spec, width=FFN_BLOCK)
    return pl.pallas_call(
        block_grad,
        grid=(length // FFN_BLOCK,),
        in_specs=[spec(features)] * 2 + [spec(1)] + [spec(features)] * 2 + [full_spec(gain.shape)],
        out_specs=spec(features),
        out_shape=shape_of((features, length), kind),
        compiler_params=pltpu.CompilerParams(vmem_limit_bytes=32 * MIB),
        cost_estimate=cost(0, grad, normed, own, other),
        name="block_grad",
    )(*in_hbm(grad, normed), inverse, own, other, gain)


def gather_groups(owner, device, *refs):
    sources, (wqkv_out, wout_out), arrived = refs[:4], refs[4:6], refs[6]
    heights = [source.shape[1] for source in sources]
    joint = sum(heights[:3])
    slots = wqkv_out.shape[0] // joint
    for action in ("start", "wait"):
        for slot in range(slots):
            group, held = group_of(slot, owner, device)
            first = slot * joint
            for place, (source, height) in enumerate(zip(sources, heights)):
                if place < 3:
                    target = wqkv_out.at[pl.ds(first, height)]
                    first += height
                else:
                    target = wout_out.at[pl.ds(slot * height, height)]
                copy = pltpu.make_async_copy(source.at[group], target, arrived.at[4 * slot + place])

                def empty(target=target):
                    target[...] = jnp.zeros(target.shape, bf16)

                pl.when(held)(getattr(copy, action))
                if action == "start":
                    pl.when(jnp.logical_not(held))(empty)


def group_of(slot, owner, device):
    found, count = 0, 0
    for group in range(owner.shape[0]):
        mine = owner[group] == device[0]
        found = jnp.where(mine & (count == slot), group, found)
        count = count + jnp.where(mine, 1, 0)
    return found, count > slot


def call_gather_groups(owner, device, w_query, w_key, w_value, w_out, slots):
    features = w_query.shape[2]
    arrays = (w_query, w_key, w_value, w_out)
    joint = slots * (w_query.shape[1] + w_key.shape[1] + w_value.shape[1])
    outs = [(joint, features), (slots * w_out.shape[1], features)]
    return pl.pallas_call(
        gather_groups,
        grid_spec=pltpu.PrefetchScalarGridSpec(
            num_scalar_prefetch=2,
            grid=(1,),
            in_specs=[pl.BlockSpec(memory_space=pl.ANY)] * 4,
            out_specs=[out_full_spec(o) for o in outs],
            scratch_shapes=[pltpu.SemaphoreType.DMA((4 * slots,))],
        ),
        out_shape=[shape_of(o, bf16) for o in outs],
        name="gather_groups",
    )(owner, device, *in_hbm(*arrays))


def rotary_tables(length):
    position = np.arange(length, dtype=np.float64)[None, :]
    column = np.arange(HEAD // 2, dtype=np.float64)[:, None]
    angles = position * np.exp(column * (-2.0 * math.log(10000.0) / HEAD))
    return jnp.asarray(np.cos(angles), f32), jnp.asarray(np.sin(angles), f32)


def exchange(own):
    return lax.ppermute(own, "mp", [(0, 1), (1, 0)])


def stage_plans(bit_count):
    bits = list(range(bit_count))
    turned = [bits[:3], bits[1:3] + bits[:1], bits[2:3] + bits[:2]]
    return [[[bit] for bit in first + bits[3:]] for first in turned]


def shard_order(plan):
    bits = [bit for stage in plan for bit in stage]
    order = []
    for place in range(1 << len(bits)):
        shard = 0
        for rank, bit in enumerate(bits):
            if place >> (len(bits) - 1 - rank) & 1:
                shard |= 1 << bit
        order.append(shard)
    return order


def after(value, *others):
    return lax.optimization_barrier((value, others))[0]


def slices(arrays, index, pieces):
    parts = [lax.dynamic_slice_in_dim(array, index * pieces, pieces, 0) for array in arrays]
    if len(parts) == 1:
        return parts[0]
    return sum(part.astype(f32) for part in parts).astype(bf16)


class Stream:
    def __init__(self, kept, stages):
        self.kept, self.stages = kept, list(stages)

    @classmethod
    def started(cls, kept, sent, plan):
        stream = cls([[kept]], plan)
        stream.transfer(sent, stream.stages.pop(0)[0])
        return stream

    def transfer(self, sent, bit):
        size = lax.axis_size("dp")
        received = lax.ppermute(sent, "dp", [(i, i ^ (1 << bit)) for i in range(size)])
        if len(self.kept) > 1:
            self.kept = [[jnp.concatenate([terms[0] for terms in self.kept], axis=2)]]
        self.kept[0].append(received)
        self.sent = sent

    def hold(self, *others):
        self.kept = after(self.kept, *others)
        return self

    def send(self):
        bit = self.stages.pop(0)[0]
        mine = (lax.axis_index("dp") >> bit) & 1
        pieces = self.kept[0][0].shape[0] // 2
        sent = [slices(terms, 1 - mine, pieces) for terms in self.kept]
        self.kept = [[slices(terms, mine, pieces)] for terms in self.kept]
        self.transfer(sent[0] if len(sent) == 1 else jnp.concatenate(sent, axis=2), bit)
        return self.sent

    def total(self):
        (terms,) = self.kept
        return sum(term[0].astype(f32) for term in terms)


def joined(streams):
    return Stream([terms for stream in streams for terms in stream.kept], streams[0].stages)


def per_device(
    tokens_in,
    segment_ids,
    kv_owner,
    w_query,
    w_key,
    w_value,
    w_out,
    attn_gain,
    w_gate,
    w_up,
    w_down,
    ffn_gain,
    cotangent,
):
    features = tokens_in.shape[2]
    length = tokens_in.shape[1]
    group_cols = w_query.shape[2]
    heads = group_cols // HEAD
    slots = (kv_owner.shape[0] + lax.axis_size("mp") - 1) // lax.axis_size("mp")
    size = lax.axis_size("dp")
    rows = features // size

    device = lax.axis_index("mp").astype(jnp.int32)[None]
    wqkv, wout = call_gather_groups(
        kv_owner, device, *(jnp.swapaxes(w, 1, 2) for w in (w_query, w_key, w_value)), w_out, slots
    )
    w_down = w_down.T
    segments = segment_ids[0]
    cosine, sine = rotary_tables(length)
    gain_one, gain_two = (
        jnp.broadcast_to(gain.astype(f32)[:, None], (features, LANES)) for gain in (attn_gain, ffn_gain)
    )

    parts = (tokens_in[0].T,)
    saved = []
    for _ in range(REPEAT):
        outs = list(call_attention_forward(segments, parts, gain_one, wqkv, wout, cosine, sine, slots, heads))
        hidden = outs.pop(0) if len(parts) == 3 else parts[0]
        normed, inverse, query, key, turned_key, value, attended, partial = outs
        middle, normed_two, inverse_two, gate, lift, inner, partial_two = call_ffn_forward(
            hidden, partial, exchange(partial), gain_two, w_gate, w_up, w_down
        )
        parts = (middle, partial_two, exchange(partial_two))
        saved.append((
            normed, inverse, query, key, turned_key, value, attended, normed_two, inverse_two, gate, lift, inner,
        ))

    plans = stage_plans(size.bit_length() - 1)
    orders = [shard_order(plan) for plan in plans]
    bits = jnp.stack([(lax.axis_index("dp") >> plan[0][0]) & 1 for plan in plans]).astype(jnp.int32)
    joint = ()
    grad = cotangent[0].T
    for r in reversed(range(REPEAT)):
        (normed, inverse, query, key, turned_key, value, attended,
         normed_two, inverse_two, gate, lift, inner) = saved[r]
        last = r == 0
        outs = list(call_ffn_backward(grad, joint, gate, lift, w_gate, w_up, w_down))
        if joint:
            grad = outs.pop(0)
        ffn_grad = grad
        grad_gate, grad_lift, partial = outs
        other = exchange(partial)
        if not last:
            parts = after(parts, partial)
            tokens_out = (parts[0] + (parts[1].astype(f32) + parts[2].astype(f32))).astype(bf16)
            grad = after(grad, tokens_out)
        else:
            payloads = call_ffn_weight_grad(
                bits, (above["normed_two"], normed_two), (above["ffn_grad"], ffn_grad),
                ((above["grad_gate"], grad_gate), (above["grad_lift"], grad_lift), (above["inner"], inner)),
                orders,
            )
            track_a, track_b, down = (
                Stream.started(*payload, plan) for payload, plan in zip(payloads, plans)
            )
            partial = after(partial, payloads)
        grad, projected, partial_two = call_attention_backward(
            segments, grad, partial, other, normed_two, inverse_two, gain_two, wout, wqkv, attended, query,
            key, turned_key, value, cosine, sine,
        )
        other_two = exchange(partial_two)
        if not last:
            above = dict(
                ffn_grad=ffn_grad, inner=inner, normed_two=normed_two, grad_lift=grad_lift,
                grad_gate=grad_gate, attention=(normed, projected, grad, attended),
            )
        joint = (normed, inverse, partial_two, other_two, gain_one)
    ffn = (track_a, track_b, down)
    sent = [stream.hold(projected).send() for stream in ffn]
    payloads = call_attention_weight_grad(
        bits, above["attention"], (normed, after(projected, sent), grad, attended), orders
    )
    tracks = [Stream.started(*payload, plan) for payload, plan in zip(payloads, plans)]
    for stream in ffn:
        stream.hold(payloads, other_two)
    sent = [stream.send() for stream in (track_a, track_b)]
    grad_in = call_block_grad(after(grad, sent, payloads), *joint, f32)
    both = joined([stream.hold(grad_in) for stream in (track_a, track_b)])
    sent = [both.send(), down.hold(grad_in).send()]
    sent = [stream.hold(sent).send() for stream in tracks]
    sent = [down.hold(sent).send()]
    while len(tracks[0].stages) > 1:
        sent = [stream.hold(sent).send() for stream in tracks]
    attn = joined([stream.hold(sent) for stream in tracks])
    pending = [both, down, attn]
    while any(stream.stages for stream in pending):
        for stream in pending:
            if stream.stages:
                stream.send()
    gate_total, up_total = jnp.split(both.total(), 2, axis=1)
    down_total = down.total()
    attn_total = attn.total()[:rows]

    start = lax.axis_index("dp") * rows

    def my_rows(weights):
        return lax.dynamic_slice_in_dim(weights, start, rows, 0).astype(f32)

    gate_total, up_total, down_total = (total[:rows] for total in (gate_total, up_total, down_total))
    wqkv = after(wqkv, grad_in)
    chosen = (jnp.arange(rows)[:, None] + start == jnp.arange(features)[None, :]).astype(bf16)
    wqkv_rows = matmul(chosen, wqkv, NT)
    joint_cols = wqkv.shape[0]
    gains = jnp.stack([
        jnp.sum(attn_total[:, :joint_cols] * wqkv_rows, axis=1),
        jnp.sum(gate_total * my_rows(w_gate) + up_total * my_rows(w_up), axis=1),
    ])
    gains = gains + exchange(gains)
    gains = gains / lax.dynamic_slice_in_dim(jnp.stack([attn_gain, ffn_gain]), start, rows, 1).astype(f32)

    ends = [group_cols, group_cols + HEAD]
    by_slot = jnp.moveaxis(attn_total[:, :joint_cols].reshape(rows, slots, -1), 1, 0)
    return (
        tokens_out.T[None],
        grad_in.T[None],
        by_slot[:, :, : ends[0]],
        by_slot[:, :, ends[0] : ends[1]],
        by_slot[:, :, ends[1] :],
        attn_total[:, joint_cols:].T.reshape(slots, group_cols, rows),
        gate_total,
        up_total,
        down_total.T,
        gains[0],
        gains[1],
    )


def solution(mesh):
    in_specs = (
        P("dp", None, None),
        P("dp", None),
        P(),
        P(),
        P(),
        P(),
        P(),
        P(),
        P(None, "mp"),
        P(None, "mp"),
        P("mp", None),
        P(),
        P("dp", None, None),
    )
    out_specs = (
        P("dp", None, None),
        P("dp", None, None),
        P("mp", "dp", None),
        P("mp", "dp", None),
        P("mp", "dp", None),
        P("mp", None, "dp"),
        P("dp", "mp"),
        P("dp", "mp"),
        P("mp", "dp"),
        P("dp"),
        P("dp"),
    )
    return jax.shard_map(
        per_device, mesh=mesh, in_specs=in_specs, out_specs=out_specs, check_vma=False
    )
```

```python
import functools
import math

import jax
import jax.numpy as jnp
import numpy as np
from jax import lax
from jax.experimental import pallas as pl
from jax.experimental.pallas import tpu as pltpu
from jax.sharding import PartitionSpec as P

REPEAT = 2
BLOCK = 256
FFN_BLOCK = 512
LANES = 128
HEAD = 64
GROUP = 3
VROWS = 80
epsilon = 1e-05
masked_value = -1e30
LOG2E = math.log2(math.e)
LN2 = math.log(2.0)
f32 = jnp.float32
bf16 = jnp.bfloat16
NN = (((1,), (0,)), ((), ()))
NT = (((1,), (1,)), ((), ()))
TN = (((0,), (0,)), ((), ()))
MIB = 1024 * 1024


def matmul(a, b, dims=NN):
    return lax.dot_general(a, b, dims, preferred_element_type=f32)


def wide(column, width):
    return jnp.concatenate([column] * (width // LANES), axis=1)


def inverse_rms(values):
    return lax.rsqrt(jnp.mean(values * values, axis=0, keepdims=True) + epsilon)


def normalise(values, gain, inverse_out):
    inverse = inverse_rms(values)
    inverse_out[...] = inverse
    return (values * inverse * wide(gain, values.shape[1])).astype(bf16)


def norm_back(normed, inverse, gain, grad_normed):
    normed = normed.astype(f32)
    inner_mean = jnp.mean(grad_normed * normed, axis=0, keepdims=True)
    width = normed.shape[1]
    return inverse * (grad_normed * wide(gain, width) - normed * wide(1.0 / gain, width) * inner_mean)


def joined_sum(own_ref, other_ref):
    return own_ref[...].astype(f32) + other_ref[...].astype(f32)


def three_parts(value):
    high = value.astype(bf16).astype(f32)
    rest = value - high
    middle = rest.astype(bf16).astype(f32)
    return high, middle, rest - middle


def part_rows(value, first):
    row = lax.broadcasted_iota(jnp.int32, (8, value.shape[1]), 0)
    out = jnp.zeros((8, value.shape[1]), f32)
    for number, part in enumerate(three_parts(value)):
        out = jnp.where(row == first + number, part, out)
    return out


def causal_bias(heads):
    key = lax.broadcasted_iota(jnp.int32, (BLOCK, heads * BLOCK), 0)
    query = lax.broadcasted_iota(jnp.int32, (BLOCK, heads * BLOCK), 1) % BLOCK
    return jnp.where(key <= query, 0.0, masked_value)


def reaches(segments, step, back):
    last = jnp.maximum((step - back + 1) * BLOCK - 1, 0)
    return (step >= back) & (segments[last] == segments[step * BLOCK])


def block_at(index):
    return pl.ds(pl.multiple_of(index * BLOCK, BLOCK), BLOCK)


def turn(upper, lower, cosine, sine):
    return upper * cosine - lower * sine, lower * cosine + upper * sine


def attention_forward(joined, slots, heads, segments, *refs):
    refs = list(refs)
    hidden = refs.pop(0)[...].astype(f32)
    if joined:
        hidden = hidden + joined_sum(refs.pop(0), refs.pop(0))
    gain_ref, wqkv_ref, wout_ref, cos_ref, sin_ref, segment_ref = refs[:6]
    refs = refs[6:]
    if joined:
        refs.pop(0)[...] = hidden
    (normed_out, inverse_out, query_out, key_out, turned_key_out, value_out, attended_out, partial_out,
     turned_value, tri_ref) = refs
    step = pl.program_id(0)
    here = block_at(step)

    @pl.when(step == 0)
    def _():
        tri_ref[...] = causal_bias(heads)

    normed = normalise(hidden, gain_ref[...], inverse_out)
    normed_out[...] = normed
    projected = matmul(wqkv_ref[...], normed)
    cosine, sine = cos_ref[...], sin_ref[...]
    half = HEAD // 2

    same = lax.broadcasted_iota(jnp.int32, (8, BLOCK), 0) == segment_ref[...]
    query_rows = jnp.where(same, 1.0, 0.0)
    key_rows = jnp.where(same, 0.0, masked_value)
    row = lax.broadcasted_iota(jnp.int32, (8, BLOCK), 0)
    minus_rows = jnp.where(row < 3, -1.0, 0.0)
    scale = LOG2E / math.sqrt(HEAD)
    query_fill = jnp.concatenate(
        [query_rows, jnp.zeros((LANES - HEAD - 8, BLOCK), f32)], axis=0
    ).astype(bf16)

    for s in range(slots):
        for j in range(heads + 2):
            first = (s * (heads + 2) + j) * HEAD
            piece = projected[first : first + HEAD]
            if j > heads:
                value = jnp.concatenate([piece, jnp.ones((LANES - HEAD, BLOCK), f32)], axis=0)
                value_out[here, s * LANES : (s + 1) * LANES] = value.T.astype(bf16)
                turned_value[s * VROWS : (s + 1) * VROWS, here] = value[:VROWS].astype(bf16)
                continue
            upper, lower = turn(piece[:half], piece[half:], cosine, sine)
            if j < heads:
                lanes = slice(j * BLOCK, (j + 1) * BLOCK)
                query_out[0, s, :HEAD, lanes] = jnp.concatenate(
                    [upper * scale, lower * scale], axis=0
                ).astype(bf16)
                query_out[0, s, HEAD:, lanes] = query_fill
            else:
                turned_key_out[s * HEAD : (s + 1) * HEAD, :] = jnp.concatenate(
                    [upper, lower], axis=0
                ).astype(bf16)
                whole = jnp.concatenate(
                    [upper, lower, key_rows, minus_rows, jnp.zeros((LANES - HEAD - 16, BLOCK), f32)],
                    axis=0,
                )
                key_out[here, s * LANES : (s + 1) * LANES] = whole.T.astype(bf16)

    query_rows = jnp.concatenate([query_rows] * heads, axis=1)

    def attend(blocks):
        width = blocks * BLOCK
        keys = pl.ds(pl.multiple_of((step + 1 - blocks) * BLOCK, BLOCK), width)
        scores = [
            matmul(key_out[keys, s * LANES : (s + 1) * LANES], query_out[0, s]) for s in range(slots)
        ]
        tops, weights = [], []
        for score in scores:
            last = score[width - BLOCK :] + tri_ref[...]
            if blocks > 1:
                score = jnp.concatenate([score[: width - BLOCK], last], axis=0)
            else:
                score = last
            tops.append(jnp.max(score, axis=0, keepdims=True))
            weights.append(jnp.exp2(score - tops[-1]).astype(bf16))
        summed = [
            matmul(turned_value[s * VROWS : (s + 1) * VROWS, keys], weights[s]) for s in range(slots)
        ]
        for s in range(slots):
            weight_sum = summed[s][HEAD : HEAD + 1]
            out = (summed[s][:HEAD] * (1.0 / weight_sum)).astype(bf16)
            for j in range(heads):
                first = (s * heads + j) * HEAD
                attended_out[first : first + HEAD, :] = out[:, j * BLOCK : (j + 1) * BLOCK]
            query_out[0, s, HEAD : HEAD + 16, :] = jnp.concatenate(
                [query_rows, part_rows(tops[s] + jnp.log2(weight_sum), 0)], axis=0
            ).astype(bf16)

    one = reaches(segments, step, 1)
    two = reaches(segments, step, 2)
    pl.when(jnp.logical_not(one))(functools.partial(attend, 1))
    pl.when(one & jnp.logical_not(two))(functools.partial(attend, 2))
    pl.when(two)(functools.partial(attend, 3))
    partial_out[...] = matmul(wout_ref[...], attended_out[...], TN).astype(bf16)


def chunks(width):
    return [slice(start, start + 256) for start in range(0, width, 256)]


def cost(flops, *arrays):
    size = sum(math.prod(a.shape) * a.dtype.itemsize for a in arrays)
    return pl.CostEstimate(flops=int(flops), bytes_accessed=size, transcendentals=0)


def token_spec(rows, width=BLOCK):
    return pl.BlockSpec((rows, width), lambda i, *_: (0, i))


def unit_shape(units, length):
    return shape_of((length // FFN_BLOCK, units, FFN_BLOCK), bf16)


def unit_spec(units):
    return pl.BlockSpec((1, units, FFN_BLOCK), lambda i: (i, 0, 0))


def full_spec(shape):
    return pl.BlockSpec(
        shape, lambda *_: (0,) * len(shape), pipeline_mode=pl.Buffered(buffer_count=1)
    )


def out_full_spec(shape):
    return pl.BlockSpec(shape, lambda *_: (0,) * len(shape))


shape_of = pltpu.HBM
anywhere = jax.ShapeDtypeStruct


def in_hbm(*arrays):
    return tuple(pltpu.with_memory_space_constraint(array, pltpu.HBM) for array in arrays)


def call_attention_forward(segments, parts, gain, wqkv, wout, cosine, sine, slots, heads):
    features, length = parts[0].shape
    joined = len(parts) == 3
    total = slots * heads
    big = shape_of((features, length), bf16)
    outs = [
        (big, token_spec(features)),
        (shape_of((1, length), f32), token_spec(1)),
        (
            shape_of((length // BLOCK, slots, LANES, heads * BLOCK), bf16),
            pl.BlockSpec((1, slots, LANES, heads * BLOCK), lambda i, *_: (i, 0, 0, 0)),
        ),
        (shape_of((length, slots * LANES), bf16), out_full_spec((length, slots * LANES))),
        (shape_of((slots * HEAD, length), bf16), token_spec(slots * HEAD)),
        (shape_of((length, slots * LANES), bf16), out_full_spec((length, slots * LANES))),
        (shape_of((total * HEAD, length), bf16), token_spec(total * HEAD)),
        (anywhere((features, length), bf16), token_spec(features)),
    ]
    if joined:
        outs.insert(0, (shape_of((features, length), f32), token_spec(features)))
    return pl.pallas_call(
        functools.partial(attention_forward, joined, slots, heads),
        grid_spec=pltpu.PrefetchScalarGridSpec(
            num_scalar_prefetch=1,
            grid=(length // BLOCK,),
            in_specs=[token_spec(features)] * len(parts)
            + [full_spec(a.shape) for a in (gain, wqkv, wout)]
            + [token_spec(HEAD // 2)] * 2
            + [token_spec(1)],
            out_specs=[spec for _, spec in outs],
            scratch_shapes=[
                pltpu.VMEM((slots * VROWS, length), bf16),
                pltpu.VMEM((BLOCK, heads * BLOCK), f32),
            ],
        ),
        out_shape=[shape for shape, _ in outs],
        compiler_params=pltpu.CompilerParams(vmem_limit_bytes=32 * MIB),
        cost_estimate=cost(2 * length * features * (wqkv.shape[0] + wout.shape[0]) + 12e9, *parts),
        name="attention_forward",
    )(segments, *in_hbm(parts[0]), *parts[1:], gain, wqkv, wout, cosine, sine, segments[None, :])


def ffn_forward(hidden_ref, own_ref, other_ref, gain_ref, gate_ref, up_ref, down_ref,
                middle_out, normed_out, inverse_out, gate_out, lift_out, inner_out, partial_out):
    middle = hidden_ref[...].astype(f32) + joined_sum(own_ref, other_ref)
    middle_out[...] = middle
    normed = normalise(middle, gain_ref[...], inverse_out)
    normed_out[...] = normed
    for chunk in chunks(gate_ref.shape[1]):
        gate = matmul(gate_ref[:, chunk], normed, TN)
        lift = matmul(up_ref[:, chunk], normed, TN)
        gate_out[0, chunk, :] = gate.astype(bf16)
        lift_out[0, chunk, :] = lift.astype(bf16)
        inner_out[0, chunk, :] = (gate * jax.nn.sigmoid(gate) * lift).astype(bf16)
    partial_out[...] = matmul(down_ref[...], inner_out[0]).astype(bf16)


def call_ffn_forward(hidden, own, other, gain, w_gate, w_up, w_down):
    features, length = hidden.shape
    units = w_gate.shape[1]
    spec = functools.partial(token_spec, width=FFN_BLOCK)
    return pl.pallas_call(
        ffn_forward,
        grid=(length // FFN_BLOCK,),
        in_specs=[spec(features)] * 3 + [full_spec(a.shape) for a in (gain, w_gate, w_up, w_down)],
        out_specs=[spec(features)] * 2 + [spec(1)] + [unit_spec(units)] * 3 + [spec(features)],
        out_shape=[
            shape_of((features, length), f32), shape_of((features, length), bf16),
            shape_of((1, length), f32), *[unit_shape(units, length)] * 3,
            anywhere((features, length), bf16),
        ],
        compiler_params=pltpu.CompilerParams(vmem_limit_bytes=40 * MIB),
        cost_estimate=cost(6 * length * features * units, hidden),
        name="ffn_forward",
    )(*in_hbm(hidden), own, other, gain, w_gate, w_up, w_down)


def ffn_backward(joined, grad_ref, *refs):
    grad = grad_ref[...]
    if joined:
        normed_ref, inverse_ref, own_ref, other_ref, gain_ref = refs[:5]
        refs = refs[5:]
        back = norm_back(normed_ref[...], inverse_ref[...], gain_ref[...], joined_sum(own_ref, other_ref))
        grad = (grad.astype(f32) + back).astype(bf16)
    gate_in, lift_in, gate_ref, up_ref, down_ref = refs[:5]
    refs = refs[5:]
    if joined:
        refs[0][...] = grad
        refs = refs[1:]
    grad_gate_out, grad_lift_out, partial_out = refs
    for chunk in chunks(gate_ref.shape[1]):
        grad_inner = matmul(down_ref[:, chunk], grad, TN)
        gate = gate_in[0, chunk, :].astype(f32)
        lift = lift_in[0, chunk, :].astype(f32)
        sigmoid = jax.nn.sigmoid(gate)
        grad_gate = grad_inner * lift * sigmoid * (1.0 + gate * (1.0 - sigmoid))
        grad_gate_out[0, chunk, :] = grad_gate.astype(bf16)
        grad_lift_out[0, chunk, :] = (grad_inner * gate * sigmoid).astype(bf16)
    partial = matmul(gate_ref[...], grad_gate_out[0]) + matmul(up_ref[...], grad_lift_out[0])
    partial_out[...] = partial.astype(bf16)


def call_ffn_backward(grad, joint, gate, lift, w_gate, w_up, w_down):
    features, length = grad.shape
    units = w_gate.shape[1]
    spec = functools.partial(token_spec, width=FFN_BLOCK)
    joint_specs, extra = [], []
    if joint:
        normed, inverse, own, other, gain = joint
        joint = (*in_hbm(normed), inverse, own, other, gain)
        joint_specs = [spec(features), spec(1), spec(features), spec(features), full_spec(gain.shape)]
        extra = [(shape_of((features, length), bf16), spec(features))]
    outs = extra + [(unit_shape(units, length), unit_spec(units))] * 2
    outs.append((anywhere((features, length), bf16), spec(features)))
    return pl.pallas_call(
        functools.partial(ffn_backward, bool(joint)),
        grid=(length // FFN_BLOCK,),
        in_specs=[spec(features)] + joint_specs + [unit_spec(units)] * 2
        + [full_spec(a.shape) for a in (w_gate, w_up, w_down)],
        out_specs=[spec for _, spec in outs],
        out_shape=[shape for shape, _ in outs],
        compiler_params=pltpu.CompilerParams(vmem_limit_bytes=40 * MIB),
        cost_estimate=cost(6 * length * features * units, grad),
        name="ffn_backward",
    )(*in_hbm(grad), *joint, *in_hbm(gate, lift), w_gate, w_up, w_down)


def attention_backward(slots, heads, segments, grad_ref, own_ref, other_ref, normed_ref, inverse_ref,
                       gain_ref, wout_ref, wqkv_ref, attended_ref, query_ref, key_ref, turned_key_ref,
                       value_ref, cos_ref, sin_ref,
                       attn_grad_out, projected_out, partial_out,
                       key_total, value_total, query_total, grad_heads, tri_ref):
    step = pl.num_programs(0) - 1 - pl.program_id(0)
    half = HEAD // 2

    @pl.when(pl.program_id(0) == 0)
    def _():
        key_total[...] = jnp.zeros_like(key_total)
        value_total[...] = jnp.zeros_like(value_total)
        tri_ref[...] = causal_bias(heads)

    back = norm_back(normed_ref[...], inverse_ref[...], gain_ref[...], joined_sum(own_ref, other_ref))
    attn_grad = (grad_ref[...].astype(f32) + back).astype(bf16)
    attn_grad_out[...] = attn_grad
    grad_attended = matmul(wout_ref[...], attn_grad).astype(bf16)
    zeros = jnp.zeros((LANES - HEAD - 8, BLOCK), f32)
    for s in range(slots):
        for j in range(heads):
            first = (s * heads + j) * HEAD
            mine = grad_attended[first : first + HEAD]
            out = attended_ref[first : first + HEAD, :]
            delta = jnp.sum(mine.astype(f32) * out.astype(f32), axis=0, keepdims=True)
            lanes = slice(j * BLOCK, (j + 1) * BLOCK)
            grad_heads[s, :HEAD, lanes] = mine
            grad_heads[s, HEAD:, lanes] = jnp.concatenate(
                [part_rows(-delta, 0), zeros], axis=0
            ).astype(bf16)

    def visit(back):
        keys = block_at(step - back)
        columns = [slice(s * LANES, (s + 1) * LANES) for s in range(slots)]
        features = [slice(s * HEAD, (s + 1) * HEAD) for s in range(slots)]
        scores = [matmul(key_ref[keys, columns[s]], query_ref[0, s]) for s in range(slots)]
        grad_weights = [matmul(value_ref[keys, columns[s]], grad_heads[s]) for s in range(slots)]
        weights, grad_scores = [], []
        for s in range(slots):
            score = scores[s] + tri_ref[...] if back == 0 else scores[s]
            weight = jnp.exp2(score)
            weights.append(weight.astype(bf16))
            grad_scores.append((weight * grad_weights[s]).astype(bf16))
        for s in range(slots):
            value_total[features[s], keys] += matmul(grad_heads[s, :HEAD, :], weights[s], NT)
            key_total[features[s], keys] += matmul(query_ref[0, s, :HEAD, :], grad_scores[s], NT)
            update = matmul(turned_key_ref[features[s], keys], grad_scores[s])
            if back == 0:
                query_total[s] = update
            else:
                query_total[s] += update

    visit(0)
    for back in (1, 2):
        pl.when(reaches(segments, step, back))(functools.partial(visit, back))

    cosine, sine = cos_ref[...], sin_ref[...]
    here = block_at(step)
    for s in range(slots):
        for j in range(heads + 2):
            if j < heads:
                piece = query_total[s, :, j * BLOCK : (j + 1) * BLOCK] * (1.0 / math.sqrt(HEAD))
            elif j == heads:
                piece = key_total[s * HEAD : (s + 1) * HEAD, here] * LN2
            else:
                piece = value_total[s * HEAD : (s + 1) * HEAD, here]
            if j <= heads:
                upper, lower = turn(piece[:half], piece[half:], cosine, -sine)
                piece = jnp.concatenate([upper, lower], axis=0)
            first = (s * (heads + 2) + j) * HEAD
            projected_out[first : first + HEAD, :] = piece.astype(bf16)
    partial_out[...] = matmul(wqkv_ref[...], projected_out[...], TN).astype(bf16)


def call_attention_backward(segments, grad, own, other, normed, inverse, gain, wout, wqkv, attended, query,
                            key, turned_key, value, cosine, sine):
    features, length = grad.shape
    count = length // BLOCK
    slots, wide_heads = query.shape[1], query.shape[3]
    heads = wide_heads // BLOCK

    def spec(rows):
        return pl.BlockSpec((rows, BLOCK), lambda i, *_: (0, count - 1 - i))

    return pl.pallas_call(
        functools.partial(attention_backward, slots, heads),
        grid_spec=pltpu.PrefetchScalarGridSpec(
            num_scalar_prefetch=1,
            grid=(count,),
            in_specs=[spec(features)] * 4 + [spec(1)]
            + [full_spec(a.shape) for a in (gain, wout, wqkv)]
            + [spec(attended.shape[0])]
            + [pl.BlockSpec((1, slots, LANES, wide_heads), lambda i, *_: (count - 1 - i, 0, 0, 0))]
            + [full_spec(a.shape) for a in (key, turned_key, value)]
            + [spec(HEAD // 2)] * 2,
            out_specs=[spec(features), spec(wqkv.shape[0]), spec(features)],
            scratch_shapes=[
                pltpu.VMEM((slots * HEAD, length), f32),
                pltpu.VMEM((slots * HEAD, length), f32),
                pltpu.VMEM((slots, HEAD, wide_heads), f32),
                pltpu.VMEM((slots, LANES, wide_heads), bf16),
                pltpu.VMEM((BLOCK, wide_heads), f32),
            ],
        ),
        out_shape=[
            shape_of((features, length), bf16), shape_of((wqkv.shape[0], length), bf16),
            anywhere((features, length), bf16),
        ],
        compiler_params=pltpu.CompilerParams(vmem_limit_bytes=30 * MIB),
        cost_estimate=cost(2 * length * features * (wqkv.shape[0] + wout.shape[0]) + slots * 8e9, grad),
        name="attention_backward",
    )(segments, *in_hbm(grad), own, other, *in_hbm(normed), inverse, gain, wout, wqkv,
      *in_hbm(attended, query), key, turned_key, value, cosine, sine)


def shard_rows(total, out_ref, order, rows, mine, first=0):
    total = total.astype(bf16)
    columns = slice(first, first + total.shape[1])
    half = len(order) // 2
    for place, shard in enumerate(order):
        side = mine if place < half else 1 - mine
        out_ref[side, place % half, :rows, columns] = total[shard * rows : (shard + 1) * rows]
        if out_ref.shape[2] > rows:
            out_ref[side, place % half, rows:, columns] = jnp.zeros(
                (out_ref.shape[2] - rows, total.shape[1]), bf16
            )


def begin_sending(staged, kept, sent, kept_signal, sent_signal):
    copies = [
        pltpu.make_async_copy(staged.at[1], sent, sent_signal),
        pltpu.make_async_copy(staged.at[0], kept, kept_signal),
    ]
    begin(copies)
    return copies


def fetches(pairs, arrived):
    groups, count = [], 0
    for sources, target in pairs:
        parts = []
        for source in sources:
            parts += [source] if len(source.shape) == 2 else [source.at[i] for i in range(source.shape[0])]
        first, group = 0, []
        for part in parts:
            lanes = target.at[:, pl.ds(first, part.shape[1])]
            group.append(pltpu.make_async_copy(part, lanes, arrived.at[count]))
            first += part.shape[1]
            count += 1
        groups.append(group)
    return groups


def begin(copies):
    for copy in copies:
        copy.start()


def finish(copies):
    for copy in copies:
        copy.wait()


def halves_product(left, right, copies):
    length = left.shape[1] // 2
    finish(copies[:2])
    total = matmul(left[:, :length], right[:, :length], NT)
    finish(copies[2:])
    return total + matmul(left[:, length:], right[:, length:], NT)


def ffn_weight_grad(orders, rows, bits, *refs):
    sources, outs = refs[:10], refs[10:16]
    buffers, staged, arrived, left = refs[16:21], refs[21], refs[22], refs[23]
    copies = fetches([(sources[2 * i : 2 * i + 2], buffers[i]) for i in range(5)], arrived)
    normed, gates, lifts, grads, inners = buffers
    begin(copies[0] + copies[1])
    outgoing = []

    def write(number, product):
        slot = number % 2
        if number >= 2:
            finish(outgoing[number - 2])
        for chunk in chunks(staged.shape[4]):
            shard_rows(product(chunk), staged.at[slot], orders[number], rows, bits[number], chunk.start)
        outgoing.append(
            begin_sending(
                staged.at[slot], outs[2 * number], outs[2 * number + 1],
                left.at[2 * number], left.at[2 * number + 1],
            )
        )

    finish(copies[0] + copies[1])
    begin(copies[2] + copies[3] + copies[4])
    write(0, lambda chunk: matmul(normed[...], gates[chunk, :], NT))
    finish(copies[2])
    write(1, lambda chunk: matmul(normed[...], lifts[chunk, :], NT))
    finish(copies[3] + copies[4])
    write(2, lambda chunk: matmul(grads[...], inners[chunk, :], NT))
    for pair in outgoing[1:]:
        finish(pair)


def call_weight_grad(kernel, name, bits, pairs, orders, columns, stages, flops):
    features, length = pairs[0][0].shape
    arrivals = sum(len(pair) * (1 if pair[0].ndim == 2 else pair[0].shape[0]) for pair in pairs)
    size = len(orders[0])
    rows = features // size
    padded = -(-rows // 16) * 16
    out = (size // 2, padded, columns)
    outs = pl.pallas_call(
        functools.partial(kernel, orders, rows),
        grid_spec=pltpu.PrefetchScalarGridSpec(
            num_scalar_prefetch=1,
            grid=(1,),
            in_specs=[pl.BlockSpec(memory_space=pl.ANY)] * (2 * len(pairs)),
            out_specs=[pl.BlockSpec(memory_space=pl.ANY)] * (2 * len(orders)),
            scratch_shapes=[pltpu.VMEM((pair[0].shape[-2], 2 * length), bf16) for pair in pairs]
            + [pltpu.VMEM((stages, 2) + out, bf16)]
            + [pltpu.SemaphoreType.DMA((arrivals,)), pltpu.SemaphoreType.DMA((2 * len(orders),))],
        ),
        out_shape=[shape_of(out, bf16)] * (2 * len(orders)),
        compiler_params=pltpu.CompilerParams(vmem_limit_bytes=52 * MIB),
        cost_estimate=cost(flops, *(array for pair in pairs for array in pair)),
        name=name,
    )(bits, *in_hbm(*(array for pair in pairs for array in pair)))
    return list(zip(outs[::2], outs[1::2]))


def call_ffn_weight_grad(bits, normed, grads, rights, orders):
    units = rights[0][0].shape[1]
    pairs = (normed, rights[0], rights[1], grads, rights[2])
    flops = 12 * normed[0].shape[0] * normed[0].shape[1] * units
    return call_weight_grad(ffn_weight_grad, "ffn_weight_grad", bits, pairs, orders, units, 2, flops)


def attention_weight_grad(orders, rows, bits, *refs):
    sources, outs = refs[:8], refs[8:14]
    buffers, staged, arrived, left = refs[14:18], refs[18], refs[19], refs[20]
    copies = fetches([(sources[2 * i : 2 * i + 2], buffers[i]) for i in range(4)], arrived)
    begin(copies[0] + copies[1])
    outgoing = []
    width = staged.shape[4]

    def write(number, pieces):
        column = 0
        for piece in pieces:
            shard_rows(piece, staged.at[number], orders[number], rows, bits[number], column)
            column += piece.shape[1]
        outgoing.extend(
            begin_sending(
                staged.at[number], outs[2 * number], outs[2 * number + 1],
                left.at[2 * number], left.at[2 * number + 1],
            )
        )

    def project(start, stop):
        return matmul(buffers[0][...], buffers[1][start:stop, :], NT)

    def outward(start, stop):
        return matmul(buffers[2][...], buffers[3][start:stop, :], NT)

    columns, most = buffers[1].shape[0], buffers[3].shape[0]
    rest = 2 * width - columns
    finish(copies[0] + copies[1])
    begin(copies[2] + copies[3])
    write(0, [project(start, start + 256) for start in range(0, width, 256)])
    body, tail = project(width, width + 256), project(width + 256, columns)
    finish(copies[2] + copies[3])
    write(1, [body, jnp.concatenate([tail, outward(0, rest)], axis=1)])
    write(2, [outward(start, min(start + 256, most)) for start in range(rest, most, 256)])
    finish(outgoing)


def call_attention_weight_grad(bits, above, below, orders):
    columns = above[1].shape[0] + above[3].shape[0]
    flops = 4 * above[0].shape[0] * above[0].shape[1] * columns
    return call_weight_grad(
        attention_weight_grad, "attention_weight_grad", bits, list(zip(above, below)), orders,
        columns // len(orders), len(orders), flops,
    )


def block_grad(grad_ref, normed_ref, inverse_ref, own_ref, other_ref, gain_ref, out_ref):
    back = norm_back(normed_ref[...], inverse_ref[...], gain_ref[...], joined_sum(own_ref, other_ref))
    out_ref[...] = (grad_ref[...].astype(f32) + back).astype(out_ref.dtype)


def call_block_grad(grad, normed, inverse, own, other, gain, kind):
    features, length = grad.shape
    spec = functools.partial(token_spec, width=FFN_BLOCK)
    return pl.pallas_call(
        block_grad,
        grid=(length // FFN_BLOCK,),
        in_specs=[spec(features)] * 2 + [spec(1)] + [spec(features)] * 2 + [full_spec(gain.shape)],
        out_specs=spec(features),
        out_shape=shape_of((features, length), kind),
        compiler_params=pltpu.CompilerParams(vmem_limit_bytes=32 * MIB),
        cost_estimate=cost(0, grad, normed, own, other),
        name="block_grad",
    )(*in_hbm(grad, normed), inverse, own, other, gain)


def gather_groups(owner, device, *refs):
    sources, (wqkv_out, wout_out), arrived = refs[:4], refs[4:6], refs[6]
    heights = [source.shape[1] for source in sources]
    joint = sum(heights[:3])
    slots = wqkv_out.shape[0] // joint
    for action in ("start", "wait"):
        for slot in range(slots):
            group, held = group_of(slot, owner, device)
            first = slot * joint
            for place, (source, height) in enumerate(zip(sources, heights)):
                if place < 3:
                    target = wqkv_out.at[pl.ds(first, height)]
                    first += height
                else:
                    target = wout_out.at[pl.ds(slot * height, height)]
                copy = pltpu.make_async_copy(source.at[group], target, arrived.at[4 * slot + place])

                def empty(target=target):
                    target[...] = jnp.zeros(target.shape, bf16)

                pl.when(held)(getattr(copy, action))
                if action == "start":
                    pl.when(jnp.logical_not(held))(empty)


def group_of(slot, owner, device):
    found, count = 0, 0
    for group in range(owner.shape[0]):
        mine = owner[group] == device[0]
        found = jnp.where(mine & (count == slot), group, found)
        count = count + jnp.where(mine, 1, 0)
    return found, count > slot


def call_gather_groups(owner, device, w_query, w_key, w_value, w_out, slots):
    features = w_query.shape[2]
    arrays = (w_query, w_key, w_value, w_out)
    joint = slots * (w_query.shape[1] + w_key.shape[1] + w_value.shape[1])
    outs = [(joint, features), (slots * w_out.shape[1], features)]
    return pl.pallas_call(
        gather_groups,
        grid_spec=pltpu.PrefetchScalarGridSpec(
            num_scalar_prefetch=2,
            grid=(1,),
            in_specs=[pl.BlockSpec(memory_space=pl.ANY)] * 4,
            out_specs=[out_full_spec(o) for o in outs],
            scratch_shapes=[pltpu.SemaphoreType.DMA((4 * slots,))],
        ),
        out_shape=[shape_of(o, bf16) for o in outs],
        name="gather_groups",
    )(owner, device, *in_hbm(*arrays))


def rotary_tables(length):
    position = np.arange(length, dtype=np.float64)[None, :]
    column = np.arange(HEAD // 2, dtype=np.float64)[:, None]
    angles = position * np.exp(column * (-2.0 * math.log(10000.0) / HEAD))
    return jnp.asarray(np.cos(angles), f32), jnp.asarray(np.sin(angles), f32)


def exchange(own):
    return lax.ppermute(own, "mp", [(0, 1), (1, 0)])


def stage_plans(bit_count):
    bits = list(range(bit_count))
    turned = [bits[:3], bits[1:3] + bits[:1], bits[2:3] + bits[:2]]
    return [[[bit] for bit in first + bits[3:]] for first in turned]


def shard_order(plan):
    bits = [bit for stage in plan for bit in stage]
    order = []
    for place in range(1 << len(bits)):
        shard = 0
        for rank, bit in enumerate(bits):
            if place >> (len(bits) - 1 - rank) & 1:
                shard |= 1 << bit
        order.append(shard)
    return order


def after(value, *others):
    return lax.optimization_barrier((value, others))[0]


class Stream:
    def __init__(self, parts, widths, count, stages):
        self.parts, self.widths, self.count, self.stages = parts, widths, count, list(stages)

    @classmethod
    def started(cls, kept, sent, plan):
        stream = cls([[(kept, 0, 0)]], [kept.shape[2]], kept.shape[0], plan)
        stream.transfer(sent, stream.stages.pop(0)[0])
        return stream

    def transfer(self, sent, bit):
        size = lax.axis_size("dp")
        received = lax.ppermute(sent, "dp", [(i, i ^ (1 << bit)) for i in range(size)])
        column = 0
        for terms, width in zip(self.parts, self.widths):
            terms.append((received, 0, column))
            column += width
        self.sent = sent

    def hold(self, *others):
        received = after(self.parts[0][-1][0], *others)
        for terms in self.parts:
            terms[-1] = (received, *terms[-1][1:])
        return self

    def sums(self, first, count):
        out = []
        for terms, width in zip(self.parts, self.widths):
            pieces = [
                lax.dynamic_slice(array, (start + first, 0, column), (count, array.shape[1], width))
                for array, start, column in terms
            ]
            out.append(sum(piece.astype(f32) for piece in pieces))
        return out

    def send(self, eager=False):
        bit = self.stages.pop(0)[0]
        mine = (lax.axis_index("dp") >> bit) & 1
        self.count //= 2
        sent = [piece.astype(bf16) for piece in self.sums((1 - mine) * self.count, self.count)]
        if eager:
            kept = self.sums(mine * self.count, self.count)
            self.parts = [[(piece.astype(bf16), 0, 0)] for piece in kept]
        else:
            self.parts = [
                [(array, start + mine * self.count, column) for array, start, column in terms]
                for terms in self.parts
            ]
        self.transfer(sent[0] if len(sent) == 1 else jnp.concatenate(sent, axis=2), bit)
        return self.sent

    def totals(self):
        return [piece[0] for piece in self.sums(0, 1)]


def joined(streams):
    return Stream(
        [terms for stream in streams for terms in stream.parts],
        [width for stream in streams for width in stream.widths],
        streams[0].count,
        streams[0].stages,
    )


def per_device(
    tokens_in,
    segment_ids,
    kv_owner,
    w_query,
    w_key,
    w_value,
    w_out,
    attn_gain,
    w_gate,
    w_up,
    w_down,
    ffn_gain,
    cotangent,
):
    features = tokens_in.shape[2]
    length = tokens_in.shape[1]
    group_cols = w_query.shape[2]
    heads = group_cols // HEAD
    slots = (kv_owner.shape[0] + lax.axis_size("mp") - 1) // lax.axis_size("mp")
    size = lax.axis_size("dp")
    rows = features // size

    device = lax.axis_index("mp").astype(jnp.int32)[None]
    wqkv, wout = call_gather_groups(
        kv_owner, device, *(jnp.swapaxes(w, 1, 2) for w in (w_query, w_key, w_value)), w_out, slots
    )
    w_down = w_down.T
    segments = segment_ids[0]
    cosine, sine = rotary_tables(length)
    gain_one, gain_two = (
        jnp.broadcast_to(gain.astype(f32)[:, None], (features, LANES)) for gain in (attn_gain, ffn_gain)
    )

    parts = (tokens_in[0].T,)
    saved = []
    for _ in range(REPEAT):
        outs = list(call_attention_forward(segments, parts, gain_one, wqkv, wout, cosine, sine, slots, heads))
        hidden = outs.pop(0) if len(parts) == 3 else parts[0]
        normed, inverse, query, key, turned_key, value, attended, partial = outs
        middle, normed_two, inverse_two, gate, lift, inner, partial_two = call_ffn_forward(
            hidden, partial, exchange(partial), gain_two, w_gate, w_up, w_down
        )
        parts = (middle, partial_two, exchange(partial_two))
        saved.append((
            normed, inverse, query, key, turned_key, value, attended, normed_two, inverse_two, gate, lift, inner,
        ))

    plans = stage_plans(size.bit_length() - 1)
    orders = [shard_order(plan) for plan in plans]
    bits = jnp.stack([(lax.axis_index("dp") >> plan[0][0]) & 1 for plan in plans]).astype(jnp.int32)
    joint = ()
    grad = cotangent[0].T
    for r in reversed(range(REPEAT)):
        (normed, inverse, query, key, turned_key, value, attended,
         normed_two, inverse_two, gate, lift, inner) = saved[r]
        last = r == 0
        outs = list(call_ffn_backward(grad, joint, gate, lift, w_gate, w_up, w_down))
        if joint:
            grad = outs.pop(0)
        ffn_grad = grad
        grad_gate, grad_lift, partial = outs
        other = exchange(partial)
        if not last:
            parts = after(parts, partial)
            tokens_out = (parts[0] + (parts[1].astype(f32) + parts[2].astype(f32))).astype(bf16)
            grad = after(grad, tokens_out)
        else:
            payloads = call_ffn_weight_grad(
                bits, (above["normed_two"], normed_two), (above["ffn_grad"], ffn_grad),
                ((above["grad_gate"], grad_gate), (above["grad_lift"], grad_lift), (above["inner"], inner)),
                orders,
            )
            track_a, track_b, down = (
                Stream.started(*payload, plan) for payload, plan in zip(payloads, plans)
            )
            partial = after(partial, payloads)
        grad, projected, partial_two = call_attention_backward(
            segments, grad, partial, other, normed_two, inverse_two, gain_two, wout, wqkv, attended, query,
            key, turned_key, value, cosine, sine,
        )
        other_two = exchange(partial_two)
        if not last:
            above = dict(
                ffn_grad=ffn_grad, inner=inner, normed_two=normed_two, grad_lift=grad_lift,
                grad_gate=grad_gate, attention=(normed, projected, grad, attended),
            )
        joint = (normed, inverse, partial_two, other_two, gain_one)
    ffn = (track_a, track_b, down)
    sent = [stream.hold(projected).send() for stream in ffn]
    payloads = call_attention_weight_grad(
        bits, above["attention"], (normed, after(projected, sent), grad, attended), orders
    )
    tracks = [Stream.started(*payload, plan) for payload, plan in zip(payloads, plans)]
    for stream in ffn:
        stream.hold(payloads, other_two)
    sent = [stream.send() for stream in (track_a, track_b)]
    grad_in = call_block_grad(after(grad, sent, payloads), *joint, f32)
    both = joined([stream.hold(grad_in) for stream in (track_a, track_b)])
    sent = [both.send(True), down.hold(grad_in).send(True)]
    sent = [stream.hold(sent).send(True) for stream in tracks]
    sent = [down.hold(sent).send(True)]
    while len(tracks[0].stages) > 1:
        sent = [stream.hold(sent).send(True) for stream in tracks]
    attn = joined([stream.hold(sent) for stream in tracks])
    pending = [both, down, attn]
    while any(stream.stages for stream in pending):
        for stream in pending:
            if stream.stages:
                stream.send(True)
    gate_total, up_total = both.totals()
    (down_total,) = down.totals()
    attn_total = jnp.concatenate(attn.totals(), axis=1)[:rows]

    start = lax.axis_index("dp") * rows

    def my_rows(weights):
        return lax.dynamic_slice_in_dim(weights, start, rows, 0).astype(f32)

    gate_total, up_total, down_total = (total[:rows] for total in (gate_total, up_total, down_total))
    wqkv = after(wqkv, grad_in)
    chosen = (jnp.arange(rows)[:, None] + start == jnp.arange(features)[None, :]).astype(bf16)
    wqkv_rows = matmul(chosen, wqkv, NT)
    joint_cols = wqkv.shape[0]
    gains = jnp.stack([
        jnp.sum(attn_total[:, :joint_cols] * wqkv_rows, axis=1),
        jnp.sum(gate_total * my_rows(w_gate) + up_total * my_rows(w_up), axis=1),
    ])
    gains = gains + exchange(gains)
    gains = gains / lax.dynamic_slice_in_dim(jnp.stack([attn_gain, ffn_gain]), start, rows, 1).astype(f32)

    ends = [group_cols, group_cols + HEAD]
    by_slot = jnp.moveaxis(attn_total[:, :joint_cols].reshape(rows, slots, -1), 1, 0)
    return (
        tokens_out.T[None],
        grad_in.T[None],
        by_slot[:, :, : ends[0]],
        by_slot[:, :, ends[0] : ends[1]],
        by_slot[:, :, ends[1] :],
        attn_total[:, joint_cols:].T.reshape(slots, group_cols, rows),
        gate_total,
        up_total,
        down_total.T,
        gains[0],
        gains[1],
    )


def solution(mesh):
    in_specs = (
        P("dp", None, None),
        P("dp", None),
        P(),
        P(),
        P(),
        P(),
        P(),
        P(),
        P(None, "mp"),
        P(None, "mp"),
        P("mp", None),
        P(),
        P("dp", None, None),
    )
    out_specs = (
        P("dp", None, None),
        P("dp", None, None),
        P("mp", "dp", None),
        P("mp", "dp", None),
        P("mp", "dp", None),
        P("mp", None, "dp"),
        P("dp", "mp"),
        P("dp", "mp"),
        P("mp", "dp"),
        P("dp"),
        P("dp"),
    )
    return jax.shard_map(
        per_device, mesh=mesh, in_specs=in_specs, out_specs=out_specs, check_vma=False
    )
```

```python
import functools
import math

import jax
import jax.numpy as jnp
import numpy as np
from jax import lax
from jax.experimental import pallas as pl
from jax.experimental.pallas import tpu as pltpu
from jax.sharding import PartitionSpec as P

REPEAT = 2
BLOCK = 256
FFN_BLOCK = 512
LANES = 128
HEAD = 64
GROUP = 3
VROWS = 80
epsilon = 1e-05
masked_value = -1e30
LOG2E = math.log2(math.e)
LN2 = math.log(2.0)
f32 = jnp.float32
bf16 = jnp.bfloat16
NN = (((1,), (0,)), ((), ()))
NT = (((1,), (1,)), ((), ()))
TN = (((0,), (0,)), ((), ()))
MIB = 1024 * 1024


def matmul(a, b, dims=NN):
    return lax.dot_general(a, b, dims, preferred_element_type=f32)


def wide(column, width):
    return jnp.concatenate([column] * (width // LANES), axis=1)


def inverse_rms(values):
    return lax.rsqrt(jnp.mean(values * values, axis=0, keepdims=True) + epsilon)


def normalise(values, gain, inverse_out):
    inverse = inverse_rms(values)
    inverse_out[...] = inverse
    return (values * inverse * wide(gain, values.shape[1])).astype(bf16)


def norm_back(normed, inverse, gain, grad_normed):
    normed = normed.astype(f32)
    inner_mean = jnp.mean(grad_normed * normed, axis=0, keepdims=True)
    width = normed.shape[1]
    return inverse * (grad_normed * wide(gain, width) - normed * wide(1.0 / gain, width) * inner_mean)


def joined_sum(own_ref, other_ref):
    return own_ref[...].astype(f32) + other_ref[...].astype(f32)


def three_parts(value):
    high = value.astype(bf16).astype(f32)
    rest = value - high
    middle = rest.astype(bf16).astype(f32)
    return high, middle, rest - middle


def part_rows(value, first):
    row = lax.broadcasted_iota(jnp.int32, (8, value.shape[1]), 0)
    out = jnp.zeros((8, value.shape[1]), f32)
    for number, part in enumerate(three_parts(value)):
        out = jnp.where(row == first + number, part, out)
    return out


def causal_bias(heads):
    key = lax.broadcasted_iota(jnp.int32, (BLOCK, heads * BLOCK), 0)
    query = lax.broadcasted_iota(jnp.int32, (BLOCK, heads * BLOCK), 1) % BLOCK
    return jnp.where(key <= query, 0.0, masked_value)


def reaches(segments, step, back):
    last = jnp.maximum((step - back + 1) * BLOCK - 1, 0)
    return (step >= back) & (segments[last] == segments[step * BLOCK])


def block_at(index):
    return pl.ds(pl.multiple_of(index * BLOCK, BLOCK), BLOCK)


def turn(upper, lower, cosine, sine):
    return upper * cosine - lower * sine, lower * cosine + upper * sine


def attention_forward(joined, slots, heads, segments, *refs):
    refs = list(refs)
    hidden = refs.pop(0)[...].astype(f32)
    if joined:
        hidden = hidden + joined_sum(refs.pop(0), refs.pop(0))
    gain_ref, wqkv_ref, wout_ref, cos_ref, sin_ref, segment_ref = refs[:6]
    refs = refs[6:]
    if joined:
        refs.pop(0)[...] = hidden
    (normed_out, inverse_out, query_out, key_out, turned_key_out, value_out, attended_out, partial_out,
     turned_value, tri_ref) = refs
    step = pl.program_id(0)
    here = block_at(step)

    @pl.when(step == 0)
    def _():
        tri_ref[...] = causal_bias(heads)

    normed = normalise(hidden, gain_ref[...], inverse_out)
    normed_out[...] = normed
    projected = matmul(wqkv_ref[...], normed)
    cosine, sine = cos_ref[...], sin_ref[...]
    half = HEAD // 2

    same = lax.broadcasted_iota(jnp.int32, (8, BLOCK), 0) == segment_ref[...]
    query_rows = jnp.where(same, 1.0, 0.0)
    key_rows = jnp.where(same, 0.0, masked_value)
    row = lax.broadcasted_iota(jnp.int32, (8, BLOCK), 0)
    minus_rows = jnp.where(row < 3, -1.0, 0.0)
    scale = LOG2E / math.sqrt(HEAD)
    query_fill = jnp.concatenate(
        [query_rows, jnp.zeros((LANES - HEAD - 8, BLOCK), f32)], axis=0
    ).astype(bf16)

    for s in range(slots):
        for j in range(heads + 2):
            first = (s * (heads + 2) + j) * HEAD
            piece = projected[first : first + HEAD]
            if j > heads:
                value = jnp.concatenate([piece, jnp.ones((LANES - HEAD, BLOCK), f32)], axis=0)
                value_out[here, s * LANES : (s + 1) * LANES] = value.T.astype(bf16)
                turned_value[s * VROWS : (s + 1) * VROWS, here] = value[:VROWS].astype(bf16)
                continue
            upper, lower = turn(piece[:half], piece[half:], cosine, sine)
            if j < heads:
                lanes = slice(j * BLOCK, (j + 1) * BLOCK)
                query_out[0, s, :HEAD, lanes] = jnp.concatenate(
                    [upper * scale, lower * scale], axis=0
                ).astype(bf16)
                query_out[0, s, HEAD:, lanes] = query_fill
            else:
                turned_key_out[s * HEAD : (s + 1) * HEAD, :] = jnp.concatenate(
                    [upper, lower], axis=0
                ).astype(bf16)
                whole = jnp.concatenate(
                    [upper, lower, key_rows, minus_rows, jnp.zeros((LANES - HEAD - 16, BLOCK), f32)],
                    axis=0,
                )
                key_out[here, s * LANES : (s + 1) * LANES] = whole.T.astype(bf16)

    query_rows = jnp.concatenate([query_rows] * heads, axis=1)

    def attend(blocks):
        width = blocks * BLOCK
        keys = pl.ds(pl.multiple_of((step + 1 - blocks) * BLOCK, BLOCK), width)
        scores = [
            matmul(key_out[keys, s * LANES : (s + 1) * LANES], query_out[0, s]) for s in range(slots)
        ]
        tops, weights = [], []
        for score in scores:
            last = score[width - BLOCK :] + tri_ref[...]
            if blocks > 1:
                score = jnp.concatenate([score[: width - BLOCK], last], axis=0)
            else:
                score = last
            tops.append(jnp.max(score, axis=0, keepdims=True))
            weights.append(jnp.exp2(score - tops[-1]).astype(bf16))
        summed = [
            matmul(turned_value[s * VROWS : (s + 1) * VROWS, keys], weights[s]) for s in range(slots)
        ]
        for s in range(slots):
            weight_sum = summed[s][HEAD : HEAD + 1]
            out = (summed[s][:HEAD] * (1.0 / weight_sum)).astype(bf16)
            for j in range(heads):
                first = (s * heads + j) * HEAD
                attended_out[first : first + HEAD, :] = out[:, j * BLOCK : (j + 1) * BLOCK]
            query_out[0, s, HEAD : HEAD + 16, :] = jnp.concatenate(
                [query_rows, part_rows(tops[s] + jnp.log2(weight_sum), 0)], axis=0
            ).astype(bf16)

    one = reaches(segments, step, 1)
    two = reaches(segments, step, 2)
    pl.when(jnp.logical_not(one))(functools.partial(attend, 1))
    pl.when(one & jnp.logical_not(two))(functools.partial(attend, 2))
    pl.when(two)(functools.partial(attend, 3))
    partial_out[...] = matmul(wout_ref[...], attended_out[...], TN).astype(bf16)


def chunks(width):
    return [slice(start, start + 256) for start in range(0, width, 256)]


def cost(flops, *arrays):
    size = sum(math.prod(a.shape) * a.dtype.itemsize for a in arrays)
    return pl.CostEstimate(flops=int(flops), bytes_accessed=size, transcendentals=0)


def token_spec(rows, width=BLOCK):
    return pl.BlockSpec((rows, width), lambda i, *_: (0, i))


def unit_shape(units, length):
    return shape_of((length // FFN_BLOCK, units, FFN_BLOCK), bf16)


def unit_spec(units):
    return pl.BlockSpec((1, units, FFN_BLOCK), lambda i: (i, 0, 0))


def full_spec(shape):
    return pl.BlockSpec(
        shape, lambda *_: (0,) * len(shape), pipeline_mode=pl.Buffered(buffer_count=1)
    )


def out_full_spec(shape):
    return pl.BlockSpec(shape, lambda *_: (0,) * len(shape))


shape_of = pltpu.HBM
anywhere = jax.ShapeDtypeStruct


def in_hbm(*arrays):
    return tuple(pltpu.with_memory_space_constraint(array, pltpu.HBM) for array in arrays)


def call_attention_forward(segments, parts, gain, wqkv, wout, cosine, sine, slots, heads):
    features, length = parts[0].shape
    joined = len(parts) == 3
    total = slots * heads
    big = shape_of((features, length), bf16)
    outs = [
        (big, token_spec(features)),
        (shape_of((1, length), f32), token_spec(1)),
        (
            shape_of((length // BLOCK, slots, LANES, heads * BLOCK), bf16),
            pl.BlockSpec((1, slots, LANES, heads * BLOCK), lambda i, *_: (i, 0, 0, 0)),
        ),
        (shape_of((length, slots * LANES), bf16), out_full_spec((length, slots * LANES))),
        (shape_of((slots * HEAD, length), bf16), token_spec(slots * HEAD)),
        (shape_of((length, slots * LANES), bf16), out_full_spec((length, slots * LANES))),
        (shape_of((total * HEAD, length), bf16), token_spec(total * HEAD)),
        (anywhere((features, length), bf16), token_spec(features)),
    ]
    if joined:
        outs.insert(0, (shape_of((features, length), f32), token_spec(features)))
    return pl.pallas_call(
        functools.partial(attention_forward, joined, slots, heads),
        grid_spec=pltpu.PrefetchScalarGridSpec(
            num_scalar_prefetch=1,
            grid=(length // BLOCK,),
            in_specs=[token_spec(features)] * len(parts)
            + [full_spec(a.shape) for a in (gain, wqkv, wout)]
            + [token_spec(HEAD // 2)] * 2
            + [token_spec(1)],
            out_specs=[spec for _, spec in outs],
            scratch_shapes=[
                pltpu.VMEM((slots * VROWS, length), bf16),
                pltpu.VMEM((BLOCK, heads * BLOCK), f32),
            ],
        ),
        out_shape=[shape for shape, _ in outs],
        compiler_params=pltpu.CompilerParams(vmem_limit_bytes=32 * MIB),
        cost_estimate=cost(2 * length * features * (wqkv.shape[0] + wout.shape[0]) + 12e9, *parts),
        name="attention_forward",
    )(segments, *in_hbm(parts[0]), *parts[1:], gain, wqkv, wout, cosine, sine, segments[None, :])


def ffn_forward(hidden_ref, own_ref, other_ref, gain_ref, gate_ref, up_ref, down_ref,
                middle_out, normed_out, inverse_out, gate_out, lift_out, inner_out, partial_out):
    middle = hidden_ref[...].astype(f32) + joined_sum(own_ref, other_ref)
    middle_out[...] = middle
    normed = normalise(middle, gain_ref[...], inverse_out)
    normed_out[...] = normed
    for chunk in chunks(gate_ref.shape[1]):
        gate = matmul(gate_ref[:, chunk], normed, TN)
        lift = matmul(up_ref[:, chunk], normed, TN)
        gate_out[0, chunk, :] = gate.astype(bf16)
        lift_out[0, chunk, :] = lift.astype(bf16)
        inner_out[0, chunk, :] = (gate * jax.nn.sigmoid(gate) * lift).astype(bf16)
    partial_out[...] = matmul(down_ref[...], inner_out[0]).astype(bf16)


def call_ffn_forward(hidden, own, other, gain, w_gate, w_up, w_down):
    features, length = hidden.shape
    units = w_gate.shape[1]
    spec = functools.partial(token_spec, width=FFN_BLOCK)
    return pl.pallas_call(
        ffn_forward,
        grid=(length // FFN_BLOCK,),
        in_specs=[spec(features)] * 3 + [full_spec(a.shape) for a in (gain, w_gate, w_up, w_down)],
        out_specs=[spec(features)] * 2 + [spec(1)] + [unit_spec(units)] * 3 + [spec(features)],
        out_shape=[
            shape_of((features, length), f32), shape_of((features, length), bf16),
            shape_of((1, length), f32), *[unit_shape(units, length)] * 3,
            anywhere((features, length), bf16),
        ],
        compiler_params=pltpu.CompilerParams(vmem_limit_bytes=40 * MIB),
        cost_estimate=cost(6 * length * features * units, hidden),
        name="ffn_forward",
    )(*in_hbm(hidden), own, other, gain, w_gate, w_up, w_down)


def ffn_backward(joined, grad_ref, *refs):
    grad = grad_ref[...]
    if joined:
        normed_ref, inverse_ref, own_ref, other_ref, gain_ref = refs[:5]
        refs = refs[5:]
        back = norm_back(normed_ref[...], inverse_ref[...], gain_ref[...], joined_sum(own_ref, other_ref))
        grad = (grad.astype(f32) + back).astype(bf16)
    gate_in, lift_in, gate_ref, up_ref, down_ref = refs[:5]
    refs = refs[5:]
    if joined:
        refs[0][...] = grad
        refs = refs[1:]
    grad_gate_out, grad_lift_out, partial_out = refs
    for chunk in chunks(gate_ref.shape[1]):
        grad_inner = matmul(down_ref[:, chunk], grad, TN)
        gate = gate_in[0, chunk, :].astype(f32)
        lift = lift_in[0, chunk, :].astype(f32)
        sigmoid = jax.nn.sigmoid(gate)
        grad_gate = grad_inner * lift * sigmoid * (1.0 + gate * (1.0 - sigmoid))
        grad_gate_out[0, chunk, :] = grad_gate.astype(bf16)
        grad_lift_out[0, chunk, :] = (grad_inner * gate * sigmoid).astype(bf16)
    partial = matmul(gate_ref[...], grad_gate_out[0]) + matmul(up_ref[...], grad_lift_out[0])
    partial_out[...] = partial.astype(bf16)


def call_ffn_backward(grad, joint, gate, lift, w_gate, w_up, w_down):
    features, length = grad.shape
    units = w_gate.shape[1]
    spec = functools.partial(token_spec, width=FFN_BLOCK)
    joint_specs, extra = [], []
    if joint:
        normed, inverse, own, other, gain = joint
        joint = (*in_hbm(normed), inverse, own, other, gain)
        joint_specs = [spec(features), spec(1), spec(features), spec(features), full_spec(gain.shape)]
        extra = [(shape_of((features, length), bf16), spec(features))]
    outs = extra + [(unit_shape(units, length), unit_spec(units))] * 2
    outs.append((anywhere((features, length), bf16), spec(features)))
    return pl.pallas_call(
        functools.partial(ffn_backward, bool(joint)),
        grid=(length // FFN_BLOCK,),
        in_specs=[spec(features)] + joint_specs + [unit_spec(units)] * 2
        + [full_spec(a.shape) for a in (w_gate, w_up, w_down)],
        out_specs=[spec for _, spec in outs],
        out_shape=[shape for shape, _ in outs],
        compiler_params=pltpu.CompilerParams(vmem_limit_bytes=40 * MIB),
        cost_estimate=cost(6 * length * features * units, grad),
        name="ffn_backward",
    )(*in_hbm(grad), *joint, *in_hbm(gate, lift), w_gate, w_up, w_down)


def attention_backward(slots, heads, segments, grad_ref, own_ref, other_ref, normed_ref, inverse_ref,
                       gain_ref, wout_ref, wqkv_ref, attended_ref, query_ref, key_ref, turned_key_ref,
                       value_ref, cos_ref, sin_ref,
                       attn_grad_out, projected_out, partial_out,
                       key_total, value_total, query_total, grad_heads, tri_ref):
    pair = pl.num_programs(0) - 1 - pl.program_id(0)
    half = HEAD // 2

    @pl.when(pl.program_id(0) == 0)
    def _():
        key_total[...] = jnp.zeros_like(key_total)
        value_total[...] = jnp.zeros_like(value_total)
        tri_ref[...] = causal_bias(heads)

    back = norm_back(normed_ref[...], inverse_ref[...], gain_ref[...], joined_sum(own_ref, other_ref))
    attn_grad = (grad_ref[...].astype(f32) + back).astype(bf16)
    attn_grad_out[...] = attn_grad
    grad_attended = matmul(wout_ref[...], attn_grad).astype(bf16)
    zeros = jnp.zeros((LANES - HEAD - 8, 2 * BLOCK), f32)
    for s in range(slots):
        for j in range(heads):
            first = (s * heads + j) * HEAD
            mine = grad_attended[first : first + HEAD]
            out = attended_ref[first : first + HEAD, :]
            delta = jnp.sum(mine.astype(f32) * out.astype(f32), axis=0, keepdims=True)
            rest = jnp.concatenate([part_rows(-delta, 0), zeros], axis=0).astype(bf16)
            for sub in range(2):
                lanes = slice(j * BLOCK, (j + 1) * BLOCK)
                tokens = slice(sub * BLOCK, (sub + 1) * BLOCK)
                grad_heads[sub, s, :HEAD, lanes] = mine[:, tokens]
                grad_heads[sub, s, HEAD:, lanes] = rest[:, tokens]

    def visit(sub, back):
        keys = block_at(2 * pair + sub - back)
        columns = [slice(s * LANES, (s + 1) * LANES) for s in range(slots)]
        features = [slice(s * HEAD, (s + 1) * HEAD) for s in range(slots)]
        scores = [matmul(key_ref[keys, columns[s]], query_ref[sub, s]) for s in range(slots)]
        grad_weights = [matmul(value_ref[keys, columns[s]], grad_heads[sub, s]) for s in range(slots)]
        weights, grad_scores = [], []
        for s in range(slots):
            score = scores[s] + tri_ref[...] if back == 0 else scores[s]
            weight = jnp.exp2(score)
            weights.append(weight.astype(bf16))
            grad_scores.append((weight * grad_weights[s]).astype(bf16))
        for s in range(slots):
            value_total[features[s], keys] += matmul(grad_heads[sub, s, :HEAD, :], weights[s], NT)
            key_total[features[s], keys] += matmul(query_ref[sub, s, :HEAD, :], grad_scores[s], NT)
            update = matmul(turned_key_ref[features[s], keys], grad_scores[s])
            if back == 0:
                query_total[sub, s] = update
            else:
                query_total[sub, s] += update

    for sub in (1, 0):
        visit(sub, 0)
        for back in (1, 2):
            pl.when(reaches(segments, 2 * pair + sub, back))(functools.partial(visit, sub, back))

    cosine, sine = cos_ref[...], sin_ref[...]
    here = pl.ds(pl.multiple_of(pair * 2 * BLOCK, 2 * BLOCK), 2 * BLOCK)
    for s in range(slots):
        for j in range(heads + 2):
            if j < heads:
                lanes = slice(j * BLOCK, (j + 1) * BLOCK)
                piece = jnp.concatenate([query_total[sub, s, :, lanes] for sub in range(2)], axis=1)
                piece = piece * (1.0 / math.sqrt(HEAD))
            elif j == heads:
                piece = key_total[s * HEAD : (s + 1) * HEAD, here] * LN2
            else:
                piece = value_total[s * HEAD : (s + 1) * HEAD, here]
            if j <= heads:
                upper, lower = turn(piece[:half], piece[half:], cosine, -sine)
                piece = jnp.concatenate([upper, lower], axis=0)
            first = (s * (heads + 2) + j) * HEAD
            projected_out[first : first + HEAD, :] = piece.astype(bf16)
    partial_out[...] = matmul(wqkv_ref[...], projected_out[...], TN).astype(bf16)


def call_attention_backward(segments, grad, own, other, normed, inverse, gain, wout, wqkv, attended, query,
                            key, turned_key, value, cosine, sine):
    features, length = grad.shape
    count = length // (2 * BLOCK)
    slots, wide_heads = query.shape[1], query.shape[3]
    heads = wide_heads // BLOCK

    def spec(rows):
        return pl.BlockSpec((rows, 2 * BLOCK), lambda i, *_: (0, count - 1 - i))

    return pl.pallas_call(
        functools.partial(attention_backward, slots, heads),
        grid_spec=pltpu.PrefetchScalarGridSpec(
            num_scalar_prefetch=1,
            grid=(count,),
            in_specs=[spec(features)] * 4 + [spec(1)]
            + [full_spec(a.shape) for a in (gain, wout, wqkv)]
            + [spec(attended.shape[0])]
            + [pl.BlockSpec((2, slots, LANES, wide_heads), lambda i, *_: (count - 1 - i, 0, 0, 0))]
            + [full_spec(a.shape) for a in (key, turned_key, value)]
            + [spec(HEAD // 2)] * 2,
            out_specs=[spec(features), spec(wqkv.shape[0]), spec(features)],
            scratch_shapes=[
                pltpu.VMEM((slots * HEAD, length), f32),
                pltpu.VMEM((slots * HEAD, length), f32),
                pltpu.VMEM((2, slots, HEAD, wide_heads), f32),
                pltpu.VMEM((2, slots, LANES, wide_heads), bf16),
                pltpu.VMEM((BLOCK, wide_heads), f32),
            ],
        ),
        out_shape=[
            shape_of((features, length), bf16), shape_of((wqkv.shape[0], length), bf16),
            anywhere((features, length), bf16),
        ],
        compiler_params=pltpu.CompilerParams(vmem_limit_bytes=33 * MIB),
        cost_estimate=cost(2 * length * features * (wqkv.shape[0] + wout.shape[0]) + slots * 8e9, grad),
        name="attention_backward",
    )(segments, *in_hbm(grad), own, other, *in_hbm(normed), inverse, gain, wout, wqkv,
      *in_hbm(attended, query), key, turned_key, value, cosine, sine)


def shard_rows(total, out_ref, order, rows, mine, first=0):
    total = total.astype(bf16)
    columns = slice(first, first + total.shape[1])
    half = len(order) // 2
    for place, shard in enumerate(order):
        side = mine if place < half else 1 - mine
        out_ref[side, place % half, :rows, columns] = total[shard * rows : (shard + 1) * rows]
        if out_ref.shape[2] > rows:
            out_ref[side, place % half, rows:, columns] = jnp.zeros(
                (out_ref.shape[2] - rows, total.shape[1]), bf16
            )


def begin_sending(staged, kept, sent, kept_signal, sent_signal):
    copies = [
        pltpu.make_async_copy(staged.at[1], sent, sent_signal),
        pltpu.make_async_copy(staged.at[0], kept, kept_signal),
    ]
    begin(copies)
    return copies


def fetches(pairs, arrived):
    groups, count = [], 0
    for sources, target in pairs:
        parts = []
        for source in sources:
            parts += [source] if len(source.shape) == 2 else [source.at[i] for i in range(source.shape[0])]
        first, group = 0, []
        for part in parts:
            lanes = target.at[:, pl.ds(first, part.shape[1])]
            group.append(pltpu.make_async_copy(part, lanes, arrived.at[count]))
            first += part.shape[1]
            count += 1
        groups.append(group)
    return groups


def begin(copies):
    for copy in copies:
        copy.start()


def finish(copies):
    for copy in copies:
        copy.wait()


def halves_product(left, right, copies):
    length = left.shape[1] // 2
    finish(copies[:2])
    total = matmul(left[:, :length], right[:, :length], NT)
    finish(copies[2:])
    return total + matmul(left[:, length:], right[:, length:], NT)


def ffn_weight_grad(orders, rows, bits, *refs):
    sources, outs = refs[:10], refs[10:16]
    buffers, staged, arrived, left = refs[16:21], refs[21], refs[22], refs[23]
    copies = fetches([(sources[2 * i : 2 * i + 2], buffers[i]) for i in range(5)], arrived)
    normed, gates, lifts, grads, inners = buffers
    begin(copies[0] + copies[1])
    outgoing = []

    def write(number, product):
        slot = number % 2
        if number >= 2:
            finish(outgoing[number - 2])
        for chunk in chunks(staged.shape[4]):
            shard_rows(product(chunk), staged.at[slot], orders[number], rows, bits[number], chunk.start)
        outgoing.append(
            begin_sending(
                staged.at[slot], outs[2 * number], outs[2 * number + 1],
                left.at[2 * number], left.at[2 * number + 1],
            )
        )

    finish(copies[0] + copies[1])
    begin(copies[2] + copies[3] + copies[4])
    write(0, lambda chunk: matmul(normed[...], gates[chunk, :], NT))
    finish(copies[2])
    write(1, lambda chunk: matmul(normed[...], lifts[chunk, :], NT))
    finish(copies[3] + copies[4])
    write(2, lambda chunk: matmul(grads[...], inners[chunk, :], NT))
    for pair in outgoing[1:]:
        finish(pair)


def call_weight_grad(kernel, name, bits, pairs, orders, columns, stages, flops):
    features, length = pairs[0][0].shape
    arrivals = sum(len(pair) * (1 if pair[0].ndim == 2 else pair[0].shape[0]) for pair in pairs)
    size = len(orders[0])
    rows = features // size
    padded = -(-rows // 16) * 16
    out = (size // 2, padded, columns)
    outs = pl.pallas_call(
        functools.partial(kernel, orders, rows),
        grid_spec=pltpu.PrefetchScalarGridSpec(
            num_scalar_prefetch=1,
            grid=(1,),
            in_specs=[pl.BlockSpec(memory_space=pl.ANY)] * (2 * len(pairs)),
            out_specs=[pl.BlockSpec(memory_space=pl.ANY)] * (2 * len(orders)),
            scratch_shapes=[pltpu.VMEM((pair[0].shape[-2], 2 * length), bf16) for pair in pairs]
            + [pltpu.VMEM((stages, 2) + out, bf16)]
            + [pltpu.SemaphoreType.DMA((arrivals,)), pltpu.SemaphoreType.DMA((2 * len(orders),))],
        ),
        out_shape=[shape_of(out, bf16)] * (2 * len(orders)),
        compiler_params=pltpu.CompilerParams(vmem_limit_bytes=52 * MIB),
        cost_estimate=cost(flops, *(array for pair in pairs for array in pair)),
        name=name,
    )(bits, *in_hbm(*(array for pair in pairs for array in pair)))
    return list(zip(outs[::2], outs[1::2]))


def call_ffn_weight_grad(bits, normed, grads, rights, orders):
    units = rights[0][0].shape[1]
    pairs = (normed, rights[0], rights[1], grads, rights[2])
    flops = 12 * normed[0].shape[0] * normed[0].shape[1] * units
    return call_weight_grad(ffn_weight_grad, "ffn_weight_grad", bits, pairs, orders, units, 2, flops)


def attention_weight_grad(orders, rows, bits, *refs):
    sources, outs = refs[:8], refs[8:14]
    buffers, staged, arrived, left = refs[14:18], refs[18], refs[19], refs[20]
    copies = fetches([(sources[2 * i : 2 * i + 2], buffers[i]) for i in range(4)], arrived)
    begin(copies[0] + copies[1])
    outgoing = []
    width = staged.shape[4]

    def write(number, pieces):
        column = 0
        for piece in pieces:
            shard_rows(piece, staged.at[number], orders[number], rows, bits[number], column)
            column += piece.shape[1]
        outgoing.extend(
            begin_sending(
                staged.at[number], outs[2 * number], outs[2 * number + 1],
                left.at[2 * number], left.at[2 * number + 1],
            )
        )

    def project(start, stop):
        return matmul(buffers[0][...], buffers[1][start:stop, :], NT)

    def outward(start, stop):
        return matmul(buffers[2][...], buffers[3][start:stop, :], NT)

    columns, most = buffers[1].shape[0], buffers[3].shape[0]
    rest = 2 * width - columns
    finish(copies[0] + copies[1])
    begin(copies[2] + copies[3])
    write(0, [project(start, start + 256) for start in range(0, width, 256)])
    body, tail = project(width, width + 256), project(width + 256, columns)
    finish(copies[2] + copies[3])
    write(1, [body, jnp.concatenate([tail, outward(0, rest)], axis=1)])
    write(2, [outward(start, min(start + 256, most)) for start in range(rest, most, 256)])
    finish(outgoing)


def call_attention_weight_grad(bits, above, below, orders):
    columns = above[1].shape[0] + above[3].shape[0]
    flops = 4 * above[0].shape[0] * above[0].shape[1] * columns
    return call_weight_grad(
        attention_weight_grad, "attention_weight_grad", bits, list(zip(above, below)), orders,
        columns // len(orders), len(orders), flops,
    )


def block_grad(grad_ref, normed_ref, inverse_ref, own_ref, other_ref, gain_ref, out_ref):
    back = norm_back(normed_ref[...], inverse_ref[...], gain_ref[...], joined_sum(own_ref, other_ref))
    out_ref[...] = (grad_ref[...].astype(f32) + back).astype(out_ref.dtype)


def call_block_grad(grad, normed, inverse, own, other, gain, kind):
    features, length = grad.shape
    spec = functools.partial(token_spec, width=FFN_BLOCK)
    return pl.pallas_call(
        block_grad,
        grid=(length // FFN_BLOCK,),
        in_specs=[spec(features)] * 2 + [spec(1)] + [spec(features)] * 2 + [full_spec(gain.shape)],
        out_specs=spec(features),
        out_shape=shape_of((features, length), kind),
        compiler_params=pltpu.CompilerParams(vmem_limit_bytes=32 * MIB),
        cost_estimate=cost(0, grad, normed, own, other),
        name="block_grad",
    )(*in_hbm(grad, normed), inverse, own, other, gain)


def gather_groups(owner, device, *refs):
    sources, (wqkv_out, wout_out), arrived = refs[:4], refs[4:6], refs[6]
    heights = [source.shape[1] for source in sources]
    joint = sum(heights[:3])
    slots = wqkv_out.shape[0] // joint
    for action in ("start", "wait"):
        for slot in range(slots):
            group, held = group_of(slot, owner, device)
            first = slot * joint
            for place, (source, height) in enumerate(zip(sources, heights)):
                if place < 3:
                    target = wqkv_out.at[pl.ds(first, height)]
                    first += height
                else:
                    target = wout_out.at[pl.ds(slot * height, height)]
                copy = pltpu.make_async_copy(source.at[group], target, arrived.at[4 * slot + place])

                def empty(target=target):
                    target[...] = jnp.zeros(target.shape, bf16)

                pl.when(held)(getattr(copy, action))
                if action == "start":
                    pl.when(jnp.logical_not(held))(empty)


def group_of(slot, owner, device):
    found, count = 0, 0
    for group in range(owner.shape[0]):
        mine = owner[group] == device[0]
        found = jnp.where(mine & (count == slot), group, found)
        count = count + jnp.where(mine, 1, 0)
    return found, count > slot


def call_gather_groups(owner, device, w_query, w_key, w_value, w_out, slots):
    features = w_query.shape[2]
    arrays = (w_query, w_key, w_value, w_out)
    joint = slots * (w_query.shape[1] + w_key.shape[1] + w_value.shape[1])
    outs = [(joint, features), (slots * w_out.shape[1], features)]
    return pl.pallas_call(
        gather_groups,
        grid_spec=pltpu.PrefetchScalarGridSpec(
            num_scalar_prefetch=2,
            grid=(1,),
            in_specs=[pl.BlockSpec(memory_space=pl.ANY)] * 4,
            out_specs=[out_full_spec(o) for o in outs],
            scratch_shapes=[pltpu.SemaphoreType.DMA((4 * slots,))],
        ),
        out_shape=[shape_of(o, bf16) for o in outs],
        name="gather_groups",
    )(owner, device, *in_hbm(*arrays))


def rotary_tables(length):
    position = np.arange(length, dtype=np.float64)[None, :]
    column = np.arange(HEAD // 2, dtype=np.float64)[:, None]
    angles = position * np.exp(column * (-2.0 * math.log(10000.0) / HEAD))
    return jnp.asarray(np.cos(angles), f32), jnp.asarray(np.sin(angles), f32)


def exchange(own):
    return lax.ppermute(own, "mp", [(0, 1), (1, 0)])


def stage_plans(bit_count):
    bits = list(range(bit_count))
    turned = [bits[:3], bits[1:3] + bits[:1], bits[2:3] + bits[:2]]
    return [[[bit] for bit in first + bits[3:]] for first in turned]


def shard_order(plan):
    bits = [bit for stage in plan for bit in stage]
    order = []
    for place in range(1 << len(bits)):
        shard = 0
        for rank, bit in enumerate(bits):
            if place >> (len(bits) - 1 - rank) & 1:
                shard |= 1 << bit
        order.append(shard)
    return order


def after(value, *others):
    return lax.optimization_barrier((value, others))[0]


class Stream:
    def __init__(self, parts, widths, count, stages):
        self.parts, self.widths, self.count, self.stages = parts, widths, count, list(stages)

    @classmethod
    def started(cls, kept, sent, plan):
        stream = cls([[(kept, 0, 0)]], [kept.shape[2]], kept.shape[0], plan)
        stream.transfer(sent, stream.stages.pop(0)[0])
        return stream

    def transfer(self, sent, bit):
        size = lax.axis_size("dp")
        received = lax.ppermute(sent, "dp", [(i, i ^ (1 << bit)) for i in range(size)])
        column = 0
        for terms, width in zip(self.parts, self.widths):
            terms.append((received, 0, column))
            column += width
        self.sent = sent

    def hold(self, *others):
        received = after(self.parts[0][-1][0], *others)
        for terms in self.parts:
            terms[-1] = (received, *terms[-1][1:])
        return self

    def sums(self, first, count):
        out = []
        for terms, width in zip(self.parts, self.widths):
            pieces = [
                lax.dynamic_slice(array, (start + first, 0, column), (count, array.shape[1], width))
                for array, start, column in terms
            ]
            out.append(sum(piece.astype(f32) for piece in pieces))
        return out

    def send(self, eager=False):
        bit = self.stages.pop(0)[0]
        mine = (lax.axis_index("dp") >> bit) & 1
        self.count //= 2
        sent = [piece.astype(bf16) for piece in self.sums((1 - mine) * self.count, self.count)]
        if eager:
            kept = self.sums(mine * self.count, self.count)
            self.parts = [[(piece.astype(bf16), 0, 0)] for piece in kept]
        else:
            self.parts = [
                [(array, start + mine * self.count, column) for array, start, column in terms]
                for terms in self.parts
            ]
        self.transfer(sent[0] if len(sent) == 1 else jnp.concatenate(sent, axis=2), bit)
        return self.sent

    def totals(self):
        return [piece[0] for piece in self.sums(0, 1)]


def joined(streams):
    return Stream(
        [terms for stream in streams for terms in stream.parts],
        [width for stream in streams for width in stream.widths],
        streams[0].count,
        streams[0].stages,
    )


def per_device(
    tokens_in,
    segment_ids,
    kv_owner,
    w_query,
    w_key,
    w_value,
    w_out,
    attn_gain,
    w_gate,
    w_up,
    w_down,
    ffn_gain,
    cotangent,
):
    features = tokens_in.shape[2]
    length = tokens_in.shape[1]
    group_cols = w_query.shape[2]
    heads = group_cols // HEAD
    slots = (kv_owner.shape[0] + lax.axis_size("mp") - 1) // lax.axis_size("mp")
    size = lax.axis_size("dp")
    rows = features // size

    device = lax.axis_index("mp").astype(jnp.int32)[None]
    wqkv, wout = call_gather_groups(
        kv_owner, device, *(jnp.swapaxes(w, 1, 2) for w in (w_query, w_key, w_value)), w_out, slots
    )
    w_down = w_down.T
    segments = segment_ids[0]
    cosine, sine = rotary_tables(length)
    gain_one, gain_two = (
        jnp.broadcast_to(gain.astype(f32)[:, None], (features, LANES)) for gain in (attn_gain, ffn_gain)
    )

    parts = (tokens_in[0].T,)
    saved = []
    for _ in range(REPEAT):
        own_weights = (wqkv, wout) if len(parts) == 3 else in_hbm(wqkv, wout)
        outs = list(
            call_attention_forward(segments, parts, gain_one, *own_weights, cosine, sine, slots, heads)
        )
        hidden = outs.pop(0) if len(parts) == 3 else parts[0]
        normed, inverse, query, key, turned_key, value, attended, partial = outs
        middle, normed_two, inverse_two, gate, lift, inner, partial_two = call_ffn_forward(
            hidden, partial, exchange(partial), gain_two, w_gate, w_up, w_down
        )
        parts = (middle, partial_two, exchange(partial_two))
        saved.append((
            normed, inverse, query, key, turned_key, value, attended, normed_two, inverse_two, gate, lift, inner,
        ))

    plans = stage_plans(size.bit_length() - 1)
    orders = [shard_order(plan) for plan in plans]
    bits = jnp.stack([(lax.axis_index("dp") >> plan[0][0]) & 1 for plan in plans]).astype(jnp.int32)
    joint = ()
    grad = cotangent[0].T
    for r in reversed(range(REPEAT)):
        (normed, inverse, query, key, turned_key, value, attended,
         normed_two, inverse_two, gate, lift, inner) = saved[r]
        last = r == 0
        outs = list(call_ffn_backward(grad, joint, gate, lift, w_gate, w_up, w_down))
        if joint:
            grad = outs.pop(0)
        ffn_grad = grad
        grad_gate, grad_lift, partial = outs
        other = exchange(partial)
        if not last:
            parts = after(parts, partial)
            tokens_out = (parts[0] + (parts[1].astype(f32) + parts[2].astype(f32))).astype(bf16)
            grad = after(grad, tokens_out)
        else:
            payloads = call_ffn_weight_grad(
                bits, (above["normed_two"], normed_two), (above["ffn_grad"], ffn_grad),
                ((above["grad_gate"], grad_gate), (above["grad_lift"], grad_lift), (above["inner"], inner)),
                orders,
            )
            track_a, track_b, down = (
                Stream.started(*payload, plan) for payload, plan in zip(payloads, plans)
            )
            partial = after(partial, payloads)
        grad, projected, partial_two = call_attention_backward(
            segments, grad, partial, other, normed_two, inverse_two, gain_two, wout, wqkv, attended, query,
            key, turned_key, value, cosine, sine,
        )
        other_two = exchange(partial_two)
        if not last:
            above = dict(
                ffn_grad=ffn_grad, inner=inner, normed_two=normed_two, grad_lift=grad_lift,
                grad_gate=grad_gate, attention=(normed, projected, grad, attended),
            )
        joint = (normed, inverse, partial_two, other_two, gain_one)
    ffn = (track_a, track_b, down)
    sent = [stream.hold(projected).send() for stream in ffn]
    payloads = call_attention_weight_grad(
        bits, above["attention"], (normed, after(projected, sent), grad, attended), orders
    )
    tracks = [Stream.started(*payload, plan) for payload, plan in zip(payloads, plans)]
    for stream in ffn:
        stream.hold(payloads, other_two)
    sent = [stream.send() for stream in (track_a, track_b)]
    grad_in = call_block_grad(after(grad, sent, payloads), *joint, f32)
    both = joined([stream.hold(grad_in) for stream in (track_a, track_b)])
    sent = [both.send(True), down.hold(grad_in).send(True)]
    sent = [stream.hold(sent).send(True) for stream in tracks]
    sent = [down.hold(sent).send(True)]
    while len(tracks[0].stages) > 1:
        sent = [stream.hold(sent).send(True) for stream in tracks]
    attn = joined([stream.hold(sent) for stream in tracks])
    pending = [both, down, attn]
    while any(stream.stages for stream in pending):
        for stream in pending:
            if stream.stages:
                stream.send(True)
    gate_total, up_total = both.totals()
    (down_total,) = down.totals()
    attn_total = jnp.concatenate(attn.totals(), axis=1)[:rows]

    start = lax.axis_index("dp") * rows

    def my_rows(weights):
        return lax.dynamic_slice_in_dim(weights, start, rows, 0).astype(f32)

    gate_total, up_total, down_total = (total[:rows] for total in (gate_total, up_total, down_total))
    wqkv = after(wqkv, grad_in)
    chosen = (jnp.arange(rows)[:, None] + start == jnp.arange(features)[None, :]).astype(bf16)
    wqkv_rows = matmul(chosen, wqkv, NT)
    joint_cols = wqkv.shape[0]
    gains = jnp.stack([
        jnp.sum(attn_total[:, :joint_cols] * wqkv_rows, axis=1),
        jnp.sum(gate_total * my_rows(w_gate) + up_total * my_rows(w_up), axis=1),
    ])
    gains = gains + exchange(gains)
    gains = gains / lax.dynamic_slice_in_dim(jnp.stack([attn_gain, ffn_gain]), start, rows, 1).astype(f32)

    ends = [group_cols, group_cols + HEAD]
    by_slot = jnp.moveaxis(attn_total[:, :joint_cols].reshape(rows, slots, -1), 1, 0)
    return (
        tokens_out.T[None],
        grad_in.T[None],
        by_slot[:, :, : ends[0]],
        by_slot[:, :, ends[0] : ends[1]],
        by_slot[:, :, ends[1] :],
        attn_total[:, joint_cols:].T.reshape(slots, group_cols, rows),
        gate_total,
        up_total,
        down_total.T,
        gains[0],
        gains[1],
    )


def solution(mesh):
    in_specs = (
        P("dp", None, None),
        P("dp", None),
        P(),
        P(),
        P(),
        P(),
        P(),
        P(),
        P(None, "mp"),
        P(None, "mp"),
        P("mp", None),
        P(),
        P("dp", None, None),
    )
    out_specs = (
        P("dp", None, None),
        P("dp", None, None),
        P("mp", "dp", None),
        P("mp", "dp", None),
        P("mp", "dp", None),
        P("mp", None, "dp"),
        P("dp", "mp"),
        P("dp", "mp"),
        P("mp", "dp"),
        P("dp"),
        P("dp"),
    )
    return jax.shard_map(
        per_device, mesh=mesh, in_specs=in_specs, out_specs=out_specs, check_vma=False
    )
```

```python
import functools
import math

import jax
import jax.numpy as jnp
import numpy as np
from jax import lax
from jax.experimental import pallas as pl
from jax.experimental.pallas import tpu as pltpu
from jax.sharding import PartitionSpec as P

REPEAT = 2
BLOCK = 256
FFN_BLOCK = 512
LANES = 128
HEAD = 64
GROUP = 3
VROWS = 80
epsilon = 1e-05
masked_value = -1e30
LOG2E = math.log2(math.e)
LN2 = math.log(2.0)
f32 = jnp.float32
bf16 = jnp.bfloat16
NN = (((1,), (0,)), ((), ()))
NT = (((1,), (1,)), ((), ()))
TN = (((0,), (0,)), ((), ()))
MIB = 1024 * 1024


def matmul(a, b, dims=NN):
    return lax.dot_general(a, b, dims, preferred_element_type=f32)


def wide(column, width):
    return jnp.concatenate([column] * (width // LANES), axis=1)


def inverse_rms(values):
    return lax.rsqrt(jnp.mean(values * values, axis=0, keepdims=True) + epsilon)


def normalise(values, gain, inverse_out):
    inverse = inverse_rms(values)
    inverse_out[...] = inverse
    return (values * inverse * wide(gain, values.shape[1])).astype(bf16)


def norm_back(normed, inverse, gain, grad_normed):
    normed = normed.astype(f32)
    inner_mean = jnp.mean(grad_normed * normed, axis=0, keepdims=True)
    width = normed.shape[1]
    return inverse * (grad_normed * wide(gain, width) - normed * wide(1.0 / gain, width) * inner_mean)


def joined_sum(own_ref, other_ref):
    return own_ref[...].astype(f32) + other_ref[...].astype(f32)


def three_parts(value):
    high = value.astype(bf16).astype(f32)
    rest = value - high
    middle = rest.astype(bf16).astype(f32)
    return high, middle, rest - middle


def part_rows(value, first):
    row = lax.broadcasted_iota(jnp.int32, (8, value.shape[1]), 0)
    out = jnp.zeros((8, value.shape[1]), f32)
    for number, part in enumerate(three_parts(value)):
        out = jnp.where(row == first + number, part, out)
    return out


def causal_bias(heads):
    key = lax.broadcasted_iota(jnp.int32, (BLOCK, heads * BLOCK), 0)
    query = lax.broadcasted_iota(jnp.int32, (BLOCK, heads * BLOCK), 1) % BLOCK
    return jnp.where(key <= query, 0.0, masked_value)


def reaches(segments, step, back):
    last = jnp.maximum((step - back + 1) * BLOCK - 1, 0)
    return (step >= back) & (segments[last] == segments[step * BLOCK])


def block_at(index):
    return pl.ds(pl.multiple_of(index * BLOCK, BLOCK), BLOCK)


def turn(upper, lower, cosine, sine):
    return upper * cosine - lower * sine, lower * cosine + upper * sine


def attention_forward(joined, slots, heads, segments, *refs):
    refs = list(refs)
    hidden = refs.pop(0)[...].astype(f32)
    if joined:
        hidden = hidden + joined_sum(refs.pop(0), refs.pop(0))
    gain_ref, wqkv_ref, wout_ref, cos_ref, sin_ref, segment_ref = refs[:6]
    refs = refs[6:]
    if joined:
        refs.pop(0)[...] = hidden
    (normed_out, inverse_out, query_out, key_out, turned_key_out, value_out, attended_out, partial_out,
     turned_value, tri_ref) = refs
    step = pl.program_id(0)
    here = block_at(step)

    @pl.when(step == 0)
    def _():
        tri_ref[...] = causal_bias(heads)

    normed = normalise(hidden, gain_ref[...], inverse_out)
    normed_out[...] = normed
    projected = matmul(wqkv_ref[...], normed)
    cosine, sine = cos_ref[...], sin_ref[...]
    half = HEAD // 2

    same = lax.broadcasted_iota(jnp.int32, (8, BLOCK), 0) == segment_ref[...]
    query_rows = jnp.where(same, 1.0, 0.0)
    key_rows = jnp.where(same, 0.0, masked_value)
    row = lax.broadcasted_iota(jnp.int32, (8, BLOCK), 0)
    minus_rows = jnp.where(row < 3, -1.0, 0.0)
    scale = LOG2E / math.sqrt(HEAD)
    query_fill = jnp.concatenate(
        [query_rows, jnp.zeros((LANES - HEAD - 8, BLOCK), f32)], axis=0
    ).astype(bf16)

    for s in range(slots):
        for j in range(heads + 2):
            first = (s * (heads + 2) + j) * HEAD
            piece = projected[first : first + HEAD]
            if j > heads:
                value = jnp.concatenate([piece, jnp.ones((LANES - HEAD, BLOCK), f32)], axis=0)
                value_out[here, s * LANES : (s + 1) * LANES] = value.T.astype(bf16)
                turned_value[s * VROWS : (s + 1) * VROWS, here] = value[:VROWS].astype(bf16)
                continue
            upper, lower = turn(piece[:half], piece[half:], cosine, sine)
            if j < heads:
                lanes = slice(j * BLOCK, (j + 1) * BLOCK)
                query_out[0, s, :HEAD, lanes] = jnp.concatenate(
                    [upper * scale, lower * scale], axis=0
                ).astype(bf16)
                query_out[0, s, HEAD:, lanes] = query_fill
            else:
                turned_key_out[s * HEAD : (s + 1) * HEAD, :] = jnp.concatenate(
                    [upper, lower], axis=0
                ).astype(bf16)
                whole = jnp.concatenate(
                    [upper, lower, key_rows, minus_rows, jnp.zeros((LANES - HEAD - 16, BLOCK), f32)],
                    axis=0,
                )
                key_out[here, s * LANES : (s + 1) * LANES] = whole.T.astype(bf16)

    query_rows = jnp.concatenate([query_rows] * heads, axis=1)

    def attend(blocks):
        width = blocks * BLOCK
        keys = pl.ds(pl.multiple_of((step + 1 - blocks) * BLOCK, BLOCK), width)
        scores = [
            matmul(key_out[keys, s * LANES : (s + 1) * LANES], query_out[0, s]) for s in range(slots)
        ]
        tops, weights = [], []
        for score in scores:
            last = score[width - BLOCK :] + tri_ref[...]
            if blocks > 1:
                score = jnp.concatenate([score[: width - BLOCK], last], axis=0)
            else:
                score = last
            tops.append(jnp.max(score, axis=0, keepdims=True))
            weights.append(jnp.exp2(score - tops[-1]).astype(bf16))
        summed = [
            matmul(turned_value[s * VROWS : (s + 1) * VROWS, keys], weights[s]) for s in range(slots)
        ]
        for s in range(slots):
            weight_sum = summed[s][HEAD : HEAD + 1]
            out = (summed[s][:HEAD] * (1.0 / weight_sum)).astype(bf16)
            for j in range(heads):
                first = (s * heads + j) * HEAD
                attended_out[first : first + HEAD, :] = out[:, j * BLOCK : (j + 1) * BLOCK]
            query_out[0, s, HEAD : HEAD + 16, :] = jnp.concatenate(
                [query_rows, part_rows(tops[s] + jnp.log2(weight_sum), 0)], axis=0
            ).astype(bf16)

    one = reaches(segments, step, 1)
    two = reaches(segments, step, 2)
    pl.when(jnp.logical_not(one))(functools.partial(attend, 1))
    pl.when(one & jnp.logical_not(two))(functools.partial(attend, 2))
    pl.when(two)(functools.partial(attend, 3))
    partial_out[...] = matmul(wout_ref[...], attended_out[...], TN).astype(bf16)


def chunks(width):
    return [slice(start, start + 256) for start in range(0, width, 256)]


def cost(flops, *arrays):
    size = sum(math.prod(a.shape) * a.dtype.itemsize for a in arrays)
    return pl.CostEstimate(flops=int(flops), bytes_accessed=size, transcendentals=0)


def token_spec(rows, width=BLOCK):
    return pl.BlockSpec((rows, width), lambda i, *_: (0, i))


def unit_shape(units, length):
    return shape_of((length // FFN_BLOCK, units, FFN_BLOCK), bf16)


def unit_spec(units):
    return pl.BlockSpec((1, units, FFN_BLOCK), lambda i: (i, 0, 0))


def full_spec(shape):
    return pl.BlockSpec(
        shape, lambda *_: (0,) * len(shape), pipeline_mode=pl.Buffered(buffer_count=1)
    )


def out_full_spec(shape):
    return pl.BlockSpec(shape, lambda *_: (0,) * len(shape))


shape_of = pltpu.HBM
anywhere = jax.ShapeDtypeStruct


def in_hbm(*arrays):
    return tuple(pltpu.with_memory_space_constraint(array, pltpu.HBM) for array in arrays)


def call_attention_forward(segments, parts, gain, wqkv, wout, cosine, sine, slots, heads):
    features, length = parts[0].shape
    joined = len(parts) == 3
    total = slots * heads
    big = shape_of((features, length), bf16)
    outs = [
        (big, token_spec(features)),
        (shape_of((1, length), f32), token_spec(1)),
        (
            shape_of((length // BLOCK, slots, LANES, heads * BLOCK), bf16),
            pl.BlockSpec((1, slots, LANES, heads * BLOCK), lambda i, *_: (i, 0, 0, 0)),
        ),
        (shape_of((length, slots * LANES), bf16), out_full_spec((length, slots * LANES))),
        (shape_of((slots * HEAD, length), bf16), token_spec(slots * HEAD)),
        (shape_of((length, slots * LANES), bf16), out_full_spec((length, slots * LANES))),
        (shape_of((total * HEAD, length), bf16), token_spec(total * HEAD)),
        (anywhere((features, length), bf16), token_spec(features)),
    ]
    if joined:
        outs.insert(0, (shape_of((features, length), f32), token_spec(features)))
    return pl.pallas_call(
        functools.partial(attention_forward, joined, slots, heads),
        grid_spec=pltpu.PrefetchScalarGridSpec(
            num_scalar_prefetch=1,
            grid=(length // BLOCK,),
            in_specs=[token_spec(features)] * len(parts)
            + [full_spec(a.shape) for a in (gain, wqkv, wout)]
            + [token_spec(HEAD // 2)] * 2
            + [token_spec(1)],
            out_specs=[spec for _, spec in outs],
            scratch_shapes=[
                pltpu.VMEM((slots * VROWS, length), bf16),
                pltpu.VMEM((BLOCK, heads * BLOCK), f32),
            ],
        ),
        out_shape=[shape for shape, _ in outs],
        compiler_params=pltpu.CompilerParams(vmem_limit_bytes=32 * MIB),
        cost_estimate=cost(2 * length * features * (wqkv.shape[0] + wout.shape[0]) + 12e9, *parts),
        name="attention_forward",
    )(segments, *in_hbm(parts[0]), *parts[1:], gain, wqkv, wout, cosine, sine, segments[None, :])


def ffn_forward(hidden_ref, own_ref, other_ref, gain_ref, gate_ref, up_ref, down_ref,
                middle_out, normed_out, inverse_out, gate_out, lift_out, inner_out, partial_out):
    middle = hidden_ref[...].astype(f32) + joined_sum(own_ref, other_ref)
    middle_out[...] = middle
    normed = normalise(middle, gain_ref[...], inverse_out)
    normed_out[...] = normed
    for chunk in chunks(gate_ref.shape[1]):
        gate = matmul(gate_ref[:, chunk], normed, TN)
        lift = matmul(up_ref[:, chunk], normed, TN)
        gate_out[0, chunk, :] = gate.astype(bf16)
        lift_out[0, chunk, :] = lift.astype(bf16)
        inner_out[0, chunk, :] = (gate * jax.nn.sigmoid(gate) * lift).astype(bf16)
    partial_out[...] = matmul(down_ref[...], inner_out[0]).astype(bf16)


def call_ffn_forward(hidden, own, other, gain, w_gate, w_up, w_down):
    features, length = hidden.shape
    units = w_gate.shape[1]
    spec = functools.partial(token_spec, width=FFN_BLOCK)
    return pl.pallas_call(
        ffn_forward,
        grid=(length // FFN_BLOCK,),
        in_specs=[spec(features)] * 3 + [full_spec(a.shape) for a in (gain, w_gate, w_up, w_down)],
        out_specs=[spec(features)] * 2 + [spec(1)] + [unit_spec(units)] * 3 + [spec(features)],
        out_shape=[
            shape_of((features, length), f32), shape_of((features, length), bf16),
            shape_of((1, length), f32), *[unit_shape(units, length)] * 3,
            anywhere((features, length), bf16),
        ],
        compiler_params=pltpu.CompilerParams(vmem_limit_bytes=40 * MIB),
        cost_estimate=cost(6 * length * features * units, hidden),
        name="ffn_forward",
    )(*in_hbm(hidden), own, other, gain, w_gate, w_up, w_down)


def ffn_backward(joined, grad_ref, *refs):
    grad = grad_ref[...]
    if joined:
        normed_ref, inverse_ref, own_ref, other_ref, gain_ref = refs[:5]
        refs = refs[5:]
        back = norm_back(normed_ref[...], inverse_ref[...], gain_ref[...], joined_sum(own_ref, other_ref))
        grad = (grad.astype(f32) + back).astype(bf16)
    gate_in, lift_in, gate_ref, up_ref, down_ref = refs[:5]
    refs = refs[5:]
    if joined:
        refs[0][...] = grad
        refs = refs[1:]
    grad_gate_out, grad_lift_out, partial_out = refs
    for chunk in chunks(gate_ref.shape[1]):
        grad_inner = matmul(down_ref[:, chunk], grad, TN)
        gate = gate_in[0, chunk, :].astype(f32)
        lift = lift_in[0, chunk, :].astype(f32)
        sigmoid = jax.nn.sigmoid(gate)
        grad_gate = grad_inner * lift * sigmoid * (1.0 + gate * (1.0 - sigmoid))
        grad_gate_out[0, chunk, :] = grad_gate.astype(bf16)
        grad_lift_out[0, chunk, :] = (grad_inner * gate * sigmoid).astype(bf16)
    partial = matmul(gate_ref[...], grad_gate_out[0]) + matmul(up_ref[...], grad_lift_out[0])
    partial_out[...] = partial.astype(bf16)


def call_ffn_backward(grad, joint, gate, lift, w_gate, w_up, w_down):
    features, length = grad.shape
    units = w_gate.shape[1]
    spec = functools.partial(token_spec, width=FFN_BLOCK)
    joint_specs, extra = [], []
    if joint:
        normed, inverse, own, other, gain = joint
        joint = (*in_hbm(normed), inverse, own, other, gain)
        joint_specs = [spec(features), spec(1), spec(features), spec(features), full_spec(gain.shape)]
        extra = [(shape_of((features, length), bf16), spec(features))]
    outs = extra + [(unit_shape(units, length), unit_spec(units))] * 2
    outs.append((anywhere((features, length), bf16), spec(features)))
    return pl.pallas_call(
        functools.partial(ffn_backward, bool(joint)),
        grid=(length // FFN_BLOCK,),
        in_specs=[spec(features)] + joint_specs + [unit_spec(units)] * 2
        + [full_spec(a.shape) for a in (w_gate, w_up, w_down)],
        out_specs=[spec for _, spec in outs],
        out_shape=[shape for shape, _ in outs],
        compiler_params=pltpu.CompilerParams(vmem_limit_bytes=40 * MIB),
        cost_estimate=cost(6 * length * features * units, grad),
        name="ffn_backward",
    )(*in_hbm(grad), *joint, *in_hbm(gate, lift), w_gate, w_up, w_down)


def attention_backward(slots, heads, segments, grad_ref, own_ref, other_ref, normed_ref, inverse_ref,
                       gain_ref, wout_ref, wqkv_ref, attended_ref, query_ref, key_ref, turned_key_ref,
                       value_ref, cos_ref, sin_ref,
                       attn_grad_out, projected_out, partial_out,
                       key_total, value_total, query_total, grad_heads, tri_ref):
    pair = pl.num_programs(0) - 1 - pl.program_id(0)
    half = HEAD // 2

    @pl.when(pl.program_id(0) == 0)
    def _():
        key_total[...] = jnp.zeros_like(key_total)
        value_total[...] = jnp.zeros_like(value_total)
        tri_ref[...] = causal_bias(heads)

    back = norm_back(normed_ref[...], inverse_ref[...], gain_ref[...], joined_sum(own_ref, other_ref))
    attn_grad = (grad_ref[...].astype(f32) + back).astype(bf16)
    attn_grad_out[...] = attn_grad
    grad_attended = matmul(wout_ref[...], attn_grad).astype(bf16)
    zeros = jnp.zeros((LANES - HEAD - 8, 2 * BLOCK), f32)
    for s in range(slots):
        for j in range(heads):
            first = (s * heads + j) * HEAD
            mine = grad_attended[first : first + HEAD]
            out = attended_ref[first : first + HEAD, :]
            delta = jnp.sum(mine.astype(f32) * out.astype(f32), axis=0, keepdims=True)
            rest = jnp.concatenate([part_rows(-delta, 0), zeros], axis=0).astype(bf16)
            for sub in range(2):
                lanes = slice(j * BLOCK, (j + 1) * BLOCK)
                tokens = slice(sub * BLOCK, (sub + 1) * BLOCK)
                grad_heads[sub, s, :HEAD, lanes] = mine[:, tokens]
                grad_heads[sub, s, HEAD:, lanes] = rest[:, tokens]

    def visit(sub, back):
        keys = block_at(2 * pair + sub - back)
        columns = [slice(s * LANES, (s + 1) * LANES) for s in range(slots)]
        features = [slice(s * HEAD, (s + 1) * HEAD) for s in range(slots)]
        scores = [matmul(key_ref[keys, columns[s]], query_ref[sub, s]) for s in range(slots)]
        grad_weights = [matmul(value_ref[keys, columns[s]], grad_heads[sub, s]) for s in range(slots)]
        weights, grad_scores = [], []
        for s in range(slots):
            score = scores[s] + tri_ref[...] if back == 0 else scores[s]
            weight = jnp.exp2(score)
            weights.append(weight.astype(bf16))
            grad_scores.append((weight * grad_weights[s]).astype(bf16))
        for s in range(slots):
            value_total[features[s], keys] += matmul(grad_heads[sub, s, :HEAD, :], weights[s], NT)
            key_total[features[s], keys] += matmul(query_ref[sub, s, :HEAD, :], grad_scores[s], NT)
            update = matmul(turned_key_ref[features[s], keys], grad_scores[s])
            if back == 0:
                query_total[sub, s] = update
            else:
                query_total[sub, s] += update

    for sub in (1, 0):
        visit(sub, 0)
        for back in (1, 2):
            pl.when(reaches(segments, 2 * pair + sub, back))(functools.partial(visit, sub, back))

    cosine, sine = cos_ref[...], sin_ref[...]
    here = pl.ds(pl.multiple_of(pair * 2 * BLOCK, 2 * BLOCK), 2 * BLOCK)
    for s in range(slots):
        for j in range(heads + 2):
            if j < heads:
                lanes = slice(j * BLOCK, (j + 1) * BLOCK)
                piece = jnp.concatenate([query_total[sub, s, :, lanes] for sub in range(2)], axis=1)
                piece = piece * (1.0 / math.sqrt(HEAD))
            elif j == heads:
                piece = key_total[s * HEAD : (s + 1) * HEAD, here] * LN2
            else:
                piece = value_total[s * HEAD : (s + 1) * HEAD, here]
            if j <= heads:
                upper, lower = turn(piece[:half], piece[half:], cosine, -sine)
                piece = jnp.concatenate([upper, lower], axis=0)
            first = (s * (heads + 2) + j) * HEAD
            projected_out[first : first + HEAD, :] = piece.astype(bf16)
    partial_out[...] = matmul(wqkv_ref[...], projected_out[...], TN).astype(bf16)


def call_attention_backward(segments, grad, own, other, normed, inverse, gain, wout, wqkv, attended, query,
                            key, turned_key, value, cosine, sine):
    features, length = grad.shape
    count = length // (2 * BLOCK)
    slots, wide_heads = query.shape[1], query.shape[3]
    heads = wide_heads // BLOCK

    def spec(rows):
        return pl.BlockSpec((rows, 2 * BLOCK), lambda i, *_: (0, count - 1 - i))

    return pl.pallas_call(
        functools.partial(attention_backward, slots, heads),
        grid_spec=pltpu.PrefetchScalarGridSpec(
            num_scalar_prefetch=1,
            grid=(count,),
            in_specs=[spec(features)] * 4 + [spec(1)]
            + [full_spec(a.shape) for a in (gain, wout, wqkv)]
            + [spec(attended.shape[0])]
            + [pl.BlockSpec((2, slots, LANES, wide_heads), lambda i, *_: (count - 1 - i, 0, 0, 0))]
            + [full_spec(a.shape) for a in (key, turned_key, value)]
            + [spec(HEAD // 2)] * 2,
            out_specs=[spec(features), spec(wqkv.shape[0]), spec(features)],
            scratch_shapes=[
                pltpu.VMEM((slots * HEAD, length), f32),
                pltpu.VMEM((slots * HEAD, length), f32),
                pltpu.VMEM((2, slots, HEAD, wide_heads), f32),
                pltpu.VMEM((2, slots, LANES, wide_heads), bf16),
                pltpu.VMEM((BLOCK, wide_heads), f32),
            ],
        ),
        out_shape=[
            shape_of((features, length), bf16), shape_of((wqkv.shape[0], length), bf16),
            anywhere((features, length), bf16),
        ],
        compiler_params=pltpu.CompilerParams(vmem_limit_bytes=33 * MIB),
        cost_estimate=cost(2 * length * features * (wqkv.shape[0] + wout.shape[0]) + slots * 8e9, grad),
        name="attention_backward",
    )(segments, *in_hbm(grad), own, other, *in_hbm(normed), inverse, gain, wout, wqkv,
      *in_hbm(attended, query), key, turned_key, value, cosine, sine)


def shard_rows(total, out_ref, order, rows, mine, first=0):
    total = total.astype(bf16)
    columns = slice(first, first + total.shape[1])
    half = len(order) // 2
    for place, shard in enumerate(order):
        side = mine if place < half else 1 - mine
        out_ref[side, place % half, :rows, columns] = total[shard * rows : (shard + 1) * rows]
        if out_ref.shape[2] > rows:
            out_ref[side, place % half, rows:, columns] = jnp.zeros(
                (out_ref.shape[2] - rows, total.shape[1]), bf16
            )


def begin_sending(staged, kept, sent, kept_signal, sent_signal):
    copies = [
        pltpu.make_async_copy(staged.at[1], sent, sent_signal),
        pltpu.make_async_copy(staged.at[0], kept, kept_signal),
    ]
    begin(copies)
    return copies


def fetches(pairs, arrived):
    groups, count = [], 0
    for sources, target in pairs:
        parts = []
        for source in sources:
            parts += [source] if len(source.shape) == 2 else [source.at[i] for i in range(source.shape[0])]
        height = target.shape[0]
        taken = 256 if len(groups) == 1 else height
        bands = []
        for start in range(0, height, taken):
            rows = pl.ds(start, min(taken, height - start))
            first, group = 0, []
            for part in parts:
                target_part = target.at[rows, pl.ds(first, part.shape[1])]
                group.append(pltpu.make_async_copy(part.at[rows], target_part, arrived.at[count]))
                first += part.shape[1]
                count += 1
            bands.append(group)
        groups.append(bands if len(groups) == 1 else bands[0])
    return groups


def begin(copies):
    for copy in copies:
        copy.start()


def finish(copies):
    for copy in copies:
        copy.wait()


def halves_product(left, right, copies):
    length = left.shape[1] // 2
    finish(copies[:2])
    total = matmul(left[:, :length], right[:, :length], NT)
    finish(copies[2:])
    return total + matmul(left[:, length:], right[:, length:], NT)


def ffn_weight_grad(orders, rows, bits, *refs):
    sources, outs = refs[:10], refs[10:16]
    buffers, staged, arrived, left = refs[16:21], refs[21], refs[22], refs[23]
    copies = fetches([(sources[2 * i : 2 * i + 2], buffers[i]) for i in range(5)], arrived)
    normed, gates, lifts, grads, inners = buffers
    begin(copies[0] + sum(copies[1], []))
    outgoing = []

    def write(number, product):
        slot = number % 2
        if number >= 2:
            finish(outgoing[number - 2])
        for chunk in chunks(staged.shape[4]):
            shard_rows(product(chunk), staged.at[slot], orders[number], rows, bits[number], chunk.start)
        outgoing.append(
            begin_sending(
                staged.at[slot], outs[2 * number], outs[2 * number + 1],
                left.at[2 * number], left.at[2 * number + 1],
            )
        )

    def gate_product(chunk):
        band = chunk.start // 256
        finish(copies[1][band])
        if band == 1:
            begin(copies[2] + copies[3] + copies[4])
        return matmul(normed[...], gates[chunk, :], NT)

    finish(copies[0])
    write(0, gate_product)
    finish(copies[2])
    write(1, lambda chunk: matmul(normed[...], lifts[chunk, :], NT))
    finish(copies[3] + copies[4])
    write(2, lambda chunk: matmul(grads[...], inners[chunk, :], NT))
    for pair in outgoing[1:]:
        finish(pair)


def call_weight_grad(kernel, name, bits, pairs, orders, columns, stages, flops):
    features, length = pairs[0][0].shape
    arrivals = 0
    for number, pair in enumerate(pairs):
        bands = -(-pair[0].shape[-2] // 256) if number == 1 else 1
        arrivals += bands * len(pair) * (1 if pair[0].ndim == 2 else pair[0].shape[0])
    size = len(orders[0])
    rows = features // size
    padded = -(-rows // 16) * 16
    out = (size // 2, padded, columns)
    outs = pl.pallas_call(
        functools.partial(kernel, orders, rows),
        grid_spec=pltpu.PrefetchScalarGridSpec(
            num_scalar_prefetch=1,
            grid=(1,),
            in_specs=[pl.BlockSpec(memory_space=pl.ANY)] * (2 * len(pairs)),
            out_specs=[pl.BlockSpec(memory_space=pl.ANY)] * (2 * len(orders)),
            scratch_shapes=[pltpu.VMEM((pair[0].shape[-2], 2 * length), bf16) for pair in pairs]
            + [pltpu.VMEM((stages, 2) + out, bf16)]
            + [pltpu.SemaphoreType.DMA((arrivals,)), pltpu.SemaphoreType.DMA((2 * len(orders),))],
        ),
        out_shape=[shape_of(out, bf16)] * (2 * len(orders)),
        compiler_params=pltpu.CompilerParams(vmem_limit_bytes=52 * MIB),
        cost_estimate=cost(flops, *(array for pair in pairs for array in pair)),
        name=name,
    )(bits, *in_hbm(*(array for pair in pairs for array in pair)))
    return list(zip(outs[::2], outs[1::2]))


def call_ffn_weight_grad(bits, normed, grads, rights, orders):
    units = rights[0][0].shape[1]
    pairs = (normed, rights[0], rights[1], grads, rights[2])
    flops = 12 * normed[0].shape[0] * normed[0].shape[1] * units
    return call_weight_grad(ffn_weight_grad, "ffn_weight_grad", bits, pairs, orders, units, 2, flops)


def attention_weight_grad(orders, rows, bits, *refs):
    sources, outs = refs[:8], refs[8:14]
    buffers, staged, arrived, left = refs[14:18], refs[18], refs[19], refs[20]
    copies = fetches([(sources[2 * i : 2 * i + 2], buffers[i]) for i in range(4)], arrived)
    begin(copies[0] + sum(copies[1], []))
    outgoing = []
    width = staged.shape[4]

    def write(number, pieces):
        column = 0
        for piece in pieces:
            shard_rows(piece, staged.at[number], orders[number], rows, bits[number], column)
            column += piece.shape[1]
        outgoing.extend(
            begin_sending(
                staged.at[number], outs[2 * number], outs[2 * number + 1],
                left.at[2 * number], left.at[2 * number + 1],
            )
        )

    def project(start, stop):
        finish(copies[1][start // 256])
        if start == 256:
            begin(copies[2] + copies[3])
        return matmul(buffers[0][...], buffers[1][start:stop, :], NT)

    def outward(start, stop):
        return matmul(buffers[2][...], buffers[3][start:stop, :], NT)

    columns, most = buffers[1].shape[0], buffers[3].shape[0]
    rest = 2 * width - columns
    finish(copies[0])
    write(0, [project(start, start + 256) for start in range(0, width, 256)])
    body, tail = project(width, width + 256), project(width + 256, columns)
    finish(copies[2] + copies[3])
    write(1, [body, jnp.concatenate([tail, outward(0, rest)], axis=1)])
    write(2, [outward(start, min(start + 256, most)) for start in range(rest, most, 256)])
    finish(outgoing)


def call_attention_weight_grad(bits, above, below, orders):
    columns = above[1].shape[0] + above[3].shape[0]
    flops = 4 * above[0].shape[0] * above[0].shape[1] * columns
    return call_weight_grad(
        attention_weight_grad, "attention_weight_grad", bits, list(zip(above, below)), orders,
        columns // len(orders), len(orders), flops,
    )


def block_grad(grad_ref, normed_ref, inverse_ref, own_ref, other_ref, gain_ref, out_ref):
    back = norm_back(normed_ref[...], inverse_ref[...], gain_ref[...], joined_sum(own_ref, other_ref))
    out_ref[...] = (grad_ref[...].astype(f32) + back).astype(out_ref.dtype)


def call_block_grad(grad, normed, inverse, own, other, gain, kind):
    features, length = grad.shape
    spec = functools.partial(token_spec, width=FFN_BLOCK)
    return pl.pallas_call(
        block_grad,
        grid=(length // FFN_BLOCK,),
        in_specs=[spec(features)] * 2 + [spec(1)] + [spec(features)] * 2 + [full_spec(gain.shape)],
        out_specs=spec(features),
        out_shape=shape_of((features, length), kind),
        compiler_params=pltpu.CompilerParams(vmem_limit_bytes=32 * MIB),
        cost_estimate=cost(0, grad, normed, own, other),
        name="block_grad",
    )(*in_hbm(grad, normed), inverse, own, other, gain)


def gather_groups(owner, device, *refs):
    sources, (wqkv_out, wout_out), arrived = refs[:4], refs[4:6], refs[6]
    heights = [source.shape[1] for source in sources]
    joint = sum(heights[:3])
    slots = wqkv_out.shape[0] // joint
    for action in ("start", "wait"):
        for slot in range(slots):
            group, held = group_of(slot, owner, device)
            first = slot * joint
            for place, (source, height) in enumerate(zip(sources, heights)):
                if place < 3:
                    target = wqkv_out.at[pl.ds(first, height)]
                    first += height
                else:
                    target = wout_out.at[pl.ds(slot * height, height)]
                copy = pltpu.make_async_copy(source.at[group], target, arrived.at[4 * slot + place])

                def empty(target=target):
                    target[...] = jnp.zeros(target.shape, bf16)

                pl.when(held)(getattr(copy, action))
                if action == "start":
                    pl.when(jnp.logical_not(held))(empty)


def group_of(slot, owner, device):
    found, count = 0, 0
    for group in range(owner.shape[0]):
        mine = owner[group] == device[0]
        found = jnp.where(mine & (count == slot), group, found)
        count = count + jnp.where(mine, 1, 0)
    return found, count > slot


def call_gather_groups(owner, device, w_query, w_key, w_value, w_out, slots):
    features = w_query.shape[2]
    arrays = (w_query, w_key, w_value, w_out)
    joint = slots * (w_query.shape[1] + w_key.shape[1] + w_value.shape[1])
    outs = [(joint, features), (slots * w_out.shape[1], features)]
    return pl.pallas_call(
        gather_groups,
        grid_spec=pltpu.PrefetchScalarGridSpec(
            num_scalar_prefetch=2,
            grid=(1,),
            in_specs=[pl.BlockSpec(memory_space=pl.ANY)] * 4,
            out_specs=[out_full_spec(o) for o in outs],
            scratch_shapes=[pltpu.SemaphoreType.DMA((4 * slots,))],
        ),
        out_shape=[shape_of(o, bf16) for o in outs],
        name="gather_groups",
    )(owner, device, *in_hbm(*arrays))


def rotary_tables(length):
    position = np.arange(length, dtype=np.float64)[None, :]
    column = np.arange(HEAD // 2, dtype=np.float64)[:, None]
    angles = position * np.exp(column * (-2.0 * math.log(10000.0) / HEAD))
    return jnp.asarray(np.cos(angles), f32), jnp.asarray(np.sin(angles), f32)


def exchange(own):
    return lax.ppermute(own, "mp", [(0, 1), (1, 0)])


def stage_plans(bit_count):
    bits = list(range(bit_count))
    turned = [bits[:3], bits[1:3] + bits[:1], bits[2:3] + bits[:2]]
    return [[[bit] for bit in first + bits[3:]] for first in turned]


def shard_order(plan):
    bits = [bit for stage in plan for bit in stage]
    order = []
    for place in range(1 << len(bits)):
        shard = 0
        for rank, bit in enumerate(bits):
            if place >> (len(bits) - 1 - rank) & 1:
                shard |= 1 << bit
        order.append(shard)
    return order


def after(value, *others):
    return lax.optimization_barrier((value, others))[0]


class Stream:
    def __init__(self, parts, widths, count, stages):
        self.parts, self.widths, self.count, self.stages = parts, widths, count, list(stages)

    @classmethod
    def started(cls, kept, sent, plan):
        stream = cls([[(kept, 0, 0)]], [kept.shape[2]], kept.shape[0], plan)
        stream.transfer(sent, stream.stages.pop(0)[0])
        return stream

    def transfer(self, sent, bit):
        size = lax.axis_size("dp")
        received = lax.ppermute(sent, "dp", [(i, i ^ (1 << bit)) for i in range(size)])
        column = 0
        for terms, width in zip(self.parts, self.widths):
            terms.append((received, 0, column))
            column += width
        self.sent = sent

    def hold(self, *others):
        received = after(self.parts[0][-1][0], *others)
        for terms in self.parts:
            terms[-1] = (received, *terms[-1][1:])
        return self

    def sums(self, first, count):
        out = []
        for terms, width in zip(self.parts, self.widths):
            pieces = [
                lax.dynamic_slice(array, (start + first, 0, column), (count, array.shape[1], width))
                for array, start, column in terms
            ]
            out.append(sum(piece.astype(f32) for piece in pieces))
        return out

    def send(self, eager=False):
        bit = self.stages.pop(0)[0]
        mine = (lax.axis_index("dp") >> bit) & 1
        self.count //= 2
        sent = [piece.astype(bf16) for piece in self.sums((1 - mine) * self.count, self.count)]
        if eager:
            kept = self.sums(mine * self.count, self.count)
            self.parts = [[(piece.astype(bf16), 0, 0)] for piece in kept]
        else:
            self.parts = [
                [(array, start + mine * self.count, column) for array, start, column in terms]
                for terms in self.parts
            ]
        self.transfer(sent[0] if len(sent) == 1 else jnp.concatenate(sent, axis=2), bit)
        return self.sent

    def totals(self):
        return [piece[0] for piece in self.sums(0, 1)]


def joined(streams):
    return Stream(
        [terms for stream in streams for terms in stream.parts],
        [width for stream in streams for width in stream.widths],
        streams[0].count,
        streams[0].stages,
    )


def per_device(
    tokens_in,
    segment_ids,
    kv_owner,
    w_query,
    w_key,
    w_value,
    w_out,
    attn_gain,
    w_gate,
    w_up,
    w_down,
    ffn_gain,
    cotangent,
):
    features = tokens_in.shape[2]
    length = tokens_in.shape[1]
    group_cols = w_query.shape[2]
    heads = group_cols // HEAD
    slots = (kv_owner.shape[0] + lax.axis_size("mp") - 1) // lax.axis_size("mp")
    size = lax.axis_size("dp")
    rows = features // size

    device = lax.axis_index("mp").astype(jnp.int32)[None]
    wqkv, wout = call_gather_groups(
        kv_owner, device, *(jnp.swapaxes(w, 1, 2) for w in (w_query, w_key, w_value)), w_out, slots
    )
    w_down = w_down.T
    segments = segment_ids[0]
    cosine, sine = rotary_tables(length)
    gain_one, gain_two = (
        jnp.broadcast_to(gain.astype(f32)[:, None], (features, LANES)) for gain in (attn_gain, ffn_gain)
    )

    parts = (tokens_in[0].T,)
    saved = []
    for _ in range(REPEAT):
        own_weights = (wqkv, wout) if len(parts) == 3 else in_hbm(wqkv, wout)
        outs = list(
            call_attention_forward(segments, parts, gain_one, *own_weights, cosine, sine, slots, heads)
        )
        hidden = outs.pop(0) if len(parts) == 3 else parts[0]
        normed, inverse, query, key, turned_key, value, attended, partial = outs
        middle, normed_two, inverse_two, gate, lift, inner, partial_two = call_ffn_forward(
            hidden, partial, exchange(partial), gain_two, w_gate, w_up, w_down
        )
        parts = (middle, partial_two, exchange(partial_two))
        saved.append((
            normed, inverse, query, key, turned_key, value, attended, normed_two, inverse_two, gate, lift, inner,
        ))

    plans = stage_plans(size.bit_length() - 1)
    orders = [shard_order(plan) for plan in plans]
    bits = jnp.stack([(lax.axis_index("dp") >> plan[0][0]) & 1 for plan in plans]).astype(jnp.int32)
    joint = ()
    grad = cotangent[0].T
    for r in reversed(range(REPEAT)):
        (normed, inverse, query, key, turned_key, value, attended,
         normed_two, inverse_two, gate, lift, inner) = saved[r]
        last = r == 0
        outs = list(call_ffn_backward(grad, joint, gate, lift, w_gate, w_up, w_down))
        if joint:
            grad = outs.pop(0)
        ffn_grad = grad
        grad_gate, grad_lift, partial = outs
        other = exchange(partial)
        if not last:
            parts = after(parts, partial)
            tokens_out = (parts[0] + (parts[1].astype(f32) + parts[2].astype(f32))).astype(bf16)
            grad = after(grad, tokens_out)
        else:
            payloads = call_ffn_weight_grad(
                bits, (above["normed_two"], normed_two), (above["ffn_grad"], ffn_grad),
                ((above["grad_gate"], grad_gate), (above["grad_lift"], grad_lift), (above["inner"], inner)),
                orders,
            )
            track_a, track_b, down = (
                Stream.started(*payload, plan) for payload, plan in zip(payloads, plans)
            )
            partial = after(partial, payloads)
        grad, projected, partial_two = call_attention_backward(
            segments, grad, partial, other, normed_two, inverse_two, gain_two, wout, wqkv, attended, query,
            key, turned_key, value, cosine, sine,
        )
        other_two = exchange(partial_two)
        if not last:
            above = dict(
                ffn_grad=ffn_grad, inner=inner, normed_two=normed_two, grad_lift=grad_lift,
                grad_gate=grad_gate, attention=(normed, projected, grad, attended),
            )
        joint = (normed, inverse, partial_two, other_two, gain_one)
    ffn = (track_a, track_b, down)
    sent = [stream.hold(projected).send() for stream in ffn]
    payloads = call_attention_weight_grad(
        bits, above["attention"], (normed, after(projected, sent), grad, attended), orders
    )
    tracks = [Stream.started(*payload, plan) for payload, plan in zip(payloads, plans)]
    for stream in ffn:
        stream.hold(payloads, other_two)
    sent = [stream.send() for stream in (track_a, track_b)]
    grad_in = call_block_grad(after(grad, sent, payloads), *joint, f32)
    both = joined([stream.hold(grad_in) for stream in (track_a, track_b)])
    sent = [both.send(True), down.hold(grad_in).send(True)]
    sent = [stream.hold(sent).send(True) for stream in tracks]
    sent = [down.hold(sent).send(True)]
    while len(tracks[0].stages) > 1:
        sent = [stream.hold(sent).send(True) for stream in tracks]
    attn = joined([stream.hold(sent) for stream in tracks])
    pending = [both, down, attn]
    while any(stream.stages for stream in pending):
        for stream in pending:
            if stream.stages:
                stream.send(True)
    gate_total, up_total = both.totals()
    (down_total,) = down.totals()
    attn_total = jnp.concatenate(attn.totals(), axis=1)[:rows]

    start = lax.axis_index("dp") * rows

    def my_rows(weights):
        return lax.dynamic_slice_in_dim(weights, start, rows, 0).astype(f32)

    gate_total, up_total, down_total = (total[:rows] for total in (gate_total, up_total, down_total))
    wqkv = after(wqkv, grad_in)
    chosen = (jnp.arange(rows)[:, None] + start == jnp.arange(features)[None, :]).astype(bf16)
    wqkv_rows = matmul(chosen, wqkv, NT)
    joint_cols = wqkv.shape[0]
    gains = jnp.stack([
        jnp.sum(attn_total[:, :joint_cols] * wqkv_rows, axis=1),
        jnp.sum(gate_total * my_rows(w_gate) + up_total * my_rows(w_up), axis=1),
    ])
    gains = gains + exchange(gains)
    gains = gains / lax.dynamic_slice_in_dim(jnp.stack([attn_gain, ffn_gain]), start, rows, 1).astype(f32)

    ends = [group_cols, group_cols + HEAD]
    by_slot = jnp.moveaxis(attn_total[:, :joint_cols].reshape(rows, slots, -1), 1, 0)
    return (
        tokens_out.T[None],
        grad_in.T[None],
        by_slot[:, :, : ends[0]],
        by_slot[:, :, ends[0] : ends[1]],
        by_slot[:, :, ends[1] :],
        attn_total[:, joint_cols:].T.reshape(slots, group_cols, rows),
        gate_total,
        up_total,
        down_total.T,
        gains[0],
        gains[1],
    )


def solution(mesh):
    in_specs = (
        P("dp", None, None),
        P("dp", None),
        P(),
        P(),
        P(),
        P(),
        P(),
        P(),
        P(None, "mp"),
        P(None, "mp"),
        P("mp", None),
        P(),
        P("dp", None, None),
    )
    out_specs = (
        P("dp", None, None),
        P("dp", None, None),
        P("mp", "dp", None),
        P("mp", "dp", None),
        P("mp", "dp", None),
        P("mp", None, "dp"),
        P("dp", "mp"),
        P("dp", "mp"),
        P("mp", "dp"),
        P("dp"),
        P("dp"),
    )
    return jax.shard_map(
        per_device, mesh=mesh, in_specs=in_specs, out_specs=out_specs, check_vma=False
    )
```
